512 devices in a mesh: kb: 32 (over z, core), gr: 4 (over y), gc: 4 (over x).
Axes of the slice: x: 4, y: 4, z: 16, core: 2. Of those that a mesh axis runs over, the one named last changes fastest.
Arguments:
- wedge_pairs: bfloat16 [32, 1, 16, 2048], P('kb'), may hold values from -6 to 6
- e_cond: float32 [32, 1], P('kb'), may hold values from 0.5 to 12
- e_val: float32 [32, 16], P('kb'), may hold values from -8 to -1
- coulomb: float32 [2048], replicated, may hold values from 0.5 to 50
- owned_wedge: int32 [32, 17], replicated, may hold values from -1 to 31, as said below
- owned_op: int32 [32, 17], replicated, may hold values from 0 to 47
- gmap: int32 [48, 2048], replicated, may hold values from 0 to 2047, each once within a row
Outputs:
- panel_step: float32 [2048, 2048], P(('gr', 'kb'), 'gc')
The draws below stay inside these ranges and needn't reach their ends.
Inputs may be any that keep to these rules, and one draw needn't show every extreme that they name: `owned_wedge`: each owner lists 16 or 17 wedge k points in its first slots, the rest -1; no owner lists a wedge twice; some owner lists exactly 17. `gmap`: each row is a permutation of the plane waves.
All inputs are finite; a program needn't handle non-finite values.
Results may differ from the reference program's by a relative error of at most 0.0024.
Values may be sent and summed in bfloat16 or wider, within the bound.
A program may use at most 64 MiB of HBM per device.

```python
import math
import jax
import jax.numpy as jnp
from jax import lax

NG = 2048
NV = 16
NCB = 1
KPOINTS_PER_UNIT = 16
CAP = 17
WINDOW_SLOTS = 544
NW = 32
NOPS = 48
N_KB = 32
N_GR = 4


def draw_owned_wedge(key, part):
    key = jax.random.fold_in(key, 11)
    first, second, third, fourth, fifth = jax.random.split(key, 5)
    fewest = min(KPOINTS_PER_UNIT, N_KB - 1)
    most = fewest + 1
    frequent_owner = max(1, min(fewest, N_KB // 8))
    ranking = jnp.argsort(jax.random.permutation(first, N_KB)).astype(jnp.int32)
    indices = jnp.arange(N_KB, dtype=jnp.int32)
    owner_scores = jax.random.randint(second, (N_KB, N_KB), 0, 1 << 20, dtype=jnp.int32) * N_KB + indices[None, :]
    owner_scores = jnp.where(ranking[None, :] < frequent_owner, ranking[None, :] - frequent_owner, owner_scores)
    order = jnp.argsort(owner_scores, axis=1, stable=True).astype(jnp.int32)
    listed = order[:, :most]
    forced = jnp.argsort(jax.random.permutation(third, N_KB)).astype(jnp.int32) < 1
    coin = jax.random.randint(fourth, (N_KB,), 0, 2, dtype=jnp.int32) > 0
    owner_counts = fewest + jnp.logical_or(forced, coin).astype(jnp.int32)
    column = jnp.arange(most, dtype=jnp.int32)
    inside = column[None, :] < owner_counts[:, None]
    shuffle_scores = jax.random.randint(fifth, (N_KB, most), 0, 1 << 20, dtype=jnp.int32) * most + column[None, :]
    shuffle_scores = jnp.where(inside, shuffle_scores, (1 << 26) + column[None, :])
    position = jnp.argsort(shuffle_scores, axis=1, stable=True).astype(jnp.int32)
    shuffled = jnp.take_along_axis(listed, position, axis=1)
    return jnp.where(inside, shuffled, -1).astype(jnp.int32)


def draw_owned_op(key, part):
    key = jax.random.fold_in(key, 13)
    return jax.random.randint(key, (N_KB, CAP), 0, NOPS, dtype=jnp.int32)


def level_of(own_key, extent, cuts, low, high):
    factor_of, own = 1.0, jax.random.fold_in(own_key, 6)
    for axis_at, shards_of in cuts:
        heights = jnp.exp(jax.random.uniform(jax.random.fold_in(own, axis_at), (shards_of,), jnp.float32, low / len(cuts), high / len(cuts)))
        factor_of = factor_of * jnp.repeat(heights, extent[axis_at] // shards_of).reshape([-1 if axis == axis_at else 1 for axis in range(len(extent))])
    return factor_of


def noise(rng, extent, scale, reach, shards=(), held_as=jnp.bfloat16):
    drawn = scale * jax.random.normal(rng, extent, jnp.float32)
    if shards:
        drawn = drawn * level_of(rng, extent, shards, -0.22, 0.18)
    return jnp.clip(drawn, -reach, reach).astype(held_as)


def setup_inputs(seed: int = 0) -> dict:
    streams_of = jax.random.split(jax.random.key(seed), 8)
    wedge_pairs = noise(streams_of[0], (NW, NCB, NV, NG), 1.0, 6.0, ((0, 32),))
    e_cond = jnp.clip(0.5 + 11.5 * jax.random.uniform(streams_of[1], (NW, NCB), jnp.float32) ** level_of(streams_of[1], (NW, NCB), ((0, 32),), -0.2, 0.2), 0.5, 12.0)
    e_val = jnp.clip(-8.0 + 7.0 * jax.random.uniform(streams_of[2], (NW, NV), jnp.float32) ** level_of(streams_of[2], (NW, NV), ((0, 32),), -0.2, 0.2), -8.0, -1.0)
    coulomb = jnp.clip(jnp.exp(jax.random.uniform(streams_of[3], (NG,), jnp.float32, math.log(0.5), math.log(50.0))), 0.5, 50.0)
    owned_wedge = draw_owned_wedge(jax.random.fold_in(streams_of[7], 71), 0)
    owned_op = draw_owned_op(jax.random.fold_in(streams_of[7], 71), 0)
    gmap = jax.vmap(lambda own: jax.random.permutation(own, NG))(jax.random.split(streams_of[6], NOPS)).reshape((NOPS, NG)).astype(jnp.int32)
    return dict(wedge_pairs=wedge_pairs, e_cond=e_cond, e_val=e_val, coulomb=coulomb, owned_wedge=owned_wedge, owned_op=owned_op, gmap=gmap)


def reference(wedge_pairs, e_cond, e_val, coulomb, owned_wedge, owned_op, gmap):
    slot_wedges = owned_wedge.reshape(-1)
    slot_ops = owned_op.reshape(-1)

    def accumulate(chi, entry):
        wedge_entry, op_entry = entry
        valid_mask = (wedge_entry >= 0).astype(jnp.float32)
        wedge = jnp.maximum(wedge_entry, 0)
        block = wedge_pairs[wedge][:, :, gmap[op_entry]]
        slot_gap = e_cond[wedge][:, None] - e_val[wedge][None, :]
        kpoint_weight = jnp.sqrt(4.0 / (float(WINDOW_SLOTS) * slot_gap)) * valid_mask
        scaled = (block.astype(jnp.float32) * kpoint_weight[:, :, None]).astype(jnp.bfloat16).reshape(-1, NG)
        product = lax.dot_general(scaled.astype(jnp.float32), scaled.astype(jnp.float32), (((0,), (0,)), ((), ())), preferred_element_type=jnp.float32)
        return (chi - product, None)
    chi, unused = lax.scan(accumulate, jnp.zeros((NG, NG), jnp.float32), (slot_wedges, slot_ops))
    root = jnp.sqrt(coulomb)
    eps = jnp.eye(NG, dtype=jnp.float32) - root[:, None] * chi * root[None, :]
    width = NG // N_GR
    factor = jnp.linalg.cholesky(eps[:width, :width])
    lower = lax.linalg.triangular_solve(factor, eps[width:, :width], left_side=False, lower=True, transpose_a=True)
    upper = lax.linalg.triangular_solve(factor, eps[:width, width:], left_side=True, lower=True)
    trail = eps[width:, width:] - jnp.dot(lower, upper, precision=lax.Precision.HIGHEST)
    top_rows = jnp.concatenate([factor, eps[:width, width:]], axis=1)
    low_rows = jnp.concatenate([lower, trail], axis=1)
    return jnp.concatenate([top_rows, low_rows], axis=0)
```

```python
import functools
import jax
import jax.numpy as jnp
from jax import lax
from jax.experimental import pallas as pl
from jax.experimental.pallas import tpu as pltpu
from jax.sharding import PartitionSpec as P

MESH = pl.DeviceIdType.MESH
HI = lax.Precision.HIGHEST
NT = (((1,), (1,)), ((), ()))
TN = (((0,), (0,)), ((), ()))
LOW = 256
BLOCK = 128


def product(a, b, dims=(((1,), (0,)), ((), ()))):
    return lax.dot_general(a, b, dims, precision=HI, preferred_element_type=jnp.float32)


def inverse_factor(d, hook):
    n = d.shape[0]
    lane = lax.broadcasted_iota(jnp.int32, (8, n), 1)
    sub = lax.broadcasted_iota(jnp.int32, (8, n), 0)
    tail = d.reshape(n // 8, 8, n)
    out = []
    for g in range(n // 8):
        base = 8 * g
        hook(g)
        cols = [jnp.broadcast_to(tail[:, :, base + k:base + k + 1], tail.shape) for k in range(8)]
        inside = (lane >= base) & (lane < base + 8)
        head = jnp.where(inside, jnp.where(lane - base == sub, 1.0, 0.0), tail[0])
        rest = jnp.where(inside[None], 0.0, tail[1:]) if g + 1 < n // 8 else None
        entry = {(i, k): jnp.broadcast_to(cols[k][0, i:i + 1, :], (8, n)) for i in range(8) for k in range(i + 1)}
        row = [jnp.broadcast_to(head[i:i + 1, :], (8, n)) for i in range(8)]
        below = [c[1:] for c in cols]
        done = jnp.zeros((8, n), jnp.float32)
        for j in range(8):
            scale = lax.rsqrt(entry[j, j])
            pivot_row = row[j] * scale
            done = jnp.where(sub == j, pivot_row, done)
            mult = {i: entry[i, j] * scale for i in range(j + 1, 8)}
            for i in range(j + 1, 8):
                row[i] = row[i] - mult[i] * pivot_row
                for k in range(j + 1, i + 1):
                    entry[i, k] = entry[i, k] - mult[i] * mult[k]
            if rest is not None:
                step = below[j] * scale[None]
                rest = rest - step * pivot_row[None]
                for k in range(j + 1, 8):
                    below[k] = below[k] - step * mult[k][None]
        out.append(jnp.where(lane <= sub + base, done, 0.0))
        tail = rest
    return jnp.concatenate(out, axis=0)


def whole_kernel(chips, grid, wedge_ref, op_ref, x_ref, ec_ref, ev_ref, coulomb_ref, gmap_ref, out_ref,
                 lo_ref, hi_ref, s_ref, y_ref, p_ref, c1_recv, c2_send, c2_recv, e00_ref, total_ref,
                 pair_ref, send_ref, recv_ref, far_send_ref, far_recv_ref, f_ref, own_ref, left_ref, top_ref,
                 r_ref, inv_ref, low_ref, w_ref,
                 c1_s, c1_r, c2_s, c2_r, c3_s, c3_r, c4_s, c4_r, c5_s, c5_r,
                 pair_s, pair_r, near_s, near_r, far_s, far_r, swap_s, swap_r,
                 top_s, top_r, side_s, side_r, ag_s, ag_r, fw_s, fw_r):
    kb, gr, gc = lax.axis_index("kb"), lax.axis_index("gr"), lax.axis_index("gc")
    z, c = kb // 2, kb % 2
    other = 1 - c
    owners, slots = wedge_ref.shape
    bands, total_g = x_ref.shape
    band, width = out_ref.shape
    rows, wide = 2 * band, width // 2
    is_top, is_left = gr == 0, gc == 0

    def chip(delta, core=None):
        return (2 * ((z + delta + chips) % chips) + (c if core is None else core), gr, gc)

    def remote(src, dst, send, recv, who):
        return pltpu.make_async_remote_copy(
            src_ref=src, dst_ref=dst, send_sem=send, recv_sem=recv, device_id=who, device_id_type=MESH
        )

    partner = (2 * z + other, gr, gc)
    peers = {
        i: (kb, (gr + i // grid) % grid, (gc + i % grid) % grid) for i in range(1, grid * grid)
    }
    barrier = pltpu.get_barrier_semaphore()
    everyone = (
        [chip(d, core) for d in (1, -1, 2, -2) for core in (0, 1)]
        + [chip(d) for d in (4, -4, 8)] + [partner] + list(peers.values())
    )
    for who in everyone:
        pl.semaphore_signal(barrier, inc=1, device_id=who, device_id_type=MESH)

    eye = lax.broadcasted_iota(jnp.int32, (bands, bands), 0) == lax.broadcasted_iota(jnp.int32, (bands, bands), 1)
    gap = ec_ref[...] - ev_ref[...]
    weight = jnp.sqrt(4.0 / (float(owners * slots) * gap))
    weight = jnp.sum(jnp.where(eye, jnp.broadcast_to(weight, (bands, bands)), 0.0), axis=1, keepdims=True)
    y = (x_ref[...].astype(jnp.float32) * weight).astype(jnp.bfloat16)
    parts = total_g // LOW
    for h in range(parts):
        y_ref[h * bands:(h + 1) * bands, :] = y[:, h * LOW:(h + 1) * LOW]
    matched = jnp.where(wedge_ref[...] == kb, 1.0, 0.0)
    present = jnp.sum(matched, axis=1, keepdims=True)
    operation = jnp.sum(matched * op_ref[...].astype(jnp.float32), axis=1, keepdims=True).astype(jnp.int32)
    kinds = lax.broadcasted_iota(jnp.int32, (owners, gmap_ref.shape[0]), 1)
    chosen = jnp.where(kinds == operation, present, 0.0).astype(jnp.bfloat16)
    count = lax.broadcasted_iota(jnp.int32, (LOW, 128), 0).astype(jnp.float32).astype(jnp.bfloat16)
    one, none = jnp.ones((LOW, 128), jnp.bfloat16), jnp.zeros((LOW, 128), jnp.bfloat16)

    def gather(side, at):
        maps = gmap_ref[:, pl.ds(at, width)]
        low_bits = (maps & (LOW - 1)).astype(jnp.float32).astype(jnp.bfloat16)
        high_bits = (maps >> (LOW.bit_length() - 1)).astype(jnp.float32).astype(jnp.bfloat16)
        lo_ref[...] = jnp.dot(chosen, low_bits, preferred_element_type=jnp.float32)
        hi_ref[...] = jnp.dot(chosen, high_bits, preferred_element_type=jnp.float32) + (present - 1.0)

        def pick(o, carry):
            low = jnp.broadcast_to(lo_ref[pl.ds(o, 1), :], (LOW, width)).astype(jnp.bfloat16)
            high = hi_ref[pl.ds(o, 1), :]
            onehot = jnp.concatenate(
                [jnp.where(count == low[:, t:t + 128], one, none) for t in range(0, width, 128)], axis=1
            )
            spread = jnp.dot(y_ref[...], onehot, preferred_element_type=jnp.float32)
            picked = jnp.zeros((bands, width), jnp.float32)
            for h in range(parts):
                picked = jnp.where(high == float(h), spread[h * bands:(h + 1) * bands, :], picked)
            s_ref[pl.ds(pl.multiple_of(o * bands, bands), bands), side * width:(side + 1) * width] = picked.astype(jnp.bfloat16)
            return carry

        lax.fori_loop(0, owners, pick, 0, unroll=4)

    root = jnp.sqrt(coulomb_ref[...])

    def root_down(first, count, reach):
        ids = first + lax.broadcasted_iota(jnp.int32, (count, reach), 0)
        lanes = lax.broadcasted_iota(jnp.int32, (count, reach), 1)
        return jnp.sum(jnp.where(ids == lanes, jnp.broadcast_to(root[:, :reach], (count, reach)), 0.0), axis=1, keepdims=True)

    def dielectric(value, first_row, first_col):
        count, across = value.shape
        reach = total_g
        row = first_row + lax.broadcasted_iota(jnp.int32, (count, across), 0)
        col = first_col + lax.broadcasted_iota(jnp.int32, (count, across), 1)
        root_across = jnp.sqrt(coulomb_ref[:, pl.ds(pl.multiple_of(first_col, 128), across)])
        return jnp.where(row == col, 1.0, 0.0) + root_down(first_row, count, reach) * value * root_across

    gather(0, 0)
    p_ref[...] = lax.dot_general(
        s_ref[:, pl.ds(pl.multiple_of(gr * BLOCK, BLOCK), BLOCK)], s_ref[:, :width], TN, preferred_element_type=jnp.float32
    )
    pl.semaphore_wait(barrier, len(everyone))

    def p_part(delta, core):
        k = (z + delta + chips) % grid
        return p_ref.at[pl.ds(pl.multiple_of(gc * rows + 8 * k, 8), 8), pl.ds(pl.multiple_of(core * wide, wide), wide)]

    near_parts = [(1, 0, c), (1, 1, c), (-1, 0, 2 + c), (-1, 1, 2 + c), (2, 0, 4 + c), (-2, 1, 4 + c), (0, other, 6)]
    stage1 = [
        remote(p_part(d, core), c1_recv.at[slot], c1_s.at[i], c1_r.at[slot], chip(d, core))
        for i, (d, core, slot) in enumerate(near_parts)
    ]
    for copy in stage1:
        copy.start()

    gather(1, pl.multiple_of(gr * width, width))

    value = p_part(0, c)[...]
    for slot in range(7):
        remote(p_part(0, other), c1_recv.at[slot], c1_s.at[0], c1_r.at[slot], partner).wait_recv()
        value = value + c1_recv[slot]
    c2_send[...] = value
    stage2 = [
        remote(c2_send, c2_recv.at[i], c2_s.at[i], c2_r.at[i], chip(d)) for i, d in enumerate((8, 4, -4))
    ]
    for copy in stage2:
        copy.start()

    gather(2, pl.multiple_of(gc * width, width))

    mine = pl.ds(pl.multiple_of(c * wide, wide), wide)
    theirs = pl.ds(pl.multiple_of(other * wide, wide), wide)
    total_ref[...] = lax.dot_general(
        s_ref[:, width:2 * width], s_ref[:, 2 * width:], TN, preferred_element_type=jnp.float32
    )

    def chunk(off):
        return pl.ds(pl.multiple_of(((z + off + chips) % chips) * rows, rows), rows)

    near = [
        (9, 1, 2), (7, -1, 6), (5, 1, 1), (3, -1, 5), (6, 2, 9), (-6, -2, 11),
        (13, 1, 3), (11, -1, 7), (1, 1, 0), (15, -1, 4), (2, 2, 8), (-2, -2, 10),
    ]
    order = [off % chips for off, _, _ in near] + [8, 4, 12, 0]
    pairs = {
        off: remote(total_ref.at[chunk(off), theirs], pair_ref.at[i], pair_s.at[i], pair_r.at[i], partner)
        for i, off in enumerate(order)
    }
    for off in order:
        pairs[off].start()

    value = c2_send[...]
    for i in (1, 2, 0):
        stage2[i].wait_recv()
        value = value + c2_recv[i]
    first = gr * BLOCK + gc * rows
    first_e = pl.multiple_of(first + 8 * (z % grid), 8)
    part = e00_ref.at[pl.ds(first_e, 8), mine]
    part[...] = dielectric(value, first_e, c * wide)
    two = jnp.where(c == 0, 2, -2)
    spread_to = [(1, 0, c), (1, 1, c), (-1, 0, 2 + c), (-1, 1, 2 + c), (two, 0, 4 + c), (two, 1, 4 + c), (0, other, 6)]
    stage3 = [
        remote(part, part, c3_s.at[i], c3_r.at[slot], chip(d, core)) for i, (d, core, slot) in enumerate(spread_to)
    ]
    for copy in stage3:
        copy.start()

    def own_part(off):
        off = off % chips
        pairs[off].wait_recv()
        return total_ref[chunk(off), mine] + pair_ref[order.index(off)]

    near_copies = {}
    for off, delta, slot in near:
        send_ref[slot] = own_part(off)
        copy = remote(send_ref.at[slot], recv_ref.at[slot], near_s.at[slot], near_r.at[slot], chip(delta))
        copy.start()
        near_copies[slot] = copy

    for slot in range(7):
        remote(part, part, c3_s.at[0], c3_r.at[slot], partner).wait_recv()

    def e00_part(r, s, half):
        return e00_ref.at[pl.ds(pl.multiple_of(r * BLOCK + s * rows, rows), rows), half]

    def needed(r, core):
        return jnp.logical_or(core == 1, r < 2)

    def stage4(i):
        return remote(e00_part(gr, gc, mine), e00_part(gr, gc, mine), c4_s.at[i], c4_r.at[i], peers[i])

    def sender(i):
        return (gr + grid - i // grid) % grid, (gc + grid - i % grid) % grid

    @pl.when(needed(gr, c))
    def _():
        for i in peers:
            stage4(i).start()

    def stage5(i, half):
        r, s = sender(i)
        return remote(e00_part(r, s, half), e00_part(r, s, half), c5_s.at[i], c5_r.at[i], partner)

    for i in peers:
        @pl.when(needed(sender(i)[0], c))
        def _():
            stage4(i).wait_recv()
            stage5(i, mine).start()
    def gathered(j, extra):
        value = own_part(4 * j)
        for slot in (j, 4 + j) + extra:
            near_copies[slot].wait_recv()
            value = value + recv_ref[slot]
        return value

    far_list = [(2, (), 8), (1, (9,), 4), (3, (11,), -4)]

    def far_copy(i):
        return remote(far_send_ref.at[i], far_recv_ref.at[i], far_s.at[i], far_r.at[i], chip(far_list[i][2]))

    def end_e00_copies():
        for copy in stage3:
            copy.wait_send()

        @pl.when(needed(gr, c))
        def _():
            for i in peers:
                stage4(i).wait_send()
        for i in peers:
            @pl.when(needed(sender(i)[0], c))
            def _():
                stage5(i, mine).wait_send()

    def send_far():
        for i, (j, extra, delta) in enumerate(far_list):
            far_send_ref[i] = gathered(j, extra)
            far_copy(i).start()

    my_top = top_ref.at[chunk(0), mine]

    def to_top(i):
        return remote(f_ref, my_top, top_s.at[i - 1], top_r, (kb, (gr + i) % grid, gc))

    swap = remote(f_ref.at[pl.ds(pl.multiple_of(other * band, band), band)], own_ref.at[:, mine], swap_s, swap_r, partner)

    def send_top():
        value = gathered(0, (8, 10))
        for i in (1, 2, 0):
            far_copy(i).wait_recv()
            value = value + far_recv_ref[i]
        value = dielectric(value, gr * width + z * rows, gc * width + c * wide)
        f_ref[...] = value

        @pl.when(is_top)
        def _():
            for i in range(1, grid):
                to_top(i).start()
            my_top[...] = value

        swap.start()
        own_ref[:, mine] = f_ref[pl.ds(pl.multiple_of(c * band, band), band)]

    def piece(off):
        return top_ref.at[chunk(off), mine]

    def forward(off):
        return remote(piece(off), piece(off), fw_s.at[off], fw_r.at[off], partner)

    gossip = {
        0: ((8, 0), (4, 1), (-4, 2), (1, 3), (-1, 4), (2, 5), (-2, 6)),
        4: ((1, 7), (-1, 8), (-2, 9)),
        12: ((1, 10), (-1, 11), (2, 12)),
        8: ((1, 13), (-1, 14)),
    }

    def gossip_copy(off, delta, i):
        return remote(piece(off), piece(off), ag_s.at[i], ag_r.at[(off - delta) % chips], chip(delta))

    def arrive(off):
        remote(piece(off), piece(off), ag_s.at[0], ag_r.at[off], partner).wait_recv()

    def to_side(i):
        return remote(own_ref, left_ref, side_s.at[i - 1], side_r, (kb, gr, (gc + i) % grid))

    def send_first():
        @pl.when(jnp.logical_not(is_top))
        def _():
            to_top(1).wait_recv()

        for delta, i in gossip[0]:
            gossip_copy(0, delta, i).start()
        forward(0).start()
        swap.wait_recv()

        @pl.when(is_left)
        def _():
            for i in range(1, grid):
                to_side(i).start()

    def send_second():
        for off in (4, 12, 8):
            arrive(off)
            for delta, i in gossip[off]:
                gossip_copy(off, delta, i).start()
            forward(off).start()

    send_far()
    for i in peers:
        @pl.when(needed(sender(i)[0], other))
        def _():
            stage5(i, theirs).wait_recv()

    plan = {(0, 15): end_e00_copies, (1, 6): send_top, (2, 2): send_first, (3, 8): send_second}
    cuts = [slice(b * BLOCK, (b + 1) * BLOCK) for b in range(width // BLOCK)]
    for b, cut in enumerate(cuts):
        def hook(g):
            if (b, g) in plan:
                plan[b, g]()

        inverse = inverse_factor(e00_ref[cut, cut], hook)
        inv_ref[cut, :] = inverse
        after = (b + 1) * BLOCK
        if after < width:
            across = product(inverse, e00_ref[cut, after:])
            r_ref[cut, after:] = across
            for cut2 in cuts[b + 1:]:
                at = cut2.start
                e00_ref[cut2, at:] = e00_ref[cut2, at:] - product(
                    across[:, at - after:at - after + BLOCK], across[:, at - after:], TN
                )

    @pl.when(jnp.logical_not(is_left))
    def _():
        to_side(1).wait_recv()

    @pl.when(is_left)
    def _():
        left_ref[...] = own_ref[...]

    for b, cut in enumerate(cuts):
        value = left_ref[:, cut]
        if b:
            value = value - product(low_ref[:, :b * BLOCK], r_ref[:b * BLOCK, cut])
        low_ref[:, cut] = product(value, inv_ref[cut, :], NT)
    for b in reversed(range(len(cuts))):
        cut = cuts[b]
        value = low_ref[:, cut]
        if b + 1 < len(cuts):
            value = value - product(w_ref[:, (b + 1) * BLOCK:], r_ref[cut, (b + 1) * BLOCK:], NT)
        w_ref[:, cut] = product(value, inv_ref[cut, :])

    for off in (1, 15, 2, 14, 5, 3, 13, 11, 6, 10, 7, 9):
        arrive(off)
        forward(off).start()
    for off in range(chips):
        forward(off).wait_recv()

    row = kb * band + lax.broadcasted_iota(jnp.int32, (band, width), 0)
    col = lax.broadcasted_iota(jnp.int32, (band, width), 1)
    factor_side = jnp.where(is_top & (col > row), 0.0, low_ref[...])
    trail = own_ref[...] - product(w_ref[...], top_ref[...])
    out_ref[...] = jnp.where(is_left, factor_side, jnp.where(is_top, own_ref[...], trail))

    for copy in stage1 + stage2 + list(pairs.values()) + list(near_copies.values()) + [swap]:
        copy.wait_send()
    for i in range(3):
        far_copy(i).wait_send()
    for off, sends in gossip.items():
        for delta, i in sends:
            gossip_copy(off, delta, i).wait_send()
    for off in range(chips):
        forward(off).wait_send()

    @pl.when(is_top)
    def _():
        for i in range(1, grid):
            to_top(i).wait_send()

    @pl.when(is_left)
    def _():
        for i in range(1, grid):
            to_side(i).wait_send()


def body(wedge_pairs, e_cond, e_val, coulomb, owned_wedge, owned_op, gmap):
    members = lax.axis_size("kb")
    grid = lax.axis_size("gr")
    chips = members // 2
    total_g = gmap.shape[1]
    width = total_g // grid
    band = width // members
    owners = owned_wedge.shape[0]
    x = wedge_pairs.reshape(-1, total_g)
    bands = x.shape[0]
    vmem = pl.BlockSpec(memory_space=pltpu.VMEM)
    dma = pltpu.SemaphoreType.DMA
    piece = (2 * band, width // 2)
    f32 = jnp.float32
    return pl.pallas_call(
        functools.partial(whole_kernel, chips, grid),
        out_shape=jax.ShapeDtypeStruct((band, width), f32),
        in_specs=[vmem] * 7,
        out_specs=vmem,
        scratch_shapes=[
            pltpu.VMEM((owners, width), f32),
            pltpu.VMEM((owners, width), f32),
            pltpu.VMEM((owners * bands, 3 * width), jnp.bfloat16),
            pltpu.VMEM((bands * (total_g // LOW), LOW), jnp.bfloat16),
            pltpu.VMEM((BLOCK, width), f32),
            pltpu.VMEM((7, 8, width // 2), f32),
            pltpu.VMEM((8, width // 2), f32),
            pltpu.VMEM((3, 8, width // 2), f32),
            pltpu.VMEM((width, width), f32),
            pltpu.VMEM((width, width), f32),
            pltpu.VMEM((chips,) + piece, f32),
            pltpu.VMEM((12,) + piece, f32),
            pltpu.VMEM((12,) + piece, f32),
            pltpu.VMEM((3,) + piece, f32),
            pltpu.VMEM((3,) + piece, f32),
            pltpu.VMEM(piece, f32),
            pltpu.VMEM((band, width), f32),
            pltpu.VMEM((band, width), f32),
            pltpu.VMEM((width, width), f32),
            pltpu.VMEM((width, width), f32),
            pltpu.VMEM((width, BLOCK), f32),
            pltpu.VMEM((band, width), f32),
            pltpu.VMEM((band, width), f32),
            dma((7,)), dma((7,)),
            dma((3,)), dma((3,)),
            dma((7,)), dma((7,)),
            dma((grid * grid,)), dma((grid * grid,)),
            dma((grid * grid,)), dma((grid * grid,)),
            dma((chips,)), dma((chips,)),
            dma((12,)), dma((12,)),
            dma((3,)), dma((3,)),
            dma, dma,
            dma((grid - 1,)), dma,
            dma((grid - 1,)), dma,
            dma((15,)), dma((chips,)),
            dma((chips,)), dma((chips,)),
        ],
        compiler_params=pltpu.CompilerParams(
            collective_id=0, has_side_effects=True, vmem_limit_bytes=40 << 20
        ),
        name="whole",
    )(owned_wedge, owned_op, x, e_cond, e_val, coulomb.reshape(1, -1), gmap)


def solution(mesh):
    placed = (P("kb", None, None, None), P("kb", None), P("kb", None), P(), P(), P(), P())
    return jax.shard_map(
        body, mesh=mesh, in_specs=placed, out_specs=P(("gr", "kb"), "gc"), check_vma=False
    )
```

```python
import functools
import jax
import jax.numpy as jnp
from jax import lax
from jax.experimental import pallas as pl
from jax.experimental.pallas import tpu as pltpu
from jax.sharding import PartitionSpec as P

MESH = pl.DeviceIdType.MESH
HI = lax.Precision.HIGHEST
NT = (((1,), (1,)), ((), ()))
TN = (((0,), (0,)), ((), ()))
LOW = 256
BLOCK = 128


def product(a, b, dims=(((1,), (0,)), ((), ()))):
    return lax.dot_general(a, b, dims, precision=HI, preferred_element_type=jnp.float32)


def inverse_factor(d, hook):
    n = d.shape[0]
    lane = lax.broadcasted_iota(jnp.int32, (8, n), 1)
    sub = lax.broadcasted_iota(jnp.int32, (8, n), 0)
    tail = d.reshape(n // 8, 8, n)
    out = []
    for g in range(n // 8):
        base = 8 * g
        hook(g)
        cols = [jnp.broadcast_to(tail[:, :, base + k:base + k + 1], tail.shape) for k in range(8)]
        inside = (lane >= base) & (lane < base + 8)
        head = jnp.where(inside, jnp.where(lane - base == sub, 1.0, 0.0), tail[0])
        rest = jnp.where(inside[None], 0.0, tail[1:]) if g + 1 < n // 8 else None
        entry = {(i, k): jnp.broadcast_to(cols[k][0, i:i + 1, :], (8, n)) for i in range(8) for k in range(i + 1)}
        row = [jnp.broadcast_to(head[i:i + 1, :], (8, n)) for i in range(8)]
        below = [c[1:] for c in cols]
        done = jnp.zeros((8, n), jnp.float32)
        for j in range(8):
            scale = lax.rsqrt(entry[j, j])
            pivot_row = row[j] * scale
            done = jnp.where(sub == j, pivot_row, done)
            mult = {i: entry[i, j] * scale for i in range(j + 1, 8)}
            for i in range(j + 1, 8):
                row[i] = row[i] - mult[i] * pivot_row
                for k in range(j + 1, i + 1):
                    entry[i, k] = entry[i, k] - mult[i] * mult[k]
            if rest is not None:
                step = below[j] * scale[None]
                rest = rest - step * pivot_row[None]
                for k in range(j + 1, 8):
                    below[k] = below[k] - step * mult[k][None]
        out.append(jnp.where(lane <= sub + base, done, 0.0))
        tail = rest
    return jnp.concatenate(out, axis=0)


def whole_kernel(chips, grid, wedge_hbm, op_hbm, x_hbm, ec_ref, ev_ref, coulomb_hbm, gmap_hbm, out_ref,
                 wedge_ref, op_ref, x_ref, coulomb_ref, gmap_ref, scale_ref, g_ref,
                 lo_ref, hi_ref, s_ref, y_ref, p_ref, c1_recv, c2_send, c2_recv, e00_ref, total_ref,
                 pair_ref, send_ref, recv_ref, far_send_ref, far_recv_ref, f_ref, own_ref, left_ref, top_ref,
                 low_ref, w_ref,
                 c1_s, c1_r, c2_s, c2_r, c3_s, c3_r, c4_s, c4_r, c5_s, c5_r,
                 pair_s, pair_r, near_s, near_r, far_s, far_r, swap_s, swap_r,
                 top_s, top_r, side_s, side_r, ag_s, ag_r, fw_s, fw_r, in_s):
    kb, gr, gc = lax.axis_index("kb"), lax.axis_index("gr"), lax.axis_index("gc")
    z, c = kb // 2, kb % 2
    other = 1 - c
    slots, owners = wedge_ref.shape
    bands, total_g = x_ref.shape
    band, width = out_ref.shape
    rows, wide = 2 * band, width // 2
    is_top, is_left = gr == 0, gc == 0

    fetched = [
        pltpu.make_async_copy(src, dst, in_s.at[i])
        for i, (src, dst) in enumerate([
            (gmap_hbm, gmap_ref), (x_hbm, x_ref), (wedge_hbm, wedge_ref), (op_hbm, op_ref), (coulomb_hbm, coulomb_ref)
        ])
    ]
    for copy in fetched:
        copy.start()

    def chip(delta, core=None):
        return (2 * ((z + delta + chips) % chips) + (c if core is None else core), gr, gc)

    def remote(src, dst, send, recv, who):
        return pltpu.make_async_remote_copy(
            src_ref=src, dst_ref=dst, send_sem=send, recv_sem=recv, device_id=who, device_id_type=MESH
        )

    partner = (2 * z + other, gr, gc)
    peers = {
        i: (kb, (gr + i // grid) % grid, (gc + i % grid) % grid) for i in range(1, grid * grid)
    }
    barrier = pltpu.get_barrier_semaphore()
    everyone = (
        [chip(d, core) for d in (1, -1, 2, -2) for core in (0, 1)]
        + [chip(d) for d in (4, -4, 8)] + [partner] + list(peers.values())
    )
    for who in everyone:
        pl.semaphore_signal(barrier, inc=1, device_id=who, device_id_type=MESH)

    for copy in fetched:
        copy.wait()

    eye = lax.broadcasted_iota(jnp.int32, (bands, bands), 0) == lax.broadcasted_iota(jnp.int32, (bands, bands), 1)
    gap = ec_ref[...] - ev_ref[...]
    weight = jnp.sqrt(4.0 / (float(owners * slots) * gap))
    weight = jnp.sum(jnp.where(eye, jnp.broadcast_to(weight, (bands, bands)), 0.0), axis=1, keepdims=True)
    y = (x_ref[...].astype(jnp.float32) * weight).astype(jnp.bfloat16)
    parts = total_g // LOW
    for h in range(parts):
        y_ref[h * bands:(h + 1) * bands, :] = y[:, h * LOW:(h + 1) * LOW]
    matched = jnp.where(wedge_ref[...] == kb, 1.0, 0.0)
    present = jnp.sum(matched, axis=0, keepdims=True)
    operation = jnp.sum(matched * op_ref[...].astype(jnp.float32), axis=0, keepdims=True)
    kinds = lax.broadcasted_iota(jnp.int32, (gmap_ref.shape[0], owners), 0).astype(jnp.float32)
    chosen = jnp.where(kinds == operation, present, 0.0).astype(jnp.bfloat16)
    count = lax.broadcasted_iota(jnp.int32, (LOW, 128), 0).astype(jnp.float32).astype(jnp.bfloat16)
    one, none = jnp.ones((LOW, 128), jnp.bfloat16), jnp.zeros((LOW, 128), jnp.bfloat16)

    def gather(side, at):
        maps = gmap_ref[:, pl.ds(at, width)]
        low_bits = (maps & (LOW - 1)).astype(jnp.float32).astype(jnp.bfloat16)
        high_bits = ((maps >> (LOW.bit_length() - 1)) + 1).astype(jnp.float32).astype(jnp.bfloat16)
        lo_ref[...] = lax.dot_general(chosen, low_bits, TN, preferred_element_type=jnp.float32)
        hi_ref[...] = lax.dot_general(chosen, high_bits, TN, preferred_element_type=jnp.float32)

        def pick(o, carry):
            low = jnp.broadcast_to(lo_ref[pl.ds(o, 1), :], (LOW, width)).astype(jnp.bfloat16)
            high = hi_ref[pl.ds(o, 1), :]
            onehot = jnp.concatenate(
                [jnp.where(count == low[:, t:t + 128], one, none) for t in range(0, width, 128)], axis=1
            )
            spread = jnp.dot(y_ref[...], onehot, preferred_element_type=jnp.float32)
            picked = jnp.zeros((bands, width), jnp.float32)
            for h in range(parts):
                picked = jnp.where(high == float(h + 1), spread[h * bands:(h + 1) * bands, :], picked)
            s_ref[pl.ds(pl.multiple_of(o * bands, bands), bands), side * width:(side + 1) * width] = picked.astype(jnp.bfloat16)
            return carry

        lax.fori_loop(0, owners, pick, 0, unroll=4)

    root = jnp.sqrt(coulomb_ref[...])

    def root_down(first, count, reach):
        ids = first + lax.broadcasted_iota(jnp.int32, (count, reach), 0)
        lanes = lax.broadcasted_iota(jnp.int32, (count, reach), 1)
        return jnp.sum(jnp.where(ids == lanes, jnp.broadcast_to(root[:, :reach], (count, reach)), 0.0), axis=1, keepdims=True)

    def scale_of(first_row, first_col, count, across):
        return root_down(first_row, count, total_g) * jnp.sqrt(
            coulomb_ref[:, pl.ds(pl.multiple_of(first_col, 128), across)]
        )

    def dielectric(value, scale, first_row, first_col):
        row = first_row + lax.broadcasted_iota(jnp.int32, value.shape, 0)
        col = first_col + lax.broadcasted_iota(jnp.int32, value.shape, 1)
        return jnp.where(row == col, 1.0, 0.0) + scale * value

    gather(0, 0)
    p_ref[...] = lax.dot_general(
        s_ref[:, pl.ds(pl.multiple_of(gr * BLOCK, BLOCK), BLOCK)], s_ref[:, :width], TN, preferred_element_type=jnp.float32
    )
    pl.semaphore_wait(barrier, len(everyone))

    def p_part(delta, core):
        k = (z + delta + chips) % grid
        return p_ref.at[pl.ds(pl.multiple_of(gc * rows + 8 * k, 8), 8), pl.ds(pl.multiple_of(core * wide, wide), wide)]

    near_parts = [(1, 0, c), (1, 1, c), (-1, 0, 2 + c), (-1, 1, 2 + c), (2, 0, 4 + c), (-2, 1, 4 + c), (0, other, 6)]
    stage1 = [
        remote(p_part(d, core), c1_recv.at[slot], c1_s.at[i], c1_r.at[slot], chip(d, core))
        for i, (d, core, slot) in enumerate(near_parts)
    ]
    for copy in stage1:
        copy.start()

    gather(1, pl.multiple_of(gr * width, width))
    first_e = pl.multiple_of(gr * BLOCK + gc * rows + 8 * (z % grid), 8)
    scale_e = scale_of(first_e, c * wide, 8, wide)
    first_row, first_col = gr * width + z * rows, gc * width + c * wide
    scale_ref[...] = scale_of(first_row, first_col, rows, wide)

    value = p_part(0, c)[...]
    for slot in range(7):
        remote(p_part(0, other), c1_recv.at[slot], c1_s.at[0], c1_r.at[slot], partner).wait_recv()
        value = value + c1_recv[slot]
    c2_send[...] = value
    stage2 = [
        remote(c2_send, c2_recv.at[i], c2_s.at[i], c2_r.at[i], chip(d)) for i, d in enumerate((8, 4, -4))
    ]
    for copy in stage2:
        copy.start()

    gather(2, pl.multiple_of(gc * width, width))

    mine = pl.ds(pl.multiple_of(c * wide, wide), wide)
    theirs = pl.ds(pl.multiple_of(other * wide, wide), wide)
    total_ref[...] = lax.dot_general(
        s_ref[:, width:2 * width], s_ref[:, 2 * width:], TN, preferred_element_type=jnp.float32
    )

    def chunk(off):
        return pl.ds(pl.multiple_of(((z + off + chips) % chips) * rows, rows), rows)

    near = [
        (9, 1, 2), (7, -1, 6), (5, 1, 1), (3, -1, 5), (6, 2, 9), (-6, -2, 11),
        (13, 1, 3), (11, -1, 7), (1, 1, 0), (15, -1, 4), (2, 2, 8), (-2, -2, 10),
    ]
    order = [off % chips for off, _, _ in near] + [8, 4, 12, 0]
    pairs = {
        off: remote(total_ref.at[chunk(off), theirs], pair_ref.at[i], pair_s.at[i], pair_r.at[i], partner)
        for i, off in enumerate(order)
    }
    for off in order:
        pairs[off].start()

    value = c2_send[...]
    for i in (1, 2, 0):
        stage2[i].wait_recv()
        value = value + c2_recv[i]
    part = e00_ref.at[pl.ds(first_e, 8), mine]
    part[...] = dielectric(value, scale_e, first_e, c * wide)
    two = jnp.where(c == 0, 2, -2)
    spread_to = [(1, 0, c), (1, 1, c), (-1, 0, 2 + c), (-1, 1, 2 + c), (two, 0, 4 + c), (two, 1, 4 + c), (0, other, 6)]
    stage3 = [
        remote(part, part, c3_s.at[i], c3_r.at[slot], chip(d, core)) for i, (d, core, slot) in enumerate(spread_to)
    ]
    for copy in stage3:
        copy.start()

    def own_part(off):
        off = off % chips
        pairs[off].wait_recv()
        return total_ref[chunk(off), mine] + pair_ref[order.index(off)]

    near_copies = {}
    for off, delta, slot in near:
        send_ref[slot] = own_part(off)
        copy = remote(send_ref.at[slot], recv_ref.at[slot], near_s.at[slot], near_r.at[slot], chip(delta))
        copy.start()
        near_copies[slot] = copy

    for slot in range(7):
        remote(part, part, c3_s.at[0], c3_r.at[slot], partner).wait_recv()

    def e00_part(r, s, half):
        return e00_ref.at[pl.ds(pl.multiple_of(r * BLOCK + s * rows, rows), rows), half]

    def needed(r, core):
        return jnp.logical_or(core == 1, r < 2)

    def stage4(i):
        return remote(e00_part(gr, gc, mine), e00_part(gr, gc, mine), c4_s.at[i], c4_r.at[i], peers[i])

    def sender(i):
        return (gr + grid - i // grid) % grid, (gc + grid - i % grid) % grid

    @pl.when(needed(gr, c))
    def _():
        for i in peers:
            stage4(i).start()

    def stage5(i, half):
        r, s = sender(i)
        return remote(e00_part(r, s, half), e00_part(r, s, half), c5_s.at[i], c5_r.at[i], partner)


    def gathered(j, extra):
        value = own_part(4 * j)
        for slot in (j, 4 + j) + extra:
            near_copies[slot].wait_recv()
            value = value + recv_ref[slot]
        return value

    far_list = [(2, (), 8), (1, (9,), 4), (3, (11,), -4)]

    def far_copy(i):
        return remote(far_send_ref.at[i], far_recv_ref.at[i], far_s.at[i], far_r.at[i], chip(far_list[i][2]))

    def end_e00_copies():
        for copy in stage3:
            copy.wait_send()

        @pl.when(needed(gr, c))
        def _():
            for i in peers:
                stage4(i).wait_send()
        for i in peers:
            @pl.when(needed(sender(i)[0], c))
            def _():
                stage5(i, mine).wait_send()

    def send_far():
        for i, (j, extra, delta) in enumerate(far_list):
            far_send_ref[i] = gathered(j, extra)
            far_copy(i).start()

    my_top = top_ref.at[chunk(0), mine]

    def to_top(i):
        return remote(f_ref, my_top, top_s.at[i - 1], top_r, (kb, (gr + i) % grid, gc))

    swap = remote(f_ref.at[pl.ds(pl.multiple_of(other * band, band), band)], own_ref.at[:, mine], swap_s, swap_r, partner)

    def send_top():
        value = gathered(0, (8, 10))
        for i in (1, 2, 0):
            far_copy(i).wait_recv()
            value = value + far_recv_ref[i]
        value = dielectric(value, scale_ref[...], first_row, first_col)
        f_ref[...] = value

        @pl.when(is_top)
        def _():
            for i in range(1, grid):
                to_top(i).start()
            my_top[...] = value

        swap.start()
        own_ref[:, mine] = f_ref[pl.ds(pl.multiple_of(c * band, band), band)]

    def piece(off):
        return top_ref.at[chunk(off), mine]

    def forward(off):
        return remote(piece(off), piece(off), fw_s.at[off], fw_r.at[off], partner)

    gossip = {
        0: ((8, 0), (4, 1), (-4, 2), (1, 3), (-1, 4), (2, 5), (-2, 6)),
        4: ((1, 7), (-1, 8), (-2, 9)),
        12: ((1, 10), (-1, 11), (2, 12)),
        8: ((1, 13), (-1, 14)),
    }

    def gossip_copy(off, delta, i):
        return remote(piece(off), piece(off), ag_s.at[i], ag_r.at[(off - delta) % chips], chip(delta))

    def arrive(off):
        remote(piece(off), piece(off), ag_s.at[0], ag_r.at[off], partner).wait_recv()

    def to_side(i):
        return remote(own_ref, left_ref, side_s.at[i - 1], side_r, (kb, gr, (gc + i) % grid))

    def send_first():
        @pl.when(jnp.logical_not(is_top))
        def _():
            to_top(1).wait_recv()

        for delta, i in gossip[0]:
            gossip_copy(0, delta, i).start()
        forward(0).start()
        swap.wait_recv()

        @pl.when(is_left)
        def _():
            for i in range(1, grid):
                to_side(i).start()

    def send_second():
        for off in (4, 12, 8):
            arrive(off)
            for delta, i in gossip[off]:
                gossip_copy(off, delta, i).start()
            forward(off).start()

    send_far()
    for i in peers:
        @pl.when(needed(sender(i)[0], c))
        def _():
            stage4(i).wait_recv()
            stage5(i, mine).start()
    for i in peers:
        @pl.when(needed(sender(i)[0], other))
        def _():
            stage5(i, theirs).wait_recv()

    plan = {(0, 6): send_top, (0, 15): end_e00_copies, (1, 2): send_first, (3, 0): send_second}
    cuts = [slice(b * BLOCK, (b + 1) * BLOCK) for b in range(width // BLOCK)]
    for b, cut in enumerate(cuts):
        def hook(g):
            if (b, g) in plan:
                plan[b, g]()

        inverse = inverse_factor(e00_ref[cut, cut], hook)
        if b:
            g_ref[cut, :b * BLOCK] = product(inverse, g_ref[cut, :b * BLOCK])
        g_ref[cut, cut] = inverse
        after = (b + 1) * BLOCK
        if after < width:
            across = product(inverse, e00_ref[cut, after:])
            for cut2 in cuts[b + 1:]:
                at = cut2.start
                e00_ref[cut2, at:] = e00_ref[cut2, at:] - product(
                    across[:, at - after:at - after + BLOCK], across[:, at - after:], TN
                )
            change = product(across, g_ref[cut, :after], TN)
            if b:
                g_ref[after:, :cut.start] = g_ref[after:, :cut.start] - change[:, :cut.start]
            g_ref[after:, cut] = -change[:, cut.start:]

    @pl.when(jnp.logical_not(is_left))
    def _():
        to_side(1).wait_recv()

    @pl.when(is_left)
    def _():
        left_ref[...] = own_ref[...]

    for cut in cuts:
        low_ref[:, cut] = product(left_ref[:, :cut.stop], g_ref[cut, :cut.stop], NT)
    for cut in cuts:
        w_ref[:, cut] = product(low_ref[:, cut.start:], g_ref[cut.start:, cut])

    for off in (1, 15, 2, 14, 5, 3, 13, 11, 6, 10, 7, 9):
        arrive(off)
        forward(off).start()
    for off in range(chips):
        forward(off).wait_recv()

    row = kb * band + lax.broadcasted_iota(jnp.int32, (band, width), 0)
    col = lax.broadcasted_iota(jnp.int32, (band, width), 1)
    factor_side = jnp.where(is_top & (col > row), 0.0, low_ref[...])
    trail = own_ref[...] - product(w_ref[...], top_ref[...])
    out_ref[...] = jnp.where(is_left, factor_side, jnp.where(is_top, own_ref[...], trail))

    for copy in stage1 + stage2 + list(pairs.values()) + list(near_copies.values()) + [swap]:
        copy.wait_send()
    for i in range(3):
        far_copy(i).wait_send()
    for off, sends in gossip.items():
        for delta, i in sends:
            gossip_copy(off, delta, i).wait_send()
    for off in range(chips):
        forward(off).wait_send()

    @pl.when(is_top)
    def _():
        for i in range(1, grid):
            to_top(i).wait_send()

    @pl.when(is_left)
    def _():
        for i in range(1, grid):
            to_side(i).wait_send()


def body(wedge_pairs, e_cond, e_val, coulomb, owned_wedge, owned_op, gmap):
    members = lax.axis_size("kb")
    grid = lax.axis_size("gr")
    chips = members // 2
    total_g = gmap.shape[1]
    width = total_g // grid
    band = width // members
    owners, slots = owned_wedge.shape
    hbm = pl.BlockSpec(memory_space=pltpu.HBM)
    x = wedge_pairs.reshape(-1, total_g)
    bands = x.shape[0]
    vmem = pl.BlockSpec(memory_space=pltpu.VMEM)
    dma = pltpu.SemaphoreType.DMA
    piece = (2 * band, width // 2)
    f32 = jnp.float32
    return pl.pallas_call(
        functools.partial(whole_kernel, chips, grid),
        out_shape=jax.ShapeDtypeStruct((band, width), f32),
        in_specs=[hbm] * 3 + [vmem] * 2 + [hbm] * 2,
        out_specs=vmem,
        scratch_shapes=[
            pltpu.VMEM((slots, owners), jnp.int32),
            pltpu.VMEM((slots, owners), jnp.int32),
            pltpu.VMEM(x.shape, x.dtype),
            pltpu.VMEM((1, total_g), f32),
            pltpu.VMEM(gmap.shape, gmap.dtype),
            pltpu.VMEM(piece, f32),
            pltpu.VMEM((width, width), f32),
            pltpu.VMEM((owners, width), f32),
            pltpu.VMEM((owners, width), f32),
            pltpu.VMEM((owners * bands, 3 * width), jnp.bfloat16),
            pltpu.VMEM((bands * (total_g // LOW), LOW), jnp.bfloat16),
            pltpu.VMEM((BLOCK, width), f32),
            pltpu.VMEM((7, 8, width // 2), f32),
            pltpu.VMEM((8, width // 2), f32),
            pltpu.VMEM((3, 8, width // 2), f32),
            pltpu.VMEM((width, width), f32),
            pltpu.VMEM((width, width), f32),
            pltpu.VMEM((chips,) + piece, f32),
            pltpu.VMEM((12,) + piece, f32),
            pltpu.VMEM((12,) + piece, f32),
            pltpu.VMEM((3,) + piece, f32),
            pltpu.VMEM((3,) + piece, f32),
            pltpu.VMEM(piece, f32),
            pltpu.VMEM((band, width), f32),
            pltpu.VMEM((band, width), f32),
            pltpu.VMEM((width, width), f32),
            pltpu.VMEM((band, width), f32),
            pltpu.VMEM((band, width), f32),
            dma((7,)), dma((7,)),
            dma((3,)), dma((3,)),
            dma((7,)), dma((7,)),
            dma((grid * grid,)), dma((grid * grid,)),
            dma((grid * grid,)), dma((grid * grid,)),
            dma((chips,)), dma((chips,)),
            dma((12,)), dma((12,)),
            dma((3,)), dma((3,)),
            dma, dma,
            dma((grid - 1,)), dma,
            dma((grid - 1,)), dma,
            dma((15,)), dma((chips,)),
            dma((chips,)), dma((chips,)),
            dma((5,)),
        ],
        compiler_params=pltpu.CompilerParams(
            collective_id=0, has_side_effects=True, vmem_limit_bytes=63 << 20
        ),
        name="whole",
    )(owned_wedge.T, owned_op.T, x, e_cond, e_val, coulomb.reshape(1, -1), gmap)


def solution(mesh):
    placed = (P("kb", None, None, None), P("kb", None), P("kb", None), P(), P(), P(), P())
    return jax.shard_map(
        body, mesh=mesh, in_specs=placed, out_specs=P(("gr", "kb"), "gc"), check_vma=False
    )
```

```python
import functools
import jax
import jax.numpy as jnp
from jax import lax
from jax.experimental import pallas as pl
from jax.experimental.pallas import tpu as pltpu
from jax.sharding import PartitionSpec as P

MESH = pl.DeviceIdType.MESH
HI = lax.Precision.HIGHEST
NT = (((1,), (1,)), ((), ()))
TN = (((0,), (0,)), ((), ()))
LOW = 256
BLOCK = 128


def product(a, b, dims=(((1,), (0,)), ((), ()))):
    return lax.dot_general(a, b, dims, precision=HI, preferred_element_type=jnp.float32)


def inverse_factor(d, hook):
    n = d.shape[0]
    lane = lax.broadcasted_iota(jnp.int32, (8, n), 1)
    sub = lax.broadcasted_iota(jnp.int32, (8, n), 0)
    tail = d.reshape(n // 8, 8, n)
    out = []
    for g in range(n // 8):
        base = 8 * g
        hook(g)
        cols = [jnp.broadcast_to(tail[:, :, base + k:base + k + 1], tail.shape) for k in range(8)]
        inside = (lane >= base) & (lane < base + 8)
        head = jnp.where(inside, jnp.where(lane - base == sub, 1.0, 0.0), tail[0])
        rest = jnp.where(inside[None], 0.0, tail[1:]) if g + 1 < n // 8 else None
        entry = {(i, k): jnp.broadcast_to(cols[k][0, i:i + 1, :], (8, n)) for i in range(8) for k in range(i + 1)}
        row = [jnp.broadcast_to(head[i:i + 1, :], (8, n)) for i in range(8)]
        below = [c[1:] for c in cols]
        done = jnp.zeros((8, n), jnp.float32)
        for j in range(8):
            scale = lax.rsqrt(entry[j, j])
            pivot_row = row[j] * scale
            done = jnp.where(sub == j, pivot_row, done)
            mult = {i: entry[i, j] * scale for i in range(j + 1, 8)}
            for i in range(j + 1, 8):
                row[i] = row[i] - mult[i] * pivot_row
                for k in range(j + 1, i + 1):
                    entry[i, k] = entry[i, k] - mult[i] * mult[k]
            if rest is not None:
                step = below[j] * scale[None]
                rest = rest - step * pivot_row[None]
                for k in range(j + 1, 8):
                    below[k] = below[k] - step * mult[k][None]
        out.append(jnp.where(lane <= sub + base, done, 0.0))
        tail = rest
    return jnp.concatenate(out, axis=0)


def whole_kernel(chips, grid, wedge_hbm, op_hbm, x_hbm, ec_ref, ev_ref, coulomb_hbm, gmap_hbm, out_ref,
                 wedge_ref, op_ref, x_ref, coulomb_ref, gmap_ref, scale_ref, g_ref,
                 lo_ref, hi_ref, pt_ref, t1_recv, t2_send, t2_recv, t_scale_ref, s_ref, y_ref, p_ref, c1_recv, c2_send, c2_recv, e00_ref, total_ref,
                 pair_ref, send_ref, recv_ref, far_send_ref, far_recv_ref, f_ref, own_ref, left_ref, top_ref,
                 low_ref, w_ref,
                 c1_s, c1_r, c2_s, c2_r, c3_s, c3_r, c4_s, c4_r, c5_s, c5_r,
                 pair_s, pair_r, near_s, near_r, far_s, far_r, swap_s, swap_r,
                 side_s, side_r, t1_s, t1_r, t2_s, t2_r, t3_s, t3_r, t4_s, t4_r, t5_s, t5_r, in_s):
    kb, gr, gc = lax.axis_index("kb"), lax.axis_index("gr"), lax.axis_index("gc")
    z, c = kb // 2, kb % 2
    other = 1 - c
    slots, owners = wedge_ref.shape
    bands, total_g = x_ref.shape
    band, width = out_ref.shape
    rows, wide = 2 * band, width // 2
    is_top, is_left = gr == 0, gc == 0

    fetched = [
        pltpu.make_async_copy(src, dst, in_s.at[i])
        for i, (src, dst) in enumerate([
            (gmap_hbm, gmap_ref), (x_hbm, x_ref), (wedge_hbm, wedge_ref), (op_hbm, op_ref), (coulomb_hbm, coulomb_ref)
        ])
    ]
    for copy in fetched:
        copy.start()

    def chip(delta, core=None):
        return (2 * ((z + delta + chips) % chips) + (c if core is None else core), gr, gc)

    def remote(src, dst, send, recv, who):
        return pltpu.make_async_remote_copy(
            src_ref=src, dst_ref=dst, send_sem=send, recv_sem=recv, device_id=who, device_id_type=MESH
        )

    partner = (2 * z + other, gr, gc)
    peers = {
        i: (kb, (gr + i // grid) % grid, (gc + i % grid) % grid) for i in range(1, grid * grid)
    }
    barrier = pltpu.get_barrier_semaphore()
    everyone = (
        [chip(d, core) for d in (1, -1, 2, -2) for core in (0, 1)]
        + [chip(d) for d in (4, -4, 8)] + [partner] + list(peers.values())
    )
    for who in everyone:
        pl.semaphore_signal(barrier, inc=1, device_id=who, device_id_type=MESH)

    for copy in fetched:
        copy.wait()

    eye = lax.broadcasted_iota(jnp.int32, (bands, bands), 0) == lax.broadcasted_iota(jnp.int32, (bands, bands), 1)
    gap = ec_ref[...] - ev_ref[...]
    weight = jnp.sqrt(4.0 / (float(owners * slots) * gap))
    weight = jnp.sum(jnp.where(eye, jnp.broadcast_to(weight, (bands, bands)), 0.0), axis=1, keepdims=True)
    y = (x_ref[...].astype(jnp.float32) * weight).astype(jnp.bfloat16)
    parts = total_g // LOW
    for h in range(parts):
        y_ref[h * bands:(h + 1) * bands, :] = y[:, h * LOW:(h + 1) * LOW]
    matched = jnp.where(wedge_ref[...] == kb, 1.0, 0.0)
    present = jnp.sum(matched, axis=0, keepdims=True)
    operation = jnp.sum(matched * op_ref[...].astype(jnp.float32), axis=0, keepdims=True)
    kinds = lax.broadcasted_iota(jnp.int32, (gmap_ref.shape[0], owners), 0).astype(jnp.float32)
    chosen = jnp.where(kinds == operation, present, 0.0).astype(jnp.bfloat16)
    count = lax.broadcasted_iota(jnp.int32, (LOW, 128), 0).astype(jnp.float32).astype(jnp.bfloat16)
    one, none = jnp.ones((LOW, 128), jnp.bfloat16), jnp.zeros((LOW, 128), jnp.bfloat16)

    def gather(side, at):
        maps = gmap_ref[:, pl.ds(at, width)]
        low_bits = (maps & (LOW - 1)).astype(jnp.float32).astype(jnp.bfloat16)
        high_bits = ((maps >> (LOW.bit_length() - 1)) + 1).astype(jnp.float32).astype(jnp.bfloat16)
        lo_ref[...] = lax.dot_general(chosen, low_bits, TN, preferred_element_type=jnp.float32)
        hi_ref[...] = lax.dot_general(chosen, high_bits, TN, preferred_element_type=jnp.float32)

        def pick(o, carry):
            low = jnp.broadcast_to(lo_ref[pl.ds(o, 1), :], (LOW, width)).astype(jnp.bfloat16)
            high = hi_ref[pl.ds(o, 1), :]
            onehot = jnp.concatenate(
                [jnp.where(count == low[:, t:t + 128], one, none) for t in range(0, width, 128)], axis=1
            )
            spread = jnp.dot(y_ref[...], onehot, preferred_element_type=jnp.float32)
            picked = jnp.zeros((bands, width), jnp.float32)
            for h in range(parts):
                picked = jnp.where(high == float(h + 1), spread[h * bands:(h + 1) * bands, :], picked)
            s_ref[pl.ds(pl.multiple_of(o * bands, bands), bands), side * width:(side + 1) * width] = picked.astype(jnp.bfloat16)
            return carry

        lax.fori_loop(0, owners, pick, 0, unroll=4)

    root = jnp.sqrt(coulomb_ref[...])

    def root_down(first, count, reach):
        ids = first + lax.broadcasted_iota(jnp.int32, (count, reach), 0)
        lanes = lax.broadcasted_iota(jnp.int32, (count, reach), 1)
        return jnp.sum(jnp.where(ids == lanes, jnp.broadcast_to(root[:, :reach], (count, reach)), 0.0), axis=1, keepdims=True)

    def scale_of(first_row, first_col, count, across):
        return root_down(first_row, count, total_g) * jnp.sqrt(
            coulomb_ref[:, pl.ds(pl.multiple_of(first_col, 128), across)]
        )

    def dielectric(value, scale, first_row, first_col):
        row = first_row + lax.broadcasted_iota(jnp.int32, value.shape, 0)
        col = first_col + lax.broadcasted_iota(jnp.int32, value.shape, 1)
        return jnp.where(row == col, 1.0, 0.0) + scale * value

    gather(0, 0)
    p_ref[...] = lax.dot_general(
        s_ref[:, pl.ds(pl.multiple_of(gr * BLOCK, BLOCK), BLOCK)], s_ref[:, :width], TN, preferred_element_type=jnp.float32
    )
    pl.semaphore_wait(barrier, len(everyone))

    def p_part(delta, core):
        k = (z + delta + chips) % grid
        return p_ref.at[pl.ds(pl.multiple_of(gc * rows + 8 * k, 8), 8), pl.ds(pl.multiple_of(core * wide, wide), wide)]

    near_parts = [(1, 0, c), (1, 1, c), (-1, 0, 2 + c), (-1, 1, 2 + c), (2, 0, 4 + c), (-2, 1, 4 + c), (0, other, 6)]
    stage1 = [
        remote(p_part(d, core), c1_recv.at[slot], c1_s.at[i], c1_r.at[slot], chip(d, core))
        for i, (d, core, slot) in enumerate(near_parts)
    ]
    for copy in stage1:
        copy.start()

    mine = pl.ds(pl.multiple_of(c * wide, wide), wide)
    theirs = pl.ds(pl.multiple_of(other * wide, wide), wide)

    gather(2, pl.multiple_of(gc * width, width))
    pt_ref[...] = lax.dot_general(
        s_ref[:, pl.ds(pl.multiple_of(gr * BLOCK, BLOCK), BLOCK)], s_ref[:, 2 * width:], TN, preferred_element_type=jnp.float32
    )

    def t_part(delta, core):
        k = (z + delta + chips) % grid
        return pt_ref.at[pl.ds(pl.multiple_of(rows * k, rows), rows), pl.ds(pl.multiple_of(core * wide, wide), wide)]

    top1 = [
        remote(t_part(d, core), t1_recv.at[slot], t1_s.at[i], t1_r.at[slot], chip(d, core))
        for i, (d, core, slot) in enumerate(near_parts)
    ]
    for copy in top1:
        copy.start()

    first_e = pl.multiple_of(gr * BLOCK + gc * rows + 8 * (z % grid), 8)
    scale_e = scale_of(first_e, c * wide, 8, wide)
    first_row, first_col = gr * width + z * rows, gc * width + c * wide
    first_t = pl.multiple_of(gr * BLOCK + rows * (z % grid), rows)
    scale_ref[...] = scale_of(first_row, first_col, rows, wide)
    t_scale_ref[...] = scale_of(first_t, first_col, rows, wide)

    value = p_part(0, c)[...]
    for slot in range(7):
        remote(p_part(0, other), c1_recv.at[slot], c1_s.at[0], c1_r.at[slot], partner).wait_recv()
        value = value + c1_recv[slot]
    c2_send[...] = value
    stage2 = [
        remote(c2_send, c2_recv.at[i], c2_s.at[i], c2_r.at[i], chip(d)) for i, d in enumerate((8, 4, -4))
    ]
    for copy in stage2:
        copy.start()

    gather(1, pl.multiple_of(gr * width, width))
    total_ref[...] = lax.dot_general(
        s_ref[:, width:2 * width], s_ref[:, 2 * width:], TN, preferred_element_type=jnp.float32
    )

    def chunk(off):
        return pl.ds(pl.multiple_of(((z + off + chips) % chips) * rows, rows), rows)

    near = [
        (9, 1, 2), (7, -1, 6), (5, 1, 1), (3, -1, 5), (6, 2, 9), (-6, -2, 11),
        (13, 1, 3), (11, -1, 7), (1, 1, 0), (15, -1, 4), (2, 2, 8), (-2, -2, 10),
    ]
    order = [off % chips for off, _, _ in near] + [8, 4, 12, 0]
    pairs = {
        off: remote(total_ref.at[chunk(off), theirs], pair_ref.at[i], pair_s.at[i], pair_r.at[i], partner)
        for i, off in enumerate(order)
    }
    for off in order:
        pairs[off].start()

    value = c2_send[...]
    for i in (1, 2, 0):
        stage2[i].wait_recv()
        value = value + c2_recv[i]
    part = e00_ref.at[pl.ds(first_e, 8), mine]
    part[...] = dielectric(value, scale_e, first_e, c * wide)
    two = jnp.where(c == 0, 2, -2)
    spread_to = [(1, 0, c), (1, 1, c), (-1, 0, 2 + c), (-1, 1, 2 + c), (two, 0, 4 + c), (two, 1, 4 + c), (0, other, 6)]
    stage3 = [
        remote(part, part, c3_s.at[i], c3_r.at[slot], chip(d, core)) for i, (d, core, slot) in enumerate(spread_to)
    ]
    for copy in stage3:
        copy.start()

    value = t_part(0, c)[...]
    for slot in range(7):
        remote(t_part(0, other), t1_recv.at[slot], t1_s.at[0], t1_r.at[slot], partner).wait_recv()
        value = value + t1_recv[slot]
    t2_send[...] = value
    top2 = [
        remote(t2_send, t2_recv.at[i], t2_s.at[i], t2_r.at[i], chip(d)) for i, d in enumerate((8, 4, -4))
    ]
    for copy in top2:
        copy.start()

    def own_part(off):
        off = off % chips
        pairs[off].wait_recv()
        return total_ref[chunk(off), mine] + pair_ref[order.index(off)]

    near_copies = {}
    for off, delta, slot in near:
        send_ref[slot] = own_part(off)
        copy = remote(send_ref.at[slot], recv_ref.at[slot], near_s.at[slot], near_r.at[slot], chip(delta))
        copy.start()
        near_copies[slot] = copy

    for slot in range(7):
        remote(part, part, c3_s.at[0], c3_r.at[slot], partner).wait_recv()

    def e00_part(r, s, half):
        return e00_ref.at[pl.ds(pl.multiple_of(r * BLOCK + s * rows, rows), rows), half]

    def needed(r, core):
        return jnp.logical_or(core == 1, r < 2)

    def stage4(i):
        return remote(e00_part(gr, gc, mine), e00_part(gr, gc, mine), c4_s.at[i], c4_r.at[i], peers[i])

    def sender(i):
        return (gr + grid - i // grid) % grid, (gc + grid - i % grid) % grid

    @pl.when(needed(gr, c))
    def _():
        for i in peers:
            stage4(i).start()

    value = t2_send[...]
    for i in (1, 2, 0):
        top2[i].wait_recv()
        value = value + t2_recv[i]
    t_piece = top_ref.at[pl.ds(first_t, rows), mine]
    t_piece[...] = dielectric(value, t_scale_ref[...], first_t, first_col)
    top3 = [
        remote(t_piece, t_piece, t3_s.at[i], t3_r.at[slot], chip(d, core)) for i, (d, core, slot) in enumerate(spread_to)
    ]
    for copy in top3:
        copy.start()

    def quarter(r):
        return top_ref.at[pl.ds(pl.multiple_of(r * BLOCK, BLOCK), BLOCK), mine]

    def to_column(i):
        return remote(quarter(gr), quarter(gr), t4_s.at[i - 1], t4_r.at[i - 1], (kb, (gr + i) % grid, gc))

    def to_core(i):
        r = (gr + grid - i) % grid
        return remote(quarter(r), quarter(r), t5_s.at[i - 1], t5_r.at[i - 1], partner)

    def send_column():
        for slot in range(7):
            remote(t_piece, t_piece, t3_s.at[0], t3_r.at[slot], partner).wait_recv()
        for i in range(1, grid):
            to_column(i).start()

    def send_core():
        for i in range(1, grid):
            to_column(i).wait_recv()
            to_core(i).start()

    def stage5(i, half):
        r, s = sender(i)
        return remote(e00_part(r, s, half), e00_part(r, s, half), c5_s.at[i], c5_r.at[i], partner)


    def gathered(j, extra):
        value = own_part(4 * j)
        for slot in (j, 4 + j) + extra:
            near_copies[slot].wait_recv()
            value = value + recv_ref[slot]
        return value

    far_list = [(2, (), 8), (1, (9,), 4), (3, (11,), -4)]

    def far_copy(i):
        return remote(far_send_ref.at[i], far_recv_ref.at[i], far_s.at[i], far_r.at[i], chip(far_list[i][2]))

    def end_e00_copies():
        for copy in stage3:
            copy.wait_send()

        @pl.when(needed(gr, c))
        def _():
            for i in peers:
                stage4(i).wait_send()
        for i in peers:
            @pl.when(needed(sender(i)[0], c))
            def _():
                stage5(i, mine).wait_send()

    def send_far():
        for i, (j, extra, delta) in enumerate(far_list):
            far_send_ref[i] = gathered(j, extra)
            far_copy(i).start()

    swap = remote(f_ref.at[pl.ds(pl.multiple_of(other * band, band), band)], own_ref.at[:, mine], swap_s, swap_r, partner)

    def send_own():
        value = gathered(0, (8, 10))
        for i in (1, 2, 0):
            far_copy(i).wait_recv()
            value = value + far_recv_ref[i]
        value = dielectric(value, scale_ref[...], first_row, first_col)
        f_ref[...] = value

        swap.start()
        own_ref[:, mine] = f_ref[pl.ds(pl.multiple_of(c * band, band), band)]

    def to_side(i):
        return remote(own_ref, left_ref, side_s.at[i - 1], side_r, (kb, gr, (gc + i) % grid))

    def send_side():
        swap.wait_recv()

        @pl.when(is_left)
        def _():
            for i in range(1, grid):
                to_side(i).start()

    def wait_rows(r):
        for i in peers:
            @pl.when((sender(i)[0] == r) & needed(r, c))
            def _():
                stage4(i).wait_recv()
                stage5(i, mine).start()

    def wait_halves(r):
        for i in peers:
            @pl.when((sender(i)[0] == r) & needed(r, other))
            def _():
                stage5(i, theirs).wait_recv()

    def wait_later_rows():
        for r in range(1, grid):
            wait_rows(r)

    def wait_later_halves():
        for r in range(1, grid):
            wait_halves(r)

    wait_rows(0)
    wait_halves(0)
    plan = {
        (0, 4): wait_later_rows, (0, 8): send_column, (0, 11): wait_later_halves, (0, 13): send_far, (0, 15): end_e00_copies,
        (2, 8): send_own, (3, 0): send_core, (3, 6): send_side,
    }
    cuts = [slice(b * BLOCK, (b + 1) * BLOCK) for b in range(width // BLOCK)]
    for b, cut in enumerate(cuts):
        def hook(g):
            if (b, g) in plan:
                plan[b, g]()

        inverse = inverse_factor(e00_ref[cut, cut], hook)
        if b:
            g_ref[cut, :b * BLOCK] = product(inverse, g_ref[cut, :b * BLOCK])
        g_ref[cut, cut] = inverse
        after = (b + 1) * BLOCK
        if after < width:
            across = product(inverse, e00_ref[cut, after:])
            for cut2 in cuts[b + 1:]:
                at = cut2.start
                e00_ref[cut2, at:] = e00_ref[cut2, at:] - product(
                    across[:, at - after:at - after + BLOCK], across[:, at - after:], TN
                )
            change = product(across, g_ref[cut, :after], TN)
            if b:
                g_ref[after:, :cut.start] = g_ref[after:, :cut.start] - change[:, :cut.start]
            g_ref[after:, cut] = -change[:, cut.start:]

    @pl.when(jnp.logical_not(is_left))
    def _():
        to_side(1).wait_recv()

    @pl.when(is_left)
    def _():
        left_ref[...] = own_ref[...]

    for cut in cuts:
        low_ref[:, cut] = product(left_ref[:, :cut.stop], g_ref[cut, :cut.stop], NT)
    for cut in cuts:
        w_ref[:, cut] = product(low_ref[:, cut.start:], g_ref[cut.start:, cut])

    for i in range(1, grid):
        to_core(i).wait_recv()

    row = kb * band + lax.broadcasted_iota(jnp.int32, (band, width), 0)
    col = lax.broadcasted_iota(jnp.int32, (band, width), 1)
    factor_side = jnp.where(is_top & (col > row), 0.0, low_ref[...])
    trail = own_ref[...] - product(w_ref[...], top_ref[...])
    out_ref[...] = jnp.where(is_left, factor_side, jnp.where(is_top, own_ref[...], trail))

    for copy in stage1 + stage2 + top1 + top2 + top3 + list(pairs.values()) + list(near_copies.values()) + [swap]:
        copy.wait_send()
    for i in range(3):
        far_copy(i).wait_send()
    for i in range(1, grid):
        to_column(i).wait_send()
        to_core(i).wait_send()

    @pl.when(is_left)
    def _():
        for i in range(1, grid):
            to_side(i).wait_send()


def body(wedge_pairs, e_cond, e_val, coulomb, owned_wedge, owned_op, gmap):
    members = lax.axis_size("kb")
    grid = lax.axis_size("gr")
    chips = members // 2
    total_g = gmap.shape[1]
    width = total_g // grid
    band = width // members
    owners, slots = owned_wedge.shape
    hbm = pl.BlockSpec(memory_space=pltpu.HBM)
    x = wedge_pairs.reshape(-1, total_g)
    bands = x.shape[0]
    vmem = pl.BlockSpec(memory_space=pltpu.VMEM)
    dma = pltpu.SemaphoreType.DMA
    piece = (2 * band, width // 2)
    f32 = jnp.float32
    return pl.pallas_call(
        functools.partial(whole_kernel, chips, grid),
        out_shape=jax.ShapeDtypeStruct((band, width), f32),
        in_specs=[hbm] * 3 + [vmem] * 2 + [hbm] * 2,
        out_specs=vmem,
        scratch_shapes=[
            pltpu.VMEM((slots, owners), jnp.int32),
            pltpu.VMEM((slots, owners), jnp.int32),
            pltpu.VMEM(x.shape, x.dtype),
            pltpu.VMEM((1, total_g), f32),
            pltpu.VMEM(gmap.shape, gmap.dtype),
            pltpu.VMEM(piece, f32),
            pltpu.VMEM((width, width), f32),
            pltpu.VMEM((owners, width), f32),
            pltpu.VMEM((owners, width), f32),
            pltpu.VMEM((BLOCK, width), f32),
            pltpu.VMEM((7,) + piece, f32),
            pltpu.VMEM(piece, f32),
            pltpu.VMEM((3,) + piece, f32),
            pltpu.VMEM(piece, f32),
            pltpu.VMEM((owners * bands, 3 * width), jnp.bfloat16),
            pltpu.VMEM((bands * (total_g // LOW), LOW), jnp.bfloat16),
            pltpu.VMEM((BLOCK, width), f32),
            pltpu.VMEM((7, 8, width // 2), f32),
            pltpu.VMEM((8, width // 2), f32),
            pltpu.VMEM((3, 8, width // 2), f32),
            pltpu.VMEM((width, width), f32),
            pltpu.VMEM((width, width), f32),
            pltpu.VMEM((chips,) + piece, f32),
            pltpu.VMEM((12,) + piece, f32),
            pltpu.VMEM((12,) + piece, f32),
            pltpu.VMEM((3,) + piece, f32),
            pltpu.VMEM((3,) + piece, f32),
            pltpu.VMEM(piece, f32),
            pltpu.VMEM((band, width), f32),
            pltpu.VMEM((band, width), f32),
            pltpu.VMEM((width, width), f32),
            pltpu.VMEM((band, width), f32),
            pltpu.VMEM((band, width), f32),
            dma((7,)), dma((7,)),
            dma((3,)), dma((3,)),
            dma((7,)), dma((7,)),
            dma((grid * grid,)), dma((grid * grid,)),
            dma((grid * grid,)), dma((grid * grid,)),
            dma((chips,)), dma((chips,)),
            dma((12,)), dma((12,)),
            dma((3,)), dma((3,)),
            dma, dma,
            dma((grid - 1,)), dma,
            dma((7,)), dma((7,)),
            dma((3,)), dma((3,)),
            dma((7,)), dma((7,)),
            dma((grid - 1,)), dma((grid - 1,)),
            dma((grid - 1,)), dma((grid - 1,)),
            dma((5,)),
        ],
        compiler_params=pltpu.CompilerParams(
            collective_id=0, has_side_effects=True, vmem_limit_bytes=63 << 20
        ),
        name="whole",
    )(owned_wedge.T, owned_op.T, x, e_cond, e_val, coulomb.reshape(1, -1), gmap)


def solution(mesh):
    placed = (P("kb", None, None, None), P("kb", None), P("kb", None), P(), P(), P(), P())
    return jax.shard_map(
        body, mesh=mesh, in_specs=placed, out_specs=P(("gr", "kb"), "gc"), check_vma=False
    )
```

```python
import functools
import jax
import jax.numpy as jnp
from jax import lax
from jax.experimental import pallas as pl
from jax.experimental.pallas import tpu as pltpu
from jax.sharding import PartitionSpec as P

MESH = pl.DeviceIdType.MESH
HI = lax.Precision.HIGHEST
NT = (((1,), (1,)), ((), ()))
TN = (((0,), (0,)), ((), ()))
LOW = 256
BLOCK = 128


def product(a, b, dims=(((1,), (0,)), ((), ()))):
    return lax.dot_general(a, b, dims, precision=HI, preferred_element_type=jnp.float32)


def thirds(a):
    first = a.astype(jnp.bfloat16).astype(jnp.float32)
    second = (a - first).astype(jnp.bfloat16).astype(jnp.float32)
    return first, second, a - first - second


def gram(rows):
    p, q, r = thirds(rows)
    one = jnp.concatenate([p, p, q, p, r, q], axis=0).astype(jnp.bfloat16)
    two = jnp.concatenate([p, q, p, r, p, q], axis=0).astype(jnp.bfloat16)
    return lax.dot_general(one, two, TN, preferred_element_type=jnp.float32)


def inverse_factor(d, hook):
    n = d.shape[0]
    groups = n // 8
    lane = lax.broadcasted_iota(jnp.int32, (8, n), 1)
    sub = lax.broadcasted_iota(jnp.int32, (8, n), 0)
    rows = [d[8 * i:8 * i + 8, :] for i in range(groups)]
    out = []
    for g in range(groups):
        base = 8 * g
        hook(g)
        follows = g + 1 < groups
        head, after = rows[g], rows[g + 1] if follows else None
        cols = [jnp.broadcast_to(head[:, base + k:base + k + 1], (8, n)) for k in range(8)]
        below = [jnp.broadcast_to(after[:, base + k:base + k + 1], (8, n)) for k in range(8)] if follows else None
        inside = (lane >= base) & (lane < base + 8)
        head = jnp.where(inside, jnp.where(lane - base == sub, 1.0, 0.0), head)
        if follows:
            after = jnp.where(inside, 0.0, after)
        entry = {(i, k): jnp.broadcast_to(cols[k][i:i + 1, :], (8, n)) for i in range(8) for k in range(i + 1)}
        row = [jnp.broadcast_to(head[i:i + 1, :], (8, n)) for i in range(8)]
        done = jnp.zeros((8, n), jnp.float32)
        for j in range(8):
            scale = lax.rsqrt(entry[j, j])
            pivot_row = row[j] * scale
            done = jnp.where(sub == j, pivot_row, done)
            mult = {i: entry[i, j] * scale for i in range(j + 1, 8)}
            for i in range(j + 1, 8):
                row[i] = row[i] - mult[i] * pivot_row
                for k in range(j + 1, i + 1):
                    entry[i, k] = entry[i, k] - mult[i] * mult[k]
            if follows:
                step = below[j] * scale
                after = after - step * pivot_row
                for k in range(j + 1, 8):
                    below[k] = below[k] - step * mult[k]
        out.append(jnp.where(lane <= sub + base, done, 0.0))
        if follows:
            rows[g + 1] = after
        if g + 2 < groups:
            change = gram(done)
            for i in range(g + 2, groups):
                rows[i] = jnp.where(inside, 0.0, rows[i]) - change[8 * i:8 * i + 8, :]
    return jnp.concatenate(out, axis=0)


def whole_kernel(chips, grid, wedge_hbm, op_hbm, x_hbm, ec_ref, ev_ref, coulomb_hbm, gmap_hbm, out_ref,
                 wedge_ref, op_ref, x_ref, coulomb_ref, gmap_ref, scale_ref, g_ref,
                 lo_ref, hi_ref, pt_ref, t1_recv, t2_send, t2_recv, t_scale_ref, s_ref, y_ref, p_ref, c1_recv, c2_send, c2_recv, e00_ref, total_ref,
                 pair_ref, send_ref, recv_ref, far_send_ref, far_recv_ref, f_ref, own_ref, left_ref, top_ref,
                 low_ref, w_ref,
                 c1_s, c1_r, c2_s, c2_r, c3_s, c3_r, c4_s, c4_r, c5_s, c5_r,
                 pair_s, pair_r, near_s, near_r, far_s, far_r, swap_s, swap_r,
                 side_s, side_r, t1_s, t1_r, t2_s, t2_r, t3_s, t3_r, t4_s, t4_r, t5_s, t5_r, in_s):
    kb, gr, gc = lax.axis_index("kb"), lax.axis_index("gr"), lax.axis_index("gc")
    z, c = kb // 2, kb % 2
    other = 1 - c
    slots, owners = wedge_ref.shape
    bands, total_g = x_ref.shape
    band, width = out_ref.shape
    rows, wide = 2 * band, width // 2
    is_top, is_left = gr == 0, gc == 0

    fetched = [
        pltpu.make_async_copy(src, dst, in_s.at[i])
        for i, (src, dst) in enumerate([
            (gmap_hbm, gmap_ref), (x_hbm, x_ref), (wedge_hbm, wedge_ref), (op_hbm, op_ref), (coulomb_hbm, coulomb_ref)
        ])
    ]
    for copy in fetched:
        copy.start()

    def chip(delta, core=None):
        return (2 * ((z + delta + chips) % chips) + (c if core is None else core), gr, gc)

    def remote(src, dst, send, recv, who):
        return pltpu.make_async_remote_copy(
            src_ref=src, dst_ref=dst, send_sem=send, recv_sem=recv, device_id=who, device_id_type=MESH
        )

    partner = (2 * z + other, gr, gc)
    peers = {
        i: (kb, (gr + i // grid) % grid, (gc + i % grid) % grid) for i in range(1, grid * grid)
    }
    barrier = pltpu.get_barrier_semaphore()
    everyone = (
        [chip(d, core) for d in (1, -1, 2, -2) for core in (0, 1)]
        + [chip(d) for d in (4, -4, 8)] + [partner] + list(peers.values())
    )
    for who in everyone:
        pl.semaphore_signal(barrier, inc=1, device_id=who, device_id_type=MESH)

    for copy in fetched:
        copy.wait()

    eye = lax.broadcasted_iota(jnp.int32, (bands, bands), 0) == lax.broadcasted_iota(jnp.int32, (bands, bands), 1)
    gap = ec_ref[...] - ev_ref[...]
    weight = jnp.sqrt(4.0 / (float(owners * slots) * gap))
    weight = jnp.sum(jnp.where(eye, jnp.broadcast_to(weight, (bands, bands)), 0.0), axis=1, keepdims=True)
    y = (x_ref[...].astype(jnp.float32) * weight).astype(jnp.bfloat16)
    parts = total_g // LOW
    for h in range(parts):
        y_ref[h * bands:(h + 1) * bands, :] = y[:, h * LOW:(h + 1) * LOW]
    matched = jnp.where(wedge_ref[...] == kb, 1.0, 0.0)
    present = jnp.sum(matched, axis=0, keepdims=True)
    operation = jnp.sum(matched * op_ref[...].astype(jnp.float32), axis=0, keepdims=True)
    kinds = lax.broadcasted_iota(jnp.int32, (gmap_ref.shape[0], owners), 0).astype(jnp.float32)
    chosen = jnp.where(kinds == operation, present, 0.0).astype(jnp.bfloat16)
    count = lax.broadcasted_iota(jnp.int32, (LOW, 128), 0).astype(jnp.float32).astype(jnp.bfloat16)
    one, none = jnp.ones((LOW, 128), jnp.bfloat16), jnp.zeros((LOW, 128), jnp.bfloat16)

    def gather(side, at):
        maps = gmap_ref[:, pl.ds(at, width)]
        low_bits = (maps & (LOW - 1)).astype(jnp.float32).astype(jnp.bfloat16)
        high_bits = ((maps >> (LOW.bit_length() - 1)) + 1).astype(jnp.float32).astype(jnp.bfloat16)
        lo_ref[...] = lax.dot_general(chosen, low_bits, TN, preferred_element_type=jnp.float32)
        hi_ref[...] = lax.dot_general(chosen, high_bits, TN, preferred_element_type=jnp.float32)

        def pick(o, carry):
            low = jnp.broadcast_to(lo_ref[pl.ds(o, 1), :], (LOW, width)).astype(jnp.bfloat16)
            high = hi_ref[pl.ds(o, 1), :]
            onehot = jnp.concatenate(
                [jnp.where(count == low[:, t:t + 128], one, none) for t in range(0, width, 128)], axis=1
            )
            spread = jnp.dot(y_ref[...], onehot, preferred_element_type=jnp.float32)
            picked = jnp.zeros((bands, width), jnp.float32)
            for h in range(parts):
                picked = jnp.where(high == float(h + 1), spread[h * bands:(h + 1) * bands, :], picked)
            s_ref[pl.ds(pl.multiple_of(o * bands, bands), bands), side * width:(side + 1) * width] = picked.astype(jnp.bfloat16)
            return carry

        lax.fori_loop(0, owners, pick, 0, unroll=4)

    root = jnp.sqrt(coulomb_ref[...])

    def root_down(first, count, reach):
        ids = first + lax.broadcasted_iota(jnp.int32, (count, reach), 0)
        lanes = lax.broadcasted_iota(jnp.int32, (count, reach), 1)
        return jnp.sum(jnp.where(ids == lanes, jnp.broadcast_to(root[:, :reach], (count, reach)), 0.0), axis=1, keepdims=True)

    def scale_of(first_row, first_col, count, across):
        return root_down(first_row, count, total_g) * jnp.sqrt(
            coulomb_ref[:, pl.ds(pl.multiple_of(first_col, 128), across)]
        )

    def dielectric(value, scale, first_row, first_col):
        row = first_row + lax.broadcasted_iota(jnp.int32, value.shape, 0)
        col = first_col + lax.broadcasted_iota(jnp.int32, value.shape, 1)
        return jnp.where(row == col, 1.0, 0.0) + scale * value

    gather(0, 0)
    p_ref[...] = lax.dot_general(
        s_ref[:, pl.ds(pl.multiple_of(gr * BLOCK, BLOCK), BLOCK)], s_ref[:, :width], TN, preferred_element_type=jnp.float32
    )
    pl.semaphore_wait(barrier, len(everyone))

    def p_part(delta, core):
        k = (z + delta + chips) % grid
        return p_ref.at[pl.ds(pl.multiple_of(gc * rows + 8 * k, 8), 8), pl.ds(pl.multiple_of(core * wide, wide), wide)]

    near_parts = [(1, 0, c), (1, 1, c), (-1, 0, 2 + c), (-1, 1, 2 + c), (2, 0, 4 + c), (-2, 1, 4 + c), (0, other, 6)]
    stage1 = [
        remote(p_part(d, core), c1_recv.at[slot], c1_s.at[i], c1_r.at[slot], chip(d, core))
        for i, (d, core, slot) in enumerate(near_parts)
    ]
    for copy in stage1:
        copy.start()

    mine = pl.ds(pl.multiple_of(c * wide, wide), wide)
    theirs = pl.ds(pl.multiple_of(other * wide, wide), wide)

    gather(2, pl.multiple_of(gc * width, width))
    pt_ref[...] = lax.dot_general(
        s_ref[:, pl.ds(pl.multiple_of(gr * BLOCK, BLOCK), BLOCK)], s_ref[:, 2 * width:], TN, preferred_element_type=jnp.float32
    )

    def t_part(delta, core):
        k = (z + delta + chips) % grid
        return pt_ref.at[pl.ds(pl.multiple_of(rows * k, rows), rows), pl.ds(pl.multiple_of(core * wide, wide), wide)]

    top1 = [
        remote(t_part(d, core), t1_recv.at[slot], t1_s.at[i], t1_r.at[slot], chip(d, core))
        for i, (d, core, slot) in enumerate(near_parts)
    ]
    for copy in top1:
        copy.start()

    first_e = pl.multiple_of(gr * BLOCK + gc * rows + 8 * (z % grid), 8)
    scale_e = scale_of(first_e, c * wide, 8, wide)
    first_row, first_col = gr * width + z * rows, gc * width + c * wide
    first_t = pl.multiple_of(gr * BLOCK + rows * (z % grid), rows)
    scale_ref[...] = scale_of(first_row, first_col, rows, wide)
    t_scale_ref[...] = scale_of(first_t, first_col, rows, wide)

    value = p_part(0, c)[...]
    for slot in range(7):
        remote(p_part(0, other), c1_recv.at[slot], c1_s.at[0], c1_r.at[slot], partner).wait_recv()
        value = value + c1_recv[slot]
    c2_send[...] = value
    stage2 = [
        remote(c2_send, c2_recv.at[i], c2_s.at[i], c2_r.at[i], chip(d)) for i, d in enumerate((8, 4, -4))
    ]
    for copy in stage2:
        copy.start()

    gather(1, pl.multiple_of(gr * width, width))
    total_ref[...] = lax.dot_general(
        s_ref[:, width:2 * width], s_ref[:, 2 * width:], TN, preferred_element_type=jnp.float32
    )

    def chunk(off):
        return pl.ds(pl.multiple_of(((z + off + chips) % chips) * rows, rows), rows)

    near = [
        (9, 1, 2), (7, -1, 6), (5, 1, 1), (3, -1, 5), (6, 2, 9), (-6, -2, 11),
        (13, 1, 3), (11, -1, 7), (1, 1, 0), (15, -1, 4), (2, 2, 8), (-2, -2, 10),
    ]
    order = [off % chips for off, _, _ in near] + [8, 4, 12, 0]
    pairs = {
        off: remote(total_ref.at[chunk(off), theirs], pair_ref.at[i], pair_s.at[i], pair_r.at[i], partner)
        for i, off in enumerate(order)
    }
    for off in order:
        pairs[off].start()

    value = c2_send[...]
    for i in (1, 2, 0):
        stage2[i].wait_recv()
        value = value + c2_recv[i]
    part = e00_ref.at[pl.ds(first_e, 8), mine]
    part[...] = dielectric(value, scale_e, first_e, c * wide)
    two = jnp.where(c == 0, 2, -2)
    spread_to = [(1, 0, c), (1, 1, c), (-1, 0, 2 + c), (-1, 1, 2 + c), (two, 0, 4 + c), (two, 1, 4 + c), (0, other, 6)]
    stage3 = [
        remote(part, part, c3_s.at[i], c3_r.at[slot], chip(d, core)) for i, (d, core, slot) in enumerate(spread_to)
    ]
    for copy in stage3:
        copy.start()

    value = t_part(0, c)[...]
    for slot in range(7):
        remote(t_part(0, other), t1_recv.at[slot], t1_s.at[0], t1_r.at[slot], partner).wait_recv()
        value = value + t1_recv[slot]
    t2_send[...] = value
    top2 = [
        remote(t2_send, t2_recv.at[i], t2_s.at[i], t2_r.at[i], chip(d)) for i, d in enumerate((8, 4, -4))
    ]
    for copy in top2:
        copy.start()

    def own_part(off):
        off = off % chips
        pairs[off].wait_recv()
        return total_ref[chunk(off), mine] + pair_ref[order.index(off)]

    near_copies = {}
    for off, delta, slot in near:
        send_ref[slot] = own_part(off)
        copy = remote(send_ref.at[slot], recv_ref.at[slot], near_s.at[slot], near_r.at[slot], chip(delta))
        copy.start()
        near_copies[slot] = copy

    for slot in range(7):
        remote(part, part, c3_s.at[0], c3_r.at[slot], partner).wait_recv()

    def e00_part(r, s, half):
        return e00_ref.at[pl.ds(pl.multiple_of(r * BLOCK + s * rows, rows), rows), half]

    def needed(r, core):
        return jnp.logical_or(core == 1, r < 2)

    def stage4(i):
        return remote(e00_part(gr, gc, mine), e00_part(gr, gc, mine), c4_s.at[i], c4_r.at[i], peers[i])

    def sender(i):
        return (gr + grid - i // grid) % grid, (gc + grid - i % grid) % grid

    @pl.when(needed(gr, c))
    def _():
        for i in peers:
            stage4(i).start()

    value = t2_send[...]
    for i in (1, 2, 0):
        top2[i].wait_recv()
        value = value + t2_recv[i]
    t_piece = top_ref.at[pl.ds(first_t, rows), mine]
    t_piece[...] = dielectric(value, t_scale_ref[...], first_t, first_col)
    top3 = [
        remote(t_piece, t_piece, t3_s.at[i], t3_r.at[slot], chip(d, core)) for i, (d, core, slot) in enumerate(spread_to)
    ]
    for copy in top3:
        copy.start()

    def quarter(r):
        return top_ref.at[pl.ds(pl.multiple_of(r * BLOCK, BLOCK), BLOCK), mine]

    def to_column(i):
        return remote(quarter(gr), quarter(gr), t4_s.at[i - 1], t4_r.at[i - 1], (kb, (gr + i) % grid, gc))

    def to_core(i):
        r = (gr + grid - i) % grid
        return remote(quarter(r), quarter(r), t5_s.at[i - 1], t5_r.at[i - 1], partner)

    def send_column():
        for slot in range(7):
            remote(t_piece, t_piece, t3_s.at[0], t3_r.at[slot], partner).wait_recv()
        for i in range(1, grid):
            to_column(i).start()

    def send_core():
        for i in range(1, grid):
            to_column(i).wait_recv()
            to_core(i).start()

    def stage5(i, half):
        r, s = sender(i)
        return remote(e00_part(r, s, half), e00_part(r, s, half), c5_s.at[i], c5_r.at[i], partner)


    def gathered(j, extra):
        value = own_part(4 * j)
        for slot in (j, 4 + j) + extra:
            near_copies[slot].wait_recv()
            value = value + recv_ref[slot]
        return value

    far_list = [(2, (), 8), (1, (9,), 4), (3, (11,), -4)]

    def far_copy(i):
        return remote(far_send_ref.at[i], far_recv_ref.at[i], far_s.at[i], far_r.at[i], chip(far_list[i][2]))

    def end_e00_copies():
        for copy in stage3:
            copy.wait_send()

        @pl.when(needed(gr, c))
        def _():
            for i in peers:
                stage4(i).wait_send()
        for i in peers:
            @pl.when(needed(sender(i)[0], c))
            def _():
                stage5(i, mine).wait_send()

    def send_far():
        for i, (j, extra, delta) in enumerate(far_list):
            far_send_ref[i] = gathered(j, extra)
            far_copy(i).start()

    swap = remote(f_ref.at[pl.ds(pl.multiple_of(other * band, band), band)], own_ref.at[:, mine], swap_s, swap_r, partner)

    def send_own():
        value = gathered(0, (8, 10))
        for i in (1, 2, 0):
            far_copy(i).wait_recv()
            value = value + far_recv_ref[i]
        value = dielectric(value, scale_ref[...], first_row, first_col)
        f_ref[...] = value

        swap.start()
        own_ref[:, mine] = f_ref[pl.ds(pl.multiple_of(c * band, band), band)]

    def to_side(i):
        return remote(own_ref, left_ref, side_s.at[i - 1], side_r, (kb, gr, (gc + i) % grid))

    def send_side():
        swap.wait_recv()

        @pl.when(is_left)
        def _():
            for i in range(1, grid):
                to_side(i).start()

    def wait_rows(r):
        for i in peers:
            @pl.when((sender(i)[0] == r) & needed(r, c))
            def _():
                stage4(i).wait_recv()
                stage5(i, mine).start()

    def wait_halves(r):
        for i in peers:
            @pl.when((sender(i)[0] == r) & needed(r, other))
            def _():
                stage5(i, theirs).wait_recv()

    def wait_later_rows():
        for r in range(1, grid):
            wait_rows(r)

    def wait_later_halves():
        for r in range(1, grid):
            wait_halves(r)

    wait_rows(0)
    wait_halves(0)
    plan = {
        (0, 4): wait_later_rows, (0, 8): send_column, (0, 11): wait_later_halves, (0, 13): send_far, (0, 15): end_e00_copies,
        (2, 8): send_own, (3, 0): send_core, (3, 6): send_side,
    }
    cuts = [slice(b * BLOCK, (b + 1) * BLOCK) for b in range(width // BLOCK)]
    for b, cut in enumerate(cuts):
        def hook(g):
            if (b, g) in plan:
                plan[b, g]()

        inverse = inverse_factor(e00_ref[cut, cut], hook)
        if b:
            g_ref[cut, :b * BLOCK] = product(inverse, g_ref[cut, :b * BLOCK])
        g_ref[cut, cut] = inverse
        after = (b + 1) * BLOCK
        if after < width:
            across = product(inverse, e00_ref[cut, after:])
            for cut2 in cuts[b + 1:]:
                at = cut2.start
                e00_ref[cut2, at:] = e00_ref[cut2, at:] - product(
                    across[:, at - after:at - after + BLOCK], across[:, at - after:], TN
                )
            change = product(across, g_ref[cut, :after], TN)
            if b:
                g_ref[after:, :cut.start] = g_ref[after:, :cut.start] - change[:, :cut.start]
            g_ref[after:, cut] = -change[:, cut.start:]

    @pl.when(jnp.logical_not(is_left))
    def _():
        to_side(1).wait_recv()

    @pl.when(is_left)
    def _():
        left_ref[...] = own_ref[...]

    for cut in cuts:
        low_ref[:, cut] = product(left_ref[:, :cut.stop], g_ref[cut, :cut.stop], NT)
    for cut in cuts:
        w_ref[:, cut] = product(low_ref[:, cut.start:], g_ref[cut.start:, cut])

    for i in range(1, grid):
        to_core(i).wait_recv()

    row = kb * band + lax.broadcasted_iota(jnp.int32, (band, width), 0)
    col = lax.broadcasted_iota(jnp.int32, (band, width), 1)
    factor_side = jnp.where(is_top & (col > row), 0.0, low_ref[...])
    trail = own_ref[...] - product(w_ref[...], top_ref[...])
    out_ref[...] = jnp.where(is_left, factor_side, jnp.where(is_top, own_ref[...], trail))

    for copy in stage1 + stage2 + top1 + top2 + top3 + list(pairs.values()) + list(near_copies.values()) + [swap]:
        copy.wait_send()
    for i in range(3):
        far_copy(i).wait_send()
    for i in range(1, grid):
        to_column(i).wait_send()
        to_core(i).wait_send()

    @pl.when(is_left)
    def _():
        for i in range(1, grid):
            to_side(i).wait_send()


def body(wedge_pairs, e_cond, e_val, coulomb, owned_wedge, owned_op, gmap):
    members = lax.axis_size("kb")
    grid = lax.axis_size("gr")
    chips = members // 2
    total_g = gmap.shape[1]
    width = total_g // grid
    band = width // members
    owners, slots = owned_wedge.shape
    hbm = pl.BlockSpec(memory_space=pltpu.HBM)
    x = wedge_pairs.reshape(-1, total_g)
    bands = x.shape[0]
    vmem = pl.BlockSpec(memory_space=pltpu.VMEM)
    dma = pltpu.SemaphoreType.DMA
    piece = (2 * band, width // 2)
    f32 = jnp.float32
    return pl.pallas_call(
        functools.partial(whole_kernel, chips, grid),
        out_shape=jax.ShapeDtypeStruct((band, width), f32),
        in_specs=[hbm] * 3 + [vmem] * 2 + [hbm] * 2,
        out_specs=vmem,
        scratch_shapes=[
            pltpu.VMEM((slots, owners), jnp.int32),
            pltpu.VMEM((slots, owners), jnp.int32),
            pltpu.VMEM(x.shape, x.dtype),
            pltpu.VMEM((1, total_g), f32),
            pltpu.VMEM(gmap.shape, gmap.dtype),
            pltpu.VMEM(piece, f32),
            pltpu.VMEM((width, width), f32),
            pltpu.VMEM((owners, width), f32),
            pltpu.VMEM((owners, width), f32),
            pltpu.VMEM((BLOCK, width), f32),
            pltpu.VMEM((7,) + piece, f32),
            pltpu.VMEM(piece, f32),
            pltpu.VMEM((3,) + piece, f32),
            pltpu.VMEM(piece, f32),
            pltpu.VMEM((owners * bands, 3 * width), jnp.bfloat16),
            pltpu.VMEM((bands * (total_g // LOW), LOW), jnp.bfloat16),
            pltpu.VMEM((BLOCK, width), f32),
            pltpu.VMEM((7, 8, width // 2), f32),
            pltpu.VMEM((8, width // 2), f32),
            pltpu.VMEM((3, 8, width // 2), f32),
            pltpu.VMEM((width, width), f32),
            pltpu.VMEM((width, width), f32),
            pltpu.VMEM((chips,) + piece, f32),
            pltpu.VMEM((12,) + piece, f32),
            pltpu.VMEM((12,) + piece, f32),
            pltpu.VMEM((3,) + piece, f32),
            pltpu.VMEM((3,) + piece, f32),
            pltpu.VMEM(piece, f32),
            pltpu.VMEM((band, width), f32),
            pltpu.VMEM((band, width), f32),
            pltpu.VMEM((width, width), f32),
            pltpu.VMEM((band, width), f32),
            pltpu.VMEM((band, width), f32),
            dma((7,)), dma((7,)),
            dma((3,)), dma((3,)),
            dma((7,)), dma((7,)),
            dma((grid * grid,)), dma((grid * grid,)),
            dma((grid * grid,)), dma((grid * grid,)),
            dma((chips,)), dma((chips,)),
            dma((12,)), dma((12,)),
            dma((3,)), dma((3,)),
            dma, dma,
            dma((grid - 1,)), dma,
            dma((7,)), dma((7,)),
            dma((3,)), dma((3,)),
            dma((7,)), dma((7,)),
            dma((grid - 1,)), dma((grid - 1,)),
            dma((grid - 1,)), dma((grid - 1,)),
            dma((5,)),
        ],
        compiler_params=pltpu.CompilerParams(
            collective_id=0, has_side_effects=True, vmem_limit_bytes=63 << 20
        ),
        name="whole",
    )(owned_wedge.T, owned_op.T, x, e_cond, e_val, coulomb.reshape(1, -1), gmap)


def solution(mesh):
    placed = (P("kb", None, None, None), P("kb", None), P("kb", None), P(), P(), P(), P())
    return jax.shard_map(
        body, mesh=mesh, in_specs=placed, out_specs=P(("gr", "kb"), "gc"), check_vma=False
    )
```

```python
import functools
import jax
import jax.numpy as jnp
from jax import lax
from jax.experimental import pallas as pl
from jax.experimental.pallas import tpu as pltpu
from jax.sharding import PartitionSpec as P

MESH = pl.DeviceIdType.MESH
HI = lax.Precision.HIGHEST
NT = (((1,), (1,)), ((), ()))
TN = (((0,), (0,)), ((), ()))
LOW = 256
BLOCK = 128


def product(a, b, dims=(((1,), (0,)), ((), ()))):
    return lax.dot_general(a, b, dims, precision=HI, preferred_element_type=jnp.float32)


def thirds(a):
    first = a.astype(jnp.bfloat16).astype(jnp.float32)
    second = (a - first).astype(jnp.bfloat16).astype(jnp.float32)
    return first, second, a - first - second


def gram(rows):
    p, q, r = thirds(rows)
    one = jnp.concatenate([p, p, q, p, r, q], axis=0).astype(jnp.bfloat16)
    two = jnp.concatenate([p, q, p, r, p, q], axis=0).astype(jnp.bfloat16)
    return lax.dot_general(one, two, TN, preferred_element_type=jnp.float32)


def inverse_factor(d, hook):
    n = d.shape[0]
    groups = n // 8
    lane = lax.broadcasted_iota(jnp.int32, (8, n), 1)
    sub = lax.broadcasted_iota(jnp.int32, (8, n), 0)
    rows = [d[8 * i:8 * i + 8, :] for i in range(groups)]
    out = []
    for g in range(groups):
        base = 8 * g
        hook(g)
        follows = g + 1 < groups
        head, after = rows[g], rows[g + 1] if follows else None
        cols = [jnp.broadcast_to(head[:, base + k:base + k + 1], (8, n)) for k in range(8)]
        below = [jnp.broadcast_to(after[:, base + k:base + k + 1], (8, n)) for k in range(8)] if follows else None
        inside = (lane >= base) & (lane < base + 8)
        head = jnp.where(inside, jnp.where(lane - base == sub, 1.0, 0.0), head)
        if follows:
            after = jnp.where(inside, 0.0, after)
        entry = {(i, k): jnp.broadcast_to(cols[k][i:i + 1, :], (8, n)) for i in range(8) for k in range(i + 1)}
        row = [jnp.broadcast_to(head[i:i + 1, :], (8, n)) for i in range(8)]
        done = jnp.zeros((8, n), jnp.float32)
        for j in range(0, 8, 2):
            a, b, d2 = entry[j, j], entry[j + 1, j], entry[j + 1, j + 1]
            scale = lax.rsqrt(a)
            cross = b * scale
            scale2 = lax.rsqrt(a * d2 - b * b) * (a * scale)
            pivot_row = row[j] * scale
            pivot_row2 = (row[j + 1] - cross * pivot_row) * scale2
            done = jnp.where(sub == j, pivot_row, jnp.where(sub == j + 1, pivot_row2, done))
            mult = {i: entry[i, j] * scale for i in range(j + 2, 8)}
            mult2 = {i: (entry[i, j + 1] - cross * mult[i]) * scale2 for i in range(j + 2, 8)}
            for i in range(j + 2, 8):
                row[i] = (row[i] - mult[i] * pivot_row) - mult2[i] * pivot_row2
                for k in range(j + 2, i + 1):
                    entry[i, k] = (entry[i, k] - mult[i] * mult[k]) - mult2[i] * mult2[k]
            if follows:
                step = below[j] * scale
                step2 = (below[j + 1] - step * cross) * scale2
                after = (after - step * pivot_row) - step2 * pivot_row2
                for k in range(j + 2, 8):
                    below[k] = (below[k] - step * mult[k]) - step2 * mult2[k]
        out.append(jnp.where(lane <= sub + base, done, 0.0))
        if follows:
            rows[g + 1] = after
        if g + 2 < groups:
            change = gram(done)
            for i in range(g + 2, groups):
                rows[i] = jnp.where(inside, 0.0, rows[i]) - change[8 * i:8 * i + 8, :]
    return jnp.concatenate(out, axis=0)


def whole_kernel(chips, grid, wedge_hbm, op_hbm, x_hbm, ec_ref, ev_ref, coulomb_hbm, gmap_hbm, out_ref,
                 wedge_ref, op_ref, x_ref, coulomb_ref, gmap_ref, scale_ref, g_ref,
                 lo_ref, hi_ref, pt_ref, t1_recv, t2_send, t2_recv, t_scale_ref, s_ref, y_ref, p_ref, c1_recv, c2_send, c2_recv, e00_ref, total_ref,
                 pair_ref, send_ref, recv_ref, far_send_ref, far_recv_ref, f_ref, own_ref, left_ref, top_ref,
                 low_ref, w_ref,
                 c1_s, c1_r, c2_s, c2_r, c3_s, c3_r, c4_s, c4_r, c5_s, c5_r,
                 pair_s, pair_r, near_s, near_r, far_s, far_r, swap_s, swap_r,
                 side_s, side_r, t1_s, t1_r, t2_s, t2_r, t3_s, t3_r, t4_s, t4_r, t5_s, t5_r, in_s):
    kb, gr, gc = lax.axis_index("kb"), lax.axis_index("gr"), lax.axis_index("gc")
    z, c = kb // 2, kb % 2
    other = 1 - c
    slots, owners = wedge_ref.shape
    bands, total_g = x_ref.shape
    band, width = out_ref.shape
    rows, wide = 2 * band, width // 2
    is_top, is_left = gr == 0, gc == 0

    fetched = [
        pltpu.make_async_copy(src, dst, in_s.at[i])
        for i, (src, dst) in enumerate([
            (gmap_hbm, gmap_ref), (x_hbm, x_ref), (wedge_hbm, wedge_ref), (op_hbm, op_ref), (coulomb_hbm, coulomb_ref)
        ])
    ]
    for copy in fetched:
        copy.start()

    def chip(delta, core=None):
        return (2 * ((z + delta + chips) % chips) + (c if core is None else core), gr, gc)

    def remote(src, dst, send, recv, who):
        return pltpu.make_async_remote_copy(
            src_ref=src, dst_ref=dst, send_sem=send, recv_sem=recv, device_id=who, device_id_type=MESH
        )

    partner = (2 * z + other, gr, gc)
    peers = {
        i: (kb, (gr + i // grid) % grid, (gc + i % grid) % grid) for i in range(1, grid * grid)
    }
    barrier = pltpu.get_barrier_semaphore()
    everyone = (
        [chip(d, core) for d in (1, -1, 2, -2) for core in (0, 1)]
        + [chip(d) for d in (4, -4, 8)] + [partner] + list(peers.values())
    )
    for who in everyone:
        pl.semaphore_signal(barrier, inc=1, device_id=who, device_id_type=MESH)

    for copy in fetched:
        copy.wait()

    eye = lax.broadcasted_iota(jnp.int32, (bands, bands), 0) == lax.broadcasted_iota(jnp.int32, (bands, bands), 1)
    gap = ec_ref[...] - ev_ref[...]
    weight = jnp.sqrt(4.0 / (float(owners * slots) * gap))
    weight = jnp.sum(jnp.where(eye, jnp.broadcast_to(weight, (bands, bands)), 0.0), axis=1, keepdims=True)
    y = (x_ref[...].astype(jnp.float32) * weight).astype(jnp.bfloat16)
    parts = total_g // LOW
    for h in range(parts):
        y_ref[h * bands:(h + 1) * bands, :] = y[:, h * LOW:(h + 1) * LOW]
    matched = jnp.where(wedge_ref[...] == kb, 1.0, 0.0)
    present = jnp.sum(matched, axis=0, keepdims=True)
    operation = jnp.sum(matched * op_ref[...].astype(jnp.float32), axis=0, keepdims=True)
    kinds = lax.broadcasted_iota(jnp.int32, (gmap_ref.shape[0], owners), 0).astype(jnp.float32)
    chosen = jnp.where(kinds == operation, present, 0.0).astype(jnp.bfloat16)
    count = lax.broadcasted_iota(jnp.int32, (LOW, 128), 0).astype(jnp.float32).astype(jnp.bfloat16)
    one, none = jnp.ones((LOW, 128), jnp.bfloat16), jnp.zeros((LOW, 128), jnp.bfloat16)

    def gather(side, at):
        maps = gmap_ref[:, pl.ds(at, width)]
        low_bits = (maps & (LOW - 1)).astype(jnp.float32).astype(jnp.bfloat16)
        high_bits = ((maps >> (LOW.bit_length() - 1)) + 1).astype(jnp.float32).astype(jnp.bfloat16)
        lo_ref[...] = lax.dot_general(chosen, low_bits, TN, preferred_element_type=jnp.float32)
        hi_ref[...] = lax.dot_general(chosen, high_bits, TN, preferred_element_type=jnp.float32)

        def pick(o, carry):
            low = jnp.broadcast_to(lo_ref[pl.ds(o, 1), :], (LOW, width)).astype(jnp.bfloat16)
            high = hi_ref[pl.ds(o, 1), :]
            onehot = jnp.concatenate(
                [jnp.where(count == low[:, t:t + 128], one, none) for t in range(0, width, 128)], axis=1
            )
            spread = jnp.dot(y_ref[...], onehot, preferred_element_type=jnp.float32)
            picked = jnp.zeros((bands, width), jnp.float32)
            for h in range(parts):
                picked = jnp.where(high == float(h + 1), spread[h * bands:(h + 1) * bands, :], picked)
            s_ref[pl.ds(pl.multiple_of(o * bands, bands), bands), side * width:(side + 1) * width] = picked.astype(jnp.bfloat16)
            return carry

        lax.fori_loop(0, owners, pick, 0, unroll=4)

    root = jnp.sqrt(coulomb_ref[...])

    def root_down(first, count, reach):
        ids = first + lax.broadcasted_iota(jnp.int32, (count, reach), 0)
        lanes = lax.broadcasted_iota(jnp.int32, (count, reach), 1)
        return jnp.sum(jnp.where(ids == lanes, jnp.broadcast_to(root[:, :reach], (count, reach)), 0.0), axis=1, keepdims=True)

    def scale_of(first_row, first_col, count, across):
        return root_down(first_row, count, total_g) * jnp.sqrt(
            coulomb_ref[:, pl.ds(pl.multiple_of(first_col, 128), across)]
        )

    def dielectric(value, scale, first_row, first_col):
        row = first_row + lax.broadcasted_iota(jnp.int32, value.shape, 0)
        col = first_col + lax.broadcasted_iota(jnp.int32, value.shape, 1)
        return jnp.where(row == col, 1.0, 0.0) + scale * value

    gather(0, 0)
    p_ref[...] = lax.dot_general(
        s_ref[:, pl.ds(pl.multiple_of(gr * BLOCK, BLOCK), BLOCK)], s_ref[:, :width], TN, preferred_element_type=jnp.float32
    )
    pl.semaphore_wait(barrier, len(everyone))

    def p_part(delta, core):
        k = (z + delta + chips) % grid
        return p_ref.at[pl.ds(pl.multiple_of(gc * rows + 8 * k, 8), 8), pl.ds(pl.multiple_of(core * wide, wide), wide)]

    near_parts = [(1, 0, c), (1, 1, c), (-1, 0, 2 + c), (-1, 1, 2 + c), (2, 0, 4 + c), (-2, 1, 4 + c), (0, other, 6)]
    stage1 = [
        remote(p_part(d, core), c1_recv.at[slot], c1_s.at[i], c1_r.at[slot], chip(d, core))
        for i, (d, core, slot) in enumerate(near_parts)
    ]
    for copy in stage1:
        copy.start()

    mine = pl.ds(pl.multiple_of(c * wide, wide), wide)
    theirs = pl.ds(pl.multiple_of(other * wide, wide), wide)

    gather(2, pl.multiple_of(gc * width, width))
    pt_ref[...] = lax.dot_general(
        s_ref[:, pl.ds(pl.multiple_of(gr * BLOCK, BLOCK), BLOCK)], s_ref[:, 2 * width:], TN, preferred_element_type=jnp.float32
    )

    def t_part(delta, core):
        k = (z + delta + chips) % grid
        return pt_ref.at[pl.ds(pl.multiple_of(rows * k, rows), rows), pl.ds(pl.multiple_of(core * wide, wide), wide)]

    top1 = [
        remote(t_part(d, core), t1_recv.at[slot], t1_s.at[i], t1_r.at[slot], chip(d, core))
        for i, (d, core, slot) in enumerate(near_parts)
    ]
    for copy in top1:
        copy.start()

    first_e = pl.multiple_of(gr * BLOCK + gc * rows + 8 * (z % grid), 8)
    scale_e = scale_of(first_e, c * wide, 8, wide)
    first_row, first_col = gr * width + z * rows, gc * width + c * wide
    first_t = pl.multiple_of(gr * BLOCK + rows * (z % grid), rows)
    scale_ref[...] = scale_of(first_row, first_col, rows, wide)
    t_scale_ref[...] = scale_of(first_t, first_col, rows, wide)

    value = p_part(0, c)[...]
    for slot in range(7):
        remote(p_part(0, other), c1_recv.at[slot], c1_s.at[0], c1_r.at[slot], partner).wait_recv()
        value = value + c1_recv[slot]
    c2_send[...] = value
    stage2 = [
        remote(c2_send, c2_recv.at[i], c2_s.at[i], c2_r.at[i], chip(d)) for i, d in enumerate((8, 4, -4))
    ]
    for copy in stage2:
        copy.start()

    gather(1, pl.multiple_of(gr * width, width))
    total_ref[...] = lax.dot_general(
        s_ref[:, width:2 * width], s_ref[:, 2 * width:], TN, preferred_element_type=jnp.float32
    )

    def chunk(off):
        return pl.ds(pl.multiple_of(((z + off + chips) % chips) * rows, rows), rows)

    near = [
        (9, 1, 2), (7, -1, 6), (5, 1, 1), (3, -1, 5), (6, 2, 9), (-6, -2, 11),
        (13, 1, 3), (11, -1, 7), (1, 1, 0), (15, -1, 4), (2, 2, 8), (-2, -2, 10),
    ]
    order = [off % chips for off, _, _ in near] + [8, 4, 12, 0]
    pairs = {
        off: remote(total_ref.at[chunk(off), theirs], pair_ref.at[i], pair_s.at[i], pair_r.at[i], partner)
        for i, off in enumerate(order)
    }
    for off in order:
        pairs[off].start()

    value = c2_send[...]
    for i in (1, 2, 0):
        stage2[i].wait_recv()
        value = value + c2_recv[i]
    part = e00_ref.at[pl.ds(first_e, 8), mine]
    part[...] = dielectric(value, scale_e, first_e, c * wide)
    two = jnp.where(c == 0, 2, -2)
    spread_to = [(1, 0, c), (1, 1, c), (-1, 0, 2 + c), (-1, 1, 2 + c), (two, 0, 4 + c), (two, 1, 4 + c), (0, other, 6)]
    stage3 = [
        remote(part, part, c3_s.at[i], c3_r.at[slot], chip(d, core)) for i, (d, core, slot) in enumerate(spread_to)
    ]
    for copy in stage3:
        copy.start()

    value = t_part(0, c)[...]
    for slot in range(7):
        remote(t_part(0, other), t1_recv.at[slot], t1_s.at[0], t1_r.at[slot], partner).wait_recv()
        value = value + t1_recv[slot]
    t2_send[...] = value
    top2 = [
        remote(t2_send, t2_recv.at[i], t2_s.at[i], t2_r.at[i], chip(d)) for i, d in enumerate((8, 4, -4))
    ]
    for copy in top2:
        copy.start()

    def own_part(off):
        off = off % chips
        pairs[off].wait_recv()
        return total_ref[chunk(off), mine] + pair_ref[order.index(off)]

    for slot in range(7):
        remote(part, part, c3_s.at[0], c3_r.at[slot], partner).wait_recv()

    def e00_part(r, s, half):
        return e00_ref.at[pl.ds(pl.multiple_of(r * BLOCK + s * rows, rows), rows), half]

    def needed(r, core):
        return jnp.logical_or(core == 1, r < 2)

    def stage4(i):
        return remote(e00_part(gr, gc, mine), e00_part(gr, gc, mine), c4_s.at[i], c4_r.at[i], peers[i])

    def sender(i):
        return (gr + grid - i // grid) % grid, (gc + grid - i % grid) % grid

    @pl.when(needed(gr, c))
    def _():
        for i in peers:
            stage4(i).start()

    near_copies = {}
    for off, delta, slot in near:
        send_ref[slot] = own_part(off)
        copy = remote(send_ref.at[slot], recv_ref.at[slot], near_s.at[slot], near_r.at[slot], chip(delta))
        copy.start()
        near_copies[slot] = copy

    t_piece = top_ref.at[pl.ds(first_t, rows), mine]
    top3 = [
        remote(t_piece, t_piece, t3_s.at[i], t3_r.at[slot], chip(d, core)) for i, (d, core, slot) in enumerate(spread_to)
    ]

    def send_pieces():
        value = t2_send[...]
        for i in (1, 2, 0):
            top2[i].wait_recv()
            value = value + t2_recv[i]
        t_piece[...] = dielectric(value, t_scale_ref[...], first_t, first_col)
        for copy in top3:
            copy.start()

    def quarter(r):
        return top_ref.at[pl.ds(pl.multiple_of(r * BLOCK, BLOCK), BLOCK), mine]

    def to_column(i):
        return remote(quarter(gr), quarter(gr), t4_s.at[i - 1], t4_r.at[i - 1], (kb, (gr + i) % grid, gc))

    def to_core(i):
        r = (gr + grid - i) % grid
        return remote(quarter(r), quarter(r), t5_s.at[i - 1], t5_r.at[i - 1], partner)

    def send_column():
        for slot in range(7):
            remote(t_piece, t_piece, t3_s.at[0], t3_r.at[slot], partner).wait_recv()
        for i in range(1, grid):
            to_column(i).start()

    def send_core():
        for i in range(1, grid):
            to_column(i).wait_recv()
            to_core(i).start()

    def stage5(i, half):
        r, s = sender(i)
        return remote(e00_part(r, s, half), e00_part(r, s, half), c5_s.at[i], c5_r.at[i], partner)


    def gathered(j, extra):
        value = own_part(4 * j)
        for slot in (j, 4 + j) + extra:
            near_copies[slot].wait_recv()
            value = value + recv_ref[slot]
        return value

    far_list = [(2, (), 8), (1, (9,), 4), (3, (11,), -4)]

    def far_copy(i):
        return remote(far_send_ref.at[i], far_recv_ref.at[i], far_s.at[i], far_r.at[i], chip(far_list[i][2]))

    def end_e00_copies():
        for copy in stage3:
            copy.wait_send()

        @pl.when(needed(gr, c))
        def _():
            for i in peers:
                stage4(i).wait_send()
        for i in peers:
            @pl.when(needed(sender(i)[0], c))
            def _():
                stage5(i, mine).wait_send()

    def send_far():
        for i, (j, extra, delta) in enumerate(far_list):
            far_send_ref[i] = gathered(j, extra)
            far_copy(i).start()

    swap = remote(f_ref.at[pl.ds(pl.multiple_of(other * band, band), band)], own_ref.at[:, mine], swap_s, swap_r, partner)

    def send_own():
        value = gathered(0, (8, 10))
        for i in (1, 2, 0):
            far_copy(i).wait_recv()
            value = value + far_recv_ref[i]
        value = dielectric(value, scale_ref[...], first_row, first_col)
        f_ref[...] = value

        swap.start()
        own_ref[:, mine] = f_ref[pl.ds(pl.multiple_of(c * band, band), band)]

    def to_side(i):
        return remote(own_ref, left_ref, side_s.at[i - 1], side_r, (kb, gr, (gc + i) % grid))

    def send_side():
        swap.wait_recv()

        @pl.when(is_left)
        def _():
            for i in range(1, grid):
                to_side(i).start()

    def wait_rows(r):
        for i in peers:
            @pl.when((sender(i)[0] == r) & needed(r, c))
            def _():
                stage4(i).wait_recv()
                stage5(i, mine).start()

    def wait_halves(r):
        for i in peers:
            @pl.when((sender(i)[0] == r) & needed(r, other))
            def _():
                stage5(i, theirs).wait_recv()

    def wait_later_rows():
        for r in range(1, grid):
            wait_rows(r)

    def wait_later_halves():
        for r in range(1, grid):
            wait_halves(r)

    wait_rows(0)
    wait_halves(0)
    plan = {
        (0, 2): send_pieces, (0, 6): wait_later_rows, (0, 11): wait_later_halves, (0, 15): end_e00_copies,
        (1, 0): send_far, (1, 2): send_column, (2, 15): send_own, (3, 1): send_core, (3, 7): send_side,
    }
    cuts = [slice(b * BLOCK, (b + 1) * BLOCK) for b in range(width // BLOCK)]
    for b, cut in enumerate(cuts):
        def hook(g):
            if (b, g) in plan:
                plan[b, g]()

        inverse = inverse_factor(e00_ref[cut, cut], hook)
        if b:
            g_ref[cut, :b * BLOCK] = product(inverse, g_ref[cut, :b * BLOCK])
        g_ref[cut, cut] = inverse
        after = (b + 1) * BLOCK
        if after < width:
            across = product(inverse, e00_ref[cut, after:])
            for cut2 in cuts[b + 1:]:
                at = cut2.start
                e00_ref[cut2, at:] = e00_ref[cut2, at:] - product(
                    across[:, at - after:at - after + BLOCK], across[:, at - after:], TN
                )
            change = product(across, g_ref[cut, :after], TN)
            if b:
                g_ref[after:, :cut.start] = g_ref[after:, :cut.start] - change[:, :cut.start]
            g_ref[after:, cut] = -change[:, cut.start:]

    @pl.when(jnp.logical_not(is_left))
    def _():
        to_side(1).wait_recv()

    @pl.when(is_left)
    def _():
        left_ref[...] = own_ref[...]

    for cut in cuts:
        low_ref[:, cut] = product(left_ref[:, :cut.stop], g_ref[cut, :cut.stop], NT)
    for cut in cuts:
        w_ref[:, cut] = product(low_ref[:, cut.start:], g_ref[cut.start:, cut])

    for i in range(1, grid):
        to_core(i).wait_recv()

    row = kb * band + lax.broadcasted_iota(jnp.int32, (band, width), 0)
    col = lax.broadcasted_iota(jnp.int32, (band, width), 1)
    factor_side = jnp.where(is_top & (col > row), 0.0, low_ref[...])
    trail = own_ref[...] - product(w_ref[...], top_ref[...])
    out_ref[...] = jnp.where(is_left, factor_side, jnp.where(is_top, own_ref[...], trail))

    for copy in stage1 + stage2 + top1 + top2 + top3 + list(pairs.values()) + list(near_copies.values()) + [swap]:
        copy.wait_send()
    for i in range(3):
        far_copy(i).wait_send()
    for i in range(1, grid):
        to_column(i).wait_send()
        to_core(i).wait_send()

    @pl.when(is_left)
    def _():
        for i in range(1, grid):
            to_side(i).wait_send()


def body(wedge_pairs, e_cond, e_val, coulomb, owned_wedge, owned_op, gmap):
    members = lax.axis_size("kb")
    grid = lax.axis_size("gr")
    chips = members // 2
    total_g = gmap.shape[1]
    width = total_g // grid
    band = width // members
    owners, slots = owned_wedge.shape
    hbm = pl.BlockSpec(memory_space=pltpu.HBM)
    x = wedge_pairs.reshape(-1, total_g)
    bands = x.shape[0]
    vmem = pl.BlockSpec(memory_space=pltpu.VMEM)
    dma = pltpu.SemaphoreType.DMA
    piece = (2 * band, width // 2)
    f32 = jnp.float32
    return pl.pallas_call(
        functools.partial(whole_kernel, chips, grid),
        out_shape=jax.ShapeDtypeStruct((band, width), f32),
        in_specs=[hbm] * 3 + [vmem] * 2 + [hbm] * 2,
        out_specs=vmem,
        scratch_shapes=[
            pltpu.VMEM((slots, owners), jnp.int32),
            pltpu.VMEM((slots, owners), jnp.int32),
            pltpu.VMEM(x.shape, x.dtype),
            pltpu.VMEM((1, total_g), f32),
            pltpu.VMEM(gmap.shape, gmap.dtype),
            pltpu.VMEM(piece, f32),
            pltpu.VMEM((width, width), f32),
            pltpu.VMEM((owners, width), f32),
            pltpu.VMEM((owners, width), f32),
            pltpu.VMEM((BLOCK, width), f32),
            pltpu.VMEM((7,) + piece, f32),
            pltpu.VMEM(piece, f32),
            pltpu.VMEM((3,) + piece, f32),
            pltpu.VMEM(piece, f32),
            pltpu.VMEM((owners * bands, 3 * width), jnp.bfloat16),
            pltpu.VMEM((bands * (total_g // LOW), LOW), jnp.bfloat16),
            pltpu.VMEM((BLOCK, width), f32),
            pltpu.VMEM((7, 8, width // 2), f32),
            pltpu.VMEM((8, width // 2), f32),
            pltpu.VMEM((3, 8, width // 2), f32),
            pltpu.VMEM((width, width), f32),
            pltpu.VMEM((width, width), f32),
            pltpu.VMEM((chips,) + piece, f32),
            pltpu.VMEM((12,) + piece, f32),
            pltpu.VMEM((12,) + piece, f32),
            pltpu.VMEM((3,) + piece, f32),
            pltpu.VMEM((3,) + piece, f32),
            pltpu.VMEM(piece, f32),
            pltpu.VMEM((band, width), f32),
            pltpu.VMEM((band, width), f32),
            pltpu.VMEM((width, width), f32),
            pltpu.VMEM((band, width), f32),
            pltpu.VMEM((band, width), f32),
            dma((7,)), dma((7,)),
            dma((3,)), dma((3,)),
            dma((7,)), dma((7,)),
            dma((grid * grid,)), dma((grid * grid,)),
            dma((grid * grid,)), dma((grid * grid,)),
            dma((chips,)), dma((chips,)),
            dma((12,)), dma((12,)),
            dma((3,)), dma((3,)),
            dma, dma,
            dma((grid - 1,)), dma,
            dma((7,)), dma((7,)),
            dma((3,)), dma((3,)),
            dma((7,)), dma((7,)),
            dma((grid - 1,)), dma((grid - 1,)),
            dma((grid - 1,)), dma((grid - 1,)),
            dma((5,)),
        ],
        compiler_params=pltpu.CompilerParams(
            collective_id=0, has_side_effects=True, vmem_limit_bytes=63 << 20
        ),
        name="whole",
    )(owned_wedge.T, owned_op.T, x, e_cond, e_val, coulomb.reshape(1, -1), gmap)


def solution(mesh):
    placed = (P("kb", None, None, None), P("kb", None), P("kb", None), P(), P(), P(), P())
    return jax.shard_map(
        body, mesh=mesh, in_specs=placed, out_specs=P(("gr", "kb"), "gc"), check_vma=False
    )
```

```python
import functools
import jax
import jax.numpy as jnp
from jax import lax
from jax.experimental import pallas as pl
from jax.experimental.pallas import tpu as pltpu
from jax.sharding import PartitionSpec as P

MESH = pl.DeviceIdType.MESH
HI = lax.Precision.HIGHEST
NT = (((1,), (1,)), ((), ()))
TN = (((0,), (0,)), ((), ()))
LOW = 256
BLOCK = 128


def product(a, b, dims=(((1,), (0,)), ((), ()))):
    return lax.dot_general(a, b, dims, precision=HI, preferred_element_type=jnp.float32)


def thirds(a):
    first = a.astype(jnp.bfloat16).astype(jnp.float32)
    second = (a - first).astype(jnp.bfloat16).astype(jnp.float32)
    return first, second, a - first - second


def gram(rows):
    p, q, r = thirds(rows)
    one = jnp.concatenate([p, p, q, p, r, q], axis=0).astype(jnp.bfloat16)
    two = jnp.concatenate([p, q, p, r, p, q], axis=0).astype(jnp.bfloat16)
    return lax.dot_general(one, two, TN, preferred_element_type=jnp.float32)


def inverse_factor(d, hook):
    n = d.shape[0]
    groups = n // 8
    lane = lax.broadcasted_iota(jnp.int32, (8, n), 1)
    sub = lax.broadcasted_iota(jnp.int32, (8, n), 0)
    rows = [d[8 * i:8 * i + 8, :] for i in range(groups)]
    out = []
    for g in range(groups):
        base = 8 * g
        hook(g)
        follows = g + 1 < groups
        head, after = rows[g], rows[g + 1] if follows else None
        cols = [jnp.broadcast_to(head[:, base + k:base + k + 1], (8, n)) for k in range(8)]
        below = [jnp.broadcast_to(after[:, base + k:base + k + 1], (8, n)) for k in range(8)] if follows else None
        inside = (lane >= base) & (lane < base + 8)
        head = jnp.where(inside, jnp.where(lane - base == sub, 1.0, 0.0), head)
        if follows:
            after = jnp.where(inside, 0.0, after)
        entry = {(i, k): jnp.broadcast_to(cols[k][i:i + 1, :], (8, n)) for i in range(8) for k in range(i + 1)}
        row = [jnp.broadcast_to(head[i:i + 1, :], (8, n)) for i in range(8)]
        done = jnp.zeros((8, n), jnp.float32)
        for j in range(0, 8, 2):
            a, b, d2 = entry[j, j], entry[j + 1, j], entry[j + 1, j + 1]
            scale = lax.rsqrt(a)
            cross = b * scale
            scale2 = lax.rsqrt(a * d2 - b * b) * (a * scale)
            pivot_row = row[j] * scale
            pivot_row2 = (row[j + 1] - cross * pivot_row) * scale2
            done = jnp.where(sub == j, pivot_row, jnp.where(sub == j + 1, pivot_row2, done))
            mult = {i: entry[i, j] * scale for i in range(j + 2, 8)}
            mult2 = {i: (entry[i, j + 1] - cross * mult[i]) * scale2 for i in range(j + 2, 8)}
            for i in range(j + 2, 8):
                row[i] = (row[i] - mult[i] * pivot_row) - mult2[i] * pivot_row2
                for k in range(j + 2, i + 1):
                    entry[i, k] = (entry[i, k] - mult[i] * mult[k]) - mult2[i] * mult2[k]
            if follows:
                step = below[j] * scale
                step2 = (below[j + 1] - step * cross) * scale2
                after = (after - step * pivot_row) - step2 * pivot_row2
                for k in range(j + 2, 8):
                    below[k] = (below[k] - step * mult[k]) - step2 * mult2[k]
        out.append(jnp.where(lane <= sub + base, done, 0.0))
        if follows:
            rows[g + 1] = after
        if g + 2 < groups:
            change = gram(done)
            for i in range(g + 2, groups):
                rows[i] = jnp.where(inside, 0.0, rows[i]) - change[8 * i:8 * i + 8, :]
    return jnp.concatenate(out, axis=0)


def whole_kernel(chips, grid, wedge_hbm, op_hbm, x_hbm, ec_ref, ev_ref, coulomb_hbm, gmap_hbm, out_ref,
                 wedge_ref, op_ref, x_ref, coulomb_ref, gmap_ref, scale_ref, g_ref,
                 lo_ref, hi_ref, pt_ref, t1_recv, t2_send, t2_recv, t_scale_ref, s_ref, y_ref, p_ref, c1_recv, c2_send, c2_recv, e00_ref, total_ref,
                 pair_ref, send_ref, recv_ref, far_send_ref, far_recv_ref, f_ref, own_ref, left_ref, top_ref,
                 low_ref, w_ref,
                 c1_s, c1_r, c2_s, c2_r, c3_s, c3_r, c4_s, c4_r, c5_s, c5_r, c6_s, c6_r, c7_s, c7_r,
                 pair_s, pair_r, near_s, near_r, far_s, far_r, swap_s, swap_r,
                 side_s, side_r, t1_s, t1_r, t2_s, t2_r, t3_s, t3_r, t4_s, t4_r, t5_s, t5_r, in_s):
    kb, gr, gc = lax.axis_index("kb"), lax.axis_index("gr"), lax.axis_index("gc")
    z, c = kb // 2, kb % 2
    other = 1 - c
    slots, owners = wedge_ref.shape
    bands, total_g = x_ref.shape
    band, width = out_ref.shape
    rows, wide = 2 * band, width // 2
    is_top, is_left = gr == 0, gc == 0

    fetched = [
        pltpu.make_async_copy(src, dst, in_s.at[i])
        for i, (src, dst) in enumerate([
            (gmap_hbm, gmap_ref), (x_hbm, x_ref), (wedge_hbm, wedge_ref), (op_hbm, op_ref), (coulomb_hbm, coulomb_ref)
        ])
    ]
    for copy in fetched:
        copy.start()

    def chip(delta, core=None):
        return (2 * ((z + delta + chips) % chips) + (c if core is None else core), gr, gc)

    def remote(src, dst, send, recv, who):
        return pltpu.make_async_remote_copy(
            src_ref=src, dst_ref=dst, send_sem=send, recv_sem=recv, device_id=who, device_id_type=MESH
        )

    partner = (2 * z + other, gr, gc)
    peers = {
        i: (kb, (gr + i // grid) % grid, (gc + i % grid) % grid) for i in range(1, grid * grid)
    }
    barrier = pltpu.get_barrier_semaphore()
    everyone = (
        [chip(d, core) for d in (1, -1, 2, -2) for core in (0, 1)]
        + [chip(d) for d in (4, -4, 8)] + [partner] + list(peers.values())
    )
    for who in everyone:
        pl.semaphore_signal(barrier, inc=1, device_id=who, device_id_type=MESH)

    for copy in fetched:
        copy.wait()

    eye = lax.broadcasted_iota(jnp.int32, (bands, bands), 0) == lax.broadcasted_iota(jnp.int32, (bands, bands), 1)
    gap = ec_ref[...] - ev_ref[...]
    weight = jnp.sqrt(4.0 / (float(owners * slots) * gap))
    weight = jnp.sum(jnp.where(eye, jnp.broadcast_to(weight, (bands, bands)), 0.0), axis=1, keepdims=True)
    y = (x_ref[...].astype(jnp.float32) * weight).astype(jnp.bfloat16)
    parts = total_g // LOW
    for h in range(parts):
        y_ref[h * bands:(h + 1) * bands, :] = y[:, h * LOW:(h + 1) * LOW]
    matched = jnp.where(wedge_ref[...] == kb, 1.0, 0.0)
    present = jnp.sum(matched, axis=0, keepdims=True)
    operation = jnp.sum(matched * op_ref[...].astype(jnp.float32), axis=0, keepdims=True)
    kinds = lax.broadcasted_iota(jnp.int32, (gmap_ref.shape[0], owners), 0).astype(jnp.float32)
    chosen = jnp.where(kinds == operation, present, 0.0).astype(jnp.bfloat16)
    count = lax.broadcasted_iota(jnp.int32, (LOW, 128), 0).astype(jnp.float32).astype(jnp.bfloat16)
    one, none = jnp.ones((LOW, 128), jnp.bfloat16), jnp.zeros((LOW, 128), jnp.bfloat16)

    def gather(side, at):
        maps = gmap_ref[:, pl.ds(at, width)]
        low_bits = (maps & (LOW - 1)).astype(jnp.float32).astype(jnp.bfloat16)
        high_bits = ((maps >> (LOW.bit_length() - 1)) + 1).astype(jnp.float32).astype(jnp.bfloat16)
        lo_ref[...] = lax.dot_general(chosen, low_bits, TN, preferred_element_type=jnp.float32)
        hi_ref[...] = lax.dot_general(chosen, high_bits, TN, preferred_element_type=jnp.float32)

        def pick(o, carry):
            low = jnp.broadcast_to(lo_ref[pl.ds(o, 1), :], (LOW, width)).astype(jnp.bfloat16)
            high = hi_ref[pl.ds(o, 1), :]
            onehot = jnp.concatenate(
                [jnp.where(count == low[:, t:t + 128], one, none) for t in range(0, width, 128)], axis=1
            )
            spread = jnp.dot(y_ref[...], onehot, preferred_element_type=jnp.float32)
            picked = jnp.zeros((bands, width), jnp.float32)
            for h in range(parts):
                picked = jnp.where(high == float(h + 1), spread[h * bands:(h + 1) * bands, :], picked)
            s_ref[pl.ds(pl.multiple_of(o * bands, bands), bands), side * width:(side + 1) * width] = picked.astype(jnp.bfloat16)
            return carry

        lax.fori_loop(0, owners, pick, 0, unroll=4)

    root = jnp.sqrt(coulomb_ref[...])

    def root_down(first, count, reach):
        ids = first + lax.broadcasted_iota(jnp.int32, (count, reach), 0)
        lanes = lax.broadcasted_iota(jnp.int32, (count, reach), 1)
        return jnp.sum(jnp.where(ids == lanes, jnp.broadcast_to(root[:, :reach], (count, reach)), 0.0), axis=1, keepdims=True)

    def scale_of(first_row, first_col, count, across):
        return root_down(first_row, count, total_g) * jnp.sqrt(
            coulomb_ref[:, pl.ds(pl.multiple_of(first_col, 128), across)]
        )

    def dielectric(value, scale, first_row, first_col):
        row = first_row + lax.broadcasted_iota(jnp.int32, value.shape, 0)
        col = first_col + lax.broadcasted_iota(jnp.int32, value.shape, 1)
        return jnp.where(row == col, 1.0, 0.0) + scale * value

    gather(0, 0)
    p_ref[...] = lax.dot_general(
        s_ref[:, pl.ds(pl.multiple_of(gr * BLOCK, BLOCK), BLOCK)], s_ref[:, :width], TN, preferred_element_type=jnp.float32
    )
    pl.semaphore_wait(barrier, len(everyone))

    def p_part(delta, core):
        k = (z + delta + chips) % grid
        return p_ref.at[pl.ds(pl.multiple_of(gc * rows + 8 * k, 8), 8), pl.ds(pl.multiple_of(core * wide, wide), wide)]

    near_parts = [(1, 0, c), (1, 1, c), (-1, 0, 2 + c), (-1, 1, 2 + c), (2, 0, 4 + c), (-2, 1, 4 + c), (0, other, 6)]
    stage1 = [
        remote(p_part(d, core), c1_recv.at[slot], c1_s.at[i], c1_r.at[slot], chip(d, core))
        for i, (d, core, slot) in enumerate(near_parts)
    ]
    for copy in stage1:
        copy.start()

    mine = pl.ds(pl.multiple_of(c * wide, wide), wide)
    theirs = pl.ds(pl.multiple_of(other * wide, wide), wide)

    gather(2, pl.multiple_of(gc * width, width))
    pt_ref[...] = lax.dot_general(
        s_ref[:, pl.ds(pl.multiple_of(gr * BLOCK, BLOCK), BLOCK)], s_ref[:, 2 * width:], TN, preferred_element_type=jnp.float32
    )

    def t_part(delta, core):
        k = (z + delta + chips) % grid
        return pt_ref.at[pl.ds(pl.multiple_of(rows * k, rows), rows), pl.ds(pl.multiple_of(core * wide, wide), wide)]

    top1 = [
        remote(t_part(d, core), t1_recv.at[slot], t1_s.at[i], t1_r.at[slot], chip(d, core))
        for i, (d, core, slot) in enumerate(near_parts)
    ]
    for copy in top1:
        copy.start()

    first_e = pl.multiple_of(gr * BLOCK + gc * rows + 8 * (z % grid), 8)
    scale_e = scale_of(first_e, c * wide, 8, wide)
    first_row, first_col = gr * width + z * rows, gc * width + c * wide
    first_t = pl.multiple_of(gr * BLOCK + rows * (z % grid), rows)
    scale_ref[...] = scale_of(first_row, first_col, rows, wide)
    t_scale_ref[...] = scale_of(first_t, first_col, rows, wide)

    value = p_part(0, c)[...]
    for slot in range(7):
        remote(p_part(0, other), c1_recv.at[slot], c1_s.at[0], c1_r.at[slot], partner).wait_recv()
        value = value + c1_recv[slot]
    c2_send[...] = value
    stage2 = [
        remote(c2_send, c2_recv.at[i], c2_s.at[i], c2_r.at[i], chip(d)) for i, d in enumerate((8, 4, -4))
    ]
    for copy in stage2:
        copy.start()

    gather(1, pl.multiple_of(gr * width, width))
    total_ref[...] = lax.dot_general(
        s_ref[:, width:2 * width], s_ref[:, 2 * width:], TN, preferred_element_type=jnp.float32
    )

    def chunk(off):
        return pl.ds(pl.multiple_of(((z + off + chips) % chips) * rows, rows), rows)

    near = [
        (9, 1, 2), (7, -1, 6), (5, 1, 1), (3, -1, 5), (6, 2, 9), (-6, -2, 11),
        (13, 1, 3), (11, -1, 7), (1, 1, 0), (15, -1, 4), (2, 2, 8), (-2, -2, 10),
    ]
    order = [off % chips for off, _, _ in near] + [8, 4, 12, 0]
    pairs = {
        off: remote(total_ref.at[chunk(off), theirs], pair_ref.at[i], pair_s.at[i], pair_r.at[i], partner)
        for i, off in enumerate(order)
    }
    for off in order:
        pairs[off].start()

    value = c2_send[...]
    for i in (1, 2, 0):
        stage2[i].wait_recv()
        value = value + c2_recv[i]
    part = e00_ref.at[pl.ds(first_e, 8), mine]
    part[...] = dielectric(value, scale_e, first_e, c * wide)
    two = jnp.where(c == 0, 2, -2)
    spread_to = [(1, 0, c), (1, 1, c), (-1, 0, 2 + c), (-1, 1, 2 + c), (two, 0, 4 + c), (two, 1, 4 + c), (0, other, 6)]
    stage3 = [
        remote(part, part, c3_s.at[i], c3_r.at[slot], chip(d, core)) for i, (d, core, slot) in enumerate(spread_to)
    ]
    for copy in stage3:
        copy.start()

    value = t_part(0, c)[...]
    for slot in range(7):
        remote(t_part(0, other), t1_recv.at[slot], t1_s.at[0], t1_r.at[slot], partner).wait_recv()
        value = value + t1_recv[slot]
    t2_send[...] = value
    top2 = [
        remote(t2_send, t2_recv.at[i], t2_s.at[i], t2_r.at[i], chip(d)) for i, d in enumerate((8, 4, -4))
    ]
    for copy in top2:
        copy.start()

    def own_part(off):
        off = off % chips
        pairs[off].wait_recv()
        return total_ref[chunk(off), mine] + pair_ref[order.index(off)]

    for slot in range(7):
        remote(part, part, c3_s.at[0], c3_r.at[slot], partner).wait_recv()

    def e00_part(r, s, half):
        return e00_ref.at[pl.ds(pl.multiple_of(r * BLOCK + s * rows, rows), rows), half]

    def whole_half(r, core):
        return jnp.logical_or(core == 1, r == 1)

    def cut_half(r, core):
        return jnp.logical_and(core == 0, r == 0)

    tile, rest = slice(0, BLOCK), slice(BLOCK, wide)

    def stage4(i, half, sends=None, recvs=None):
        part = e00_part(gr, gc, half)
        return remote(part, part, (c4_s if sends is None else sends).at[i], (c4_r if recvs is None else recvs).at[i], peers[i])

    def stage4_tile(i):
        return stage4(i, tile, c6_s, c6_r)

    def sender(i):
        return (gr + grid - i // grid) % grid, (gc + grid - i % grid) % grid

    @pl.when(cut_half(gr, c))
    def _():
        for i in peers:
            stage4_tile(i).start()
        for i in peers:
            stage4(i, rest).start()

    @pl.when(whole_half(gr, c))
    def _():
        for i in peers:
            stage4(i, mine).start()

    t_piece = top_ref.at[pl.ds(first_t, rows), mine]
    top3 = [
        remote(t_piece, t_piece, t3_s.at[i], t3_r.at[slot], chip(d, core)) for i, (d, core, slot) in enumerate(spread_to)
    ]

    def send_pieces():
        value = t2_send[...]
        for i in (1, 2, 0):
            top2[i].wait_recv()
            value = value + t2_recv[i]
        t_piece[...] = dielectric(value, t_scale_ref[...], first_t, first_col)
        for copy in top3:
            copy.start()

    def quarter(r):
        return top_ref.at[pl.ds(pl.multiple_of(r * BLOCK, BLOCK), BLOCK), mine]

    def to_column(i):
        return remote(quarter(gr), quarter(gr), t4_s.at[i - 1], t4_r.at[i - 1], (kb, (gr + i) % grid, gc))

    def to_core(i):
        r = (gr + grid - i) % grid
        return remote(quarter(r), quarter(r), t5_s.at[i - 1], t5_r.at[i - 1], partner)

    def send_column():
        for slot in range(7):
            remote(t_piece, t_piece, t3_s.at[0], t3_r.at[slot], partner).wait_recv()
        for i in range(1, grid):
            to_column(i).start()

    def send_core():
        for i in range(1, grid):
            to_column(i).wait_recv()
            to_core(i).start()

    def stage5(i, half):
        r, s = sender(i)
        return remote(e00_part(r, s, half), e00_part(r, s, half), c5_s.at[i], c5_r.at[i], partner)

    def stage5_tile(i):
        r, s = sender(i)
        return remote(e00_part(r, s, tile), e00_part(r, s, tile), c7_s.at[i], c7_r.at[i], partner)


    def gathered(j, extra):
        value = own_part(4 * j)
        for slot in (j, 4 + j) + extra:
            near_copies[slot].wait_recv()
            value = value + recv_ref[slot]
        return value

    far_list = [(2, (), 8), (1, (9,), 4), (3, (11,), -4)]

    def far_copy(i):
        return remote(far_send_ref.at[i], far_recv_ref.at[i], far_s.at[i], far_r.at[i], chip(far_list[i][2]))

    def end_e00_copies():
        for copy in stage3:
            copy.wait_send()

        @pl.when(cut_half(gr, c))
        def _():
            for i in peers:
                stage4_tile(i).wait_send()
                stage4(i, rest).wait_send()

        @pl.when(whole_half(gr, c))
        def _():
            for i in peers:
                stage4(i, mine).wait_send()
        for i in peers:
            @pl.when(cut_half(sender(i)[0], c))
            def _():
                stage5_tile(i).wait_send()
                stage5(i, rest).wait_send()

            @pl.when(whole_half(sender(i)[0], c))
            def _():
                stage5(i, mine).wait_send()

    def send_far():
        for i, (j, extra, delta) in enumerate(far_list):
            far_send_ref[i] = gathered(j, extra)
            far_copy(i).start()

    swap = remote(f_ref.at[pl.ds(pl.multiple_of(other * band, band), band)], own_ref.at[:, mine], swap_s, swap_r, partner)

    def send_own():
        value = gathered(0, (8, 10))
        for i in (1, 2, 0):
            far_copy(i).wait_recv()
            value = value + far_recv_ref[i]
        value = dielectric(value, scale_ref[...], first_row, first_col)
        f_ref[...] = value

        swap.start()
        own_ref[:, mine] = f_ref[pl.ds(pl.multiple_of(c * band, band), band)]

    def to_side(i):
        return remote(own_ref, left_ref, side_s.at[i - 1], side_r, (kb, gr, (gc + i) % grid))

    def send_side():
        swap.wait_recv()

        @pl.when(is_left)
        def _():
            for i in range(1, grid):
                to_side(i).start()

    def wait_rows():
        for i in peers:
            @pl.when(cut_half(sender(i)[0], c))
            def _():
                stage4(i, rest).wait_recv()
                stage5(i, rest).start()

            @pl.when(whole_half(sender(i)[0], c))
            def _():
                stage4(i, mine).wait_recv()
                stage5(i, mine).start()

    def wait_halves():
        for i in peers:
            @pl.when(cut_half(sender(i)[0], other))
            def _():
                stage5(i, rest).wait_recv()

            @pl.when(whole_half(sender(i)[0], other))
            def _():
                stage5(i, theirs).wait_recv()

    near_copies = {}
    for off, delta, slot in near:
        send_ref[slot] = own_part(off)
        copy = remote(send_ref.at[slot], recv_ref.at[slot], near_s.at[slot], near_r.at[slot], chip(delta))
        copy.start()
        near_copies[slot] = copy

    @pl.when(c == 0)
    def _():
        for i in peers:
            @pl.when(sender(i)[0] == 0)
            def _():
                stage4_tile(i).wait_recv()
                stage5_tile(i).start()

    @pl.when(c == 1)
    def _():
        for i in peers:
            @pl.when(sender(i)[0] == 0)
            def _():
                stage5_tile(i).wait_recv()

    plan = {
        (0, 2): send_pieces, (0, 5): wait_rows, (0, 11): wait_halves, (0, 15): end_e00_copies,
        (1, 0): send_far, (1, 2): send_column, (2, 15): send_own, (3, 1): send_core, (3, 7): send_side,
    }
    cuts = [slice(b * BLOCK, (b + 1) * BLOCK) for b in range(width // BLOCK)]
    for b, cut in enumerate(cuts):
        def hook(g):
            if (b, g) in plan:
                plan[b, g]()

        inverse = inverse_factor(e00_ref[cut, cut], hook)
        if b:
            g_ref[cut, :b * BLOCK] = product(inverse, g_ref[cut, :b * BLOCK])
        g_ref[cut, cut] = inverse
        after = (b + 1) * BLOCK
        if after < width:
            across = product(inverse, e00_ref[cut, after:])
            for cut2 in cuts[b + 1:]:
                at = cut2.start
                e00_ref[cut2, at:] = e00_ref[cut2, at:] - product(
                    across[:, at - after:at - after + BLOCK], across[:, at - after:], TN
                )
            change = product(across, g_ref[cut, :after], TN)
            if b:
                g_ref[after:, :cut.start] = g_ref[after:, :cut.start] - change[:, :cut.start]
            g_ref[after:, cut] = -change[:, cut.start:]

    @pl.when(jnp.logical_not(is_left))
    def _():
        to_side(1).wait_recv()

    @pl.when(is_left)
    def _():
        left_ref[...] = own_ref[...]

    for cut in cuts:
        low_ref[:, cut] = product(left_ref[:, :cut.stop], g_ref[cut, :cut.stop], NT)
    for cut in cuts:
        w_ref[:, cut] = product(low_ref[:, cut.start:], g_ref[cut.start:, cut])

    for i in range(1, grid):
        to_core(i).wait_recv()

    row = kb * band + lax.broadcasted_iota(jnp.int32, (band, width), 0)
    col = lax.broadcasted_iota(jnp.int32, (band, width), 1)
    factor_side = jnp.where(is_top & (col > row), 0.0, low_ref[...])
    trail = own_ref[...] - product(w_ref[...], top_ref[...])
    out_ref[...] = jnp.where(is_left, factor_side, jnp.where(is_top, own_ref[...], trail))

    for copy in stage1 + stage2 + top1 + top2 + top3 + list(pairs.values()) + list(near_copies.values()) + [swap]:
        copy.wait_send()
    for i in range(3):
        far_copy(i).wait_send()
    for i in range(1, grid):
        to_column(i).wait_send()
        to_core(i).wait_send()

    @pl.when(is_left)
    def _():
        for i in range(1, grid):
            to_side(i).wait_send()


def body(wedge_pairs, e_cond, e_val, coulomb, owned_wedge, owned_op, gmap):
    members = lax.axis_size("kb")
    grid = lax.axis_size("gr")
    chips = members // 2
    total_g = gmap.shape[1]
    width = total_g // grid
    band = width // members
    owners, slots = owned_wedge.shape
    hbm = pl.BlockSpec(memory_space=pltpu.HBM)
    x = wedge_pairs.reshape(-1, total_g)
    bands = x.shape[0]
    vmem = pl.BlockSpec(memory_space=pltpu.VMEM)
    dma = pltpu.SemaphoreType.DMA
    piece = (2 * band, width // 2)
    f32 = jnp.float32
    return pl.pallas_call(
        functools.partial(whole_kernel, chips, grid),
        out_shape=jax.ShapeDtypeStruct((band, width), f32),
        in_specs=[hbm] * 3 + [vmem] * 2 + [hbm] * 2,
        out_specs=vmem,
        scratch_shapes=[
            pltpu.VMEM((slots, owners), jnp.int32),
            pltpu.VMEM((slots, owners), jnp.int32),
            pltpu.VMEM(x.shape, x.dtype),
            pltpu.VMEM((1, total_g), f32),
            pltpu.VMEM(gmap.shape, gmap.dtype),
            pltpu.VMEM(piece, f32),
            pltpu.VMEM((width, width), f32),
            pltpu.VMEM((owners, width), f32),
            pltpu.VMEM((owners, width), f32),
            pltpu.VMEM((BLOCK, width), f32),
            pltpu.VMEM((7,) + piece, f32),
            pltpu.VMEM(piece, f32),
            pltpu.VMEM((3,) + piece, f32),
            pltpu.VMEM(piece, f32),
            pltpu.VMEM((owners * bands, 3 * width), jnp.bfloat16),
            pltpu.VMEM((bands * (total_g // LOW), LOW), jnp.bfloat16),
            pltpu.VMEM((BLOCK, width), f32),
            pltpu.VMEM((7, 8, width // 2), f32),
            pltpu.VMEM((8, width // 2), f32),
            pltpu.VMEM((3, 8, width // 2), f32),
            pltpu.VMEM((width, width), f32),
            pltpu.VMEM((width, width), f32),
            pltpu.VMEM((chips,) + piece, f32),
            pltpu.VMEM((12,) + piece, f32),
            pltpu.VMEM((12,) + piece, f32),
            pltpu.VMEM((3,) + piece, f32),
            pltpu.VMEM((3,) + piece, f32),
            pltpu.VMEM(piece, f32),
            pltpu.VMEM((band, width), f32),
            pltpu.VMEM((band, width), f32),
            pltpu.VMEM((width, width), f32),
            pltpu.VMEM((band, width), f32),
            pltpu.VMEM((band, width), f32),
            dma((7,)), dma((7,)),
            dma((3,)), dma((3,)),
            dma((7,)), dma((7,)),
            dma((grid * grid,)), dma((grid * grid,)),
            dma((grid * grid,)), dma((grid * grid,)),
            dma((grid * grid,)), dma((grid * grid,)),
            dma((grid * grid,)), dma((grid * grid,)),
            dma((chips,)), dma((chips,)),
            dma((12,)), dma((12,)),
            dma((3,)), dma((3,)),
            dma, dma,
            dma((grid - 1,)), dma,
            dma((7,)), dma((7,)),
            dma((3,)), dma((3,)),
            dma((7,)), dma((7,)),
            dma((grid - 1,)), dma((grid - 1,)),
            dma((grid - 1,)), dma((grid - 1,)),
            dma((5,)),
        ],
        compiler_params=pltpu.CompilerParams(
            collective_id=0, has_side_effects=True, vmem_limit_bytes=63 << 20
        ),
        name="whole",
    )(owned_wedge.T, owned_op.T, x, e_cond, e_val, coulomb.reshape(1, -1), gmap)


def solution(mesh):
    placed = (P("kb", None, None, None), P("kb", None), P("kb", None), P(), P(), P(), P())
    return jax.shard_map(
        body, mesh=mesh, in_specs=placed, out_specs=P(("gr", "kb"), "gc"), check_vma=False
    )
```

```python
import functools
import jax
import jax.numpy as jnp
from jax import lax
from jax.experimental import pallas as pl
from jax.experimental.pallas import tpu as pltpu
from jax.sharding import PartitionSpec as P

MESH = pl.DeviceIdType.MESH
HI = lax.Precision.HIGHEST
NT = (((1,), (1,)), ((), ()))
TN = (((0,), (0,)), ((), ()))
LOW = 256
BLOCK = 128


def product(a, b, dims=(((1,), (0,)), ((), ()))):
    return lax.dot_general(a, b, dims, precision=HI, preferred_element_type=jnp.float32)


def thirds(a):
    first = a.astype(jnp.bfloat16).astype(jnp.float32)
    second = (a - first).astype(jnp.bfloat16).astype(jnp.float32)
    return first, second, a - first - second


def gram(rows):
    p, q, r = thirds(rows)
    one = jnp.concatenate([p, p, q, p, r, q], axis=0).astype(jnp.bfloat16)
    two = jnp.concatenate([p, q, p, r, p, q], axis=0).astype(jnp.bfloat16)
    return lax.dot_general(one, two, TN, preferred_element_type=jnp.float32)


def inverse_factor(d, hook):
    n = d.shape[0]
    groups = n // 8
    lane = lax.broadcasted_iota(jnp.int32, (8, n), 1)
    sub = lax.broadcasted_iota(jnp.int32, (8, n), 0)
    rows = [d[8 * i:8 * i + 8, :] for i in range(groups)]
    out = []
    for g in range(groups):
        base = 8 * g
        hook(g)
        follows = g + 1 < groups
        head, after = rows[g], rows[g + 1] if follows else None
        cols = [jnp.broadcast_to(head[:, base + k:base + k + 1], (8, n)) for k in range(8)]
        below = [jnp.broadcast_to(after[:, base + k:base + k + 1], (8, n)) for k in range(8)] if follows else None
        inside = (lane >= base) & (lane < base + 8)
        head = jnp.where(inside, jnp.where(lane - base == sub, 1.0, 0.0), head)
        if follows:
            after = jnp.where(inside, 0.0, after)
        entry = {(i, k): jnp.broadcast_to(cols[k][i:i + 1, :], (8, n)) for i in range(8) for k in range(i + 1)}
        row = [jnp.broadcast_to(head[i:i + 1, :], (8, n)) for i in range(8)]
        done = jnp.zeros((8, n), jnp.float32)
        for j in range(0, 8, 2):
            a, b, d2 = entry[j, j], entry[j + 1, j], entry[j + 1, j + 1]
            scale = lax.rsqrt(a)
            cross = b * scale
            scale2 = lax.rsqrt(a * d2 - b * b) * (a * scale)
            pivot_row = row[j] * scale
            pivot_row2 = (row[j + 1] - cross * pivot_row) * scale2
            done = jnp.where(sub == j, pivot_row, jnp.where(sub == j + 1, pivot_row2, done))
            mult = {i: entry[i, j] * scale for i in range(j + 2, 8)}
            mult2 = {i: (entry[i, j + 1] - cross * mult[i]) * scale2 for i in range(j + 2, 8)}
            for i in range(j + 2, 8):
                row[i] = (row[i] - mult[i] * pivot_row) - mult2[i] * pivot_row2
                for k in range(j + 2, i + 1):
                    entry[i, k] = (entry[i, k] - mult[i] * mult[k]) - mult2[i] * mult2[k]
            if follows:
                step = below[j] * scale
                step2 = (below[j + 1] - step * cross) * scale2
                after = (after - step * pivot_row) - step2 * pivot_row2
                for k in range(j + 2, 8):
                    below[k] = (below[k] - step * mult[k]) - step2 * mult2[k]
        out.append(jnp.where(lane <= sub + base, done, 0.0))
        if follows:
            rows[g + 1] = after
        if g + 2 < groups:
            change = gram(done)
            for i in range(g + 2, groups):
                rows[i] = jnp.where(inside, 0.0, rows[i]) - change[8 * i:8 * i + 8, :]
    return jnp.concatenate(out, axis=0)


def whole_kernel(chips, grid, wedge_hbm, op_hbm, x_hbm, ec_ref, ev_ref, coulomb_hbm, gmap_hbm, out_ref,
                 wedge_ref, op_ref, x_ref, coulomb_ref, gmap_ref, scale_ref, g_ref,
                 lo_ref, hi_ref, pt_ref, t1_recv, t2_send, t2_recv, t_scale_ref, s_ref, y_ref, p_ref, c1_recv, c2_send, c2_recv, e00_ref, total_ref,
                 pair_ref, send_ref, recv_ref, far_send_ref, far_recv_ref, f_ref, own_ref, left_ref, top_ref,
                 low_ref, w_ref,
                 c1_s, c1_r, c2_s, c2_r, c3_s, c3_r, c4_s, c4_r, c5_s, c5_r, c6_s, c6_r, c7_s, c7_r,
                 pair_s, pair_r, near_s, near_r, far_s, far_r, swap_s, swap_r,
                 side_s, side_r, t1_s, t1_r, t2_s, t2_r, t3_s, t3_r, t4_s, t4_r, t5_s, t5_r, in_s):
    kb, gr, gc = lax.axis_index("kb"), lax.axis_index("gr"), lax.axis_index("gc")
    z, c = kb // 2, kb % 2
    other = 1 - c
    slots, owners = wedge_ref.shape
    bands, total_g = x_ref.shape
    band, width = out_ref.shape
    rows, wide = 2 * band, width // 2
    is_top, is_left = gr == 0, gc == 0

    fetched = [
        pltpu.make_async_copy(src, dst, in_s.at[i])
        for i, (src, dst) in enumerate([
            (gmap_hbm, gmap_ref), (x_hbm, x_ref), (wedge_hbm, wedge_ref), (op_hbm, op_ref), (coulomb_hbm, coulomb_ref)
        ])
    ]
    for copy in fetched:
        copy.start()

    def chip(delta, core=None):
        return (2 * ((z + delta + chips) % chips) + (c if core is None else core), gr, gc)

    def remote(src, dst, send, recv, who):
        return pltpu.make_async_remote_copy(
            src_ref=src, dst_ref=dst, send_sem=send, recv_sem=recv, device_id=who, device_id_type=MESH
        )

    partner = (2 * z + other, gr, gc)
    peers = {
        i: (kb, (gr + i // grid) % grid, (gc + i % grid) % grid) for i in range(1, grid * grid)
    }
    barrier = pltpu.get_barrier_semaphore()
    everyone = (
        [chip(d, core) for d in (1, -1, 2, -2) for core in (0, 1)]
        + [chip(d) for d in (4, -4, 8)] + [partner] + list(peers.values())
    )
    for who in everyone:
        pl.semaphore_signal(barrier, inc=1, device_id=who, device_id_type=MESH)

    for copy in fetched:
        copy.wait()

    eye = lax.broadcasted_iota(jnp.int32, (bands, bands), 0) == lax.broadcasted_iota(jnp.int32, (bands, bands), 1)
    gap = ec_ref[...] - ev_ref[...]
    weight = jnp.sqrt(4.0 / (float(owners * slots) * gap))
    weight = jnp.sum(jnp.where(eye, jnp.broadcast_to(weight, (bands, bands)), 0.0), axis=1, keepdims=True)
    y = (x_ref[...].astype(jnp.float32) * weight).astype(jnp.bfloat16)
    parts = total_g // LOW
    for h in range(parts):
        y_ref[h * bands:(h + 1) * bands, :] = y[:, h * LOW:(h + 1) * LOW]
    matched = jnp.where(wedge_ref[...] == kb, 1.0, 0.0)
    present = jnp.sum(matched, axis=0, keepdims=True)
    operation = jnp.sum(matched * op_ref[...].astype(jnp.float32), axis=0, keepdims=True)
    kinds = lax.broadcasted_iota(jnp.int32, (gmap_ref.shape[0], owners), 0).astype(jnp.float32)
    chosen = jnp.where(kinds == operation, present, 0.0).astype(jnp.bfloat16)
    count = lax.broadcasted_iota(jnp.int32, (LOW, 128), 0).astype(jnp.float32).astype(jnp.bfloat16)
    one, none = jnp.ones((LOW, 128), jnp.bfloat16), jnp.zeros((LOW, 128), jnp.bfloat16)

    def gather(side, at):
        maps = gmap_ref[:, pl.ds(at, width)]
        low_bits = (maps & (LOW - 1)).astype(jnp.float32).astype(jnp.bfloat16)
        high_bits = ((maps >> (LOW.bit_length() - 1)) + 1).astype(jnp.float32).astype(jnp.bfloat16)
        lo_ref[...] = lax.dot_general(chosen, low_bits, TN, preferred_element_type=jnp.float32)
        hi_ref[...] = lax.dot_general(chosen, high_bits, TN, preferred_element_type=jnp.float32)

        def pick(o, carry):
            low = jnp.broadcast_to(lo_ref[pl.ds(o, 1), :], (LOW, width)).astype(jnp.bfloat16)
            high = hi_ref[pl.ds(o, 1), :]
            onehot = jnp.concatenate(
                [jnp.where(count == low[:, t:t + 128], one, none) for t in range(0, width, 128)], axis=1
            )
            spread = jnp.dot(y_ref[...], onehot, preferred_element_type=jnp.float32)
            picked = jnp.zeros((bands, width), jnp.float32)
            for h in range(parts):
                picked = jnp.where(high == float(h + 1), spread[h * bands:(h + 1) * bands, :], picked)
            s_ref[pl.ds(pl.multiple_of(o * bands, bands), bands), side * width:(side + 1) * width] = picked.astype(jnp.bfloat16)
            return carry

        lax.fori_loop(0, owners, pick, 0, unroll=4)

    root = jnp.sqrt(coulomb_ref[...])

    def root_down(first, count, reach):
        ids = first + lax.broadcasted_iota(jnp.int32, (count, reach), 0)
        lanes = lax.broadcasted_iota(jnp.int32, (count, reach), 1)
        return jnp.sum(jnp.where(ids == lanes, jnp.broadcast_to(root[:, :reach], (count, reach)), 0.0), axis=1, keepdims=True)

    def scale_of(first_row, first_col, count, across):
        return root_down(first_row, count, total_g) * jnp.sqrt(
            coulomb_ref[:, pl.ds(pl.multiple_of(first_col, 128), across)]
        )

    def dielectric(value, scale, first_row, first_col):
        row = first_row + lax.broadcasted_iota(jnp.int32, value.shape, 0)
        col = first_col + lax.broadcasted_iota(jnp.int32, value.shape, 1)
        return jnp.where(row == col, 1.0, 0.0) + scale * value

    gather(0, 0)
    p_ref[...] = lax.dot_general(
        s_ref[:, pl.ds(pl.multiple_of(gr * BLOCK, BLOCK), BLOCK)], s_ref[:, :width], TN, preferred_element_type=jnp.float32
    )
    pl.semaphore_wait(barrier, len(everyone))

    def p_part(delta, core):
        k = (z + delta + chips) % grid
        return p_ref.at[pl.ds(pl.multiple_of(gc * rows + 8 * k, 8), 8), pl.ds(pl.multiple_of(core * wide, wide), wide)]

    near_parts = [(1, 0, c), (1, 1, c), (-1, 0, 2 + c), (-1, 1, 2 + c), (2, 0, 4 + c), (-2, 1, 4 + c), (0, other, 6)]
    stage1 = [
        remote(p_part(d, core), c1_recv.at[slot], c1_s.at[i], c1_r.at[slot], chip(d, core))
        for i, (d, core, slot) in enumerate(near_parts)
    ]
    for copy in stage1:
        copy.start()

    mine = pl.ds(pl.multiple_of(c * wide, wide), wide)
    theirs = pl.ds(pl.multiple_of(other * wide, wide), wide)

    gather(2, pl.multiple_of(gc * width, width))
    value = p_part(0, c)[...]
    for slot in range(7):
        remote(p_part(0, other), c1_recv.at[slot], c1_s.at[0], c1_r.at[slot], partner).wait_recv()
        value = value + c1_recv[slot]
    c2_send[...] = value
    stage2 = [
        remote(c2_send, c2_recv.at[i], c2_s.at[i], c2_r.at[i], chip(d)) for i, d in enumerate((8, 4, -4))
    ]
    for copy in stage2:
        copy.start()

    pt_ref[...] = lax.dot_general(
        s_ref[:, pl.ds(pl.multiple_of(gr * BLOCK, BLOCK), BLOCK)], s_ref[:, 2 * width:], TN, preferred_element_type=jnp.float32
    )

    def t_part(delta, core):
        k = (z + delta + chips) % grid
        return pt_ref.at[pl.ds(pl.multiple_of(rows * k, rows), rows), pl.ds(pl.multiple_of(core * wide, wide), wide)]

    top1 = [
        remote(t_part(d, core), t1_recv.at[slot], t1_s.at[i], t1_r.at[slot], chip(d, core))
        for i, (d, core, slot) in enumerate(near_parts)
    ]
    for copy in top1:
        copy.start()

    first_e = pl.multiple_of(gr * BLOCK + gc * rows + 8 * (z % grid), 8)
    scale_e = scale_of(first_e, c * wide, 8, wide)
    first_row, first_col = gr * width + z * rows, gc * width + c * wide
    first_t = pl.multiple_of(gr * BLOCK + rows * (z % grid), rows)
    scale_ref[...] = scale_of(first_row, first_col, rows, wide)
    t_scale_ref[...] = scale_of(first_t, first_col, rows, wide)

    gather(1, pl.multiple_of(gr * width, width))
    value = c2_send[...]
    for i in (1, 2, 0):
        stage2[i].wait_recv()
        value = value + c2_recv[i]
    part = e00_ref.at[pl.ds(first_e, 8), mine]
    part[...] = dielectric(value, scale_e, first_e, c * wide)
    two = jnp.where(c == 0, 2, -2)
    spread_to = [(1, 0, c), (1, 1, c), (-1, 0, 2 + c), (-1, 1, 2 + c), (two, 0, 4 + c), (two, 1, 4 + c), (0, other, 6)]
    stage3 = [
        remote(part, part, c3_s.at[i], c3_r.at[slot], chip(d, core)) for i, (d, core, slot) in enumerate(spread_to)
    ]
    for copy in stage3:
        copy.start()

    value = t_part(0, c)[...]
    for slot in range(7):
        remote(t_part(0, other), t1_recv.at[slot], t1_s.at[0], t1_r.at[slot], partner).wait_recv()
        value = value + t1_recv[slot]
    t2_send[...] = value
    top2 = [
        remote(t2_send, t2_recv.at[i], t2_s.at[i], t2_r.at[i], chip(d)) for i, d in enumerate((8, 4, -4))
    ]
    for copy in top2:
        copy.start()

    total_ref[...] = lax.dot_general(
        s_ref[:, width:2 * width], s_ref[:, 2 * width:], TN, preferred_element_type=jnp.float32
    )

    def chunk(off):
        return pl.ds(pl.multiple_of(((z + off + chips) % chips) * rows, rows), rows)

    near = [
        (9, 1, 2), (7, -1, 6), (5, 1, 1), (3, -1, 5), (6, 2, 9), (-6, -2, 11),
        (13, 1, 3), (11, -1, 7), (1, 1, 0), (15, -1, 4), (2, 2, 8), (-2, -2, 10),
    ]
    order = [off % chips for off, _, _ in near] + [8, 4, 12, 0]
    pairs = {
        off: remote(total_ref.at[chunk(off), theirs], pair_ref.at[i], pair_s.at[i], pair_r.at[i], partner)
        for i, off in enumerate(order)
    }
    for off in order:
        pairs[off].start()

    def own_part(off):
        off = off % chips
        pairs[off].wait_recv()
        return total_ref[chunk(off), mine] + pair_ref[order.index(off)]

    for slot in range(7):
        remote(part, part, c3_s.at[0], c3_r.at[slot], partner).wait_recv()

    def e00_part(r, s, half):
        return e00_ref.at[pl.ds(pl.multiple_of(r * BLOCK + s * rows, rows), rows), half]

    def whole_half(r, core):
        return jnp.logical_or(core == 1, r == 1)

    def cut_half(r, core):
        return jnp.logical_and(core == 0, r == 0)

    tile, rest = slice(0, BLOCK), slice(BLOCK, wide)

    def stage4(i, half, sends=None, recvs=None):
        part = e00_part(gr, gc, half)
        return remote(part, part, (c4_s if sends is None else sends).at[i], (c4_r if recvs is None else recvs).at[i], peers[i])

    def stage4_tile(i):
        return stage4(i, tile, c6_s, c6_r)

    def sender(i):
        return (gr + grid - i // grid) % grid, (gc + grid - i % grid) % grid

    @pl.when(cut_half(gr, c))
    def _():
        for i in peers:
            stage4_tile(i).start()
        for i in peers:
            stage4(i, rest).start()

    @pl.when(whole_half(gr, c))
    def _():
        for i in peers:
            stage4(i, mine).start()

    t_piece = top_ref.at[pl.ds(first_t, rows), mine]
    top3 = [
        remote(t_piece, t_piece, t3_s.at[i], t3_r.at[slot], chip(d, core)) for i, (d, core, slot) in enumerate(spread_to)
    ]

    def send_pieces():
        value = t2_send[...]
        for i in (1, 2, 0):
            top2[i].wait_recv()
            value = value + t2_recv[i]
        t_piece[...] = dielectric(value, t_scale_ref[...], first_t, first_col)
        for copy in top3:
            copy.start()

    def quarter(r):
        return top_ref.at[pl.ds(pl.multiple_of(r * BLOCK, BLOCK), BLOCK), mine]

    def to_column(i):
        return remote(quarter(gr), quarter(gr), t4_s.at[i - 1], t4_r.at[i - 1], (kb, (gr + i) % grid, gc))

    def to_core(i):
        r = (gr + grid - i) % grid
        return remote(quarter(r), quarter(r), t5_s.at[i - 1], t5_r.at[i - 1], partner)

    def send_column():
        for slot in range(7):
            remote(t_piece, t_piece, t3_s.at[0], t3_r.at[slot], partner).wait_recv()
        for i in range(1, grid):
            to_column(i).start()

    def send_core():
        for i in range(1, grid):
            to_column(i).wait_recv()
            to_core(i).start()

    def stage5(i, half):
        r, s = sender(i)
        return remote(e00_part(r, s, half), e00_part(r, s, half), c5_s.at[i], c5_r.at[i], partner)

    def stage5_tile(i):
        r, s = sender(i)
        return remote(e00_part(r, s, tile), e00_part(r, s, tile), c7_s.at[i], c7_r.at[i], partner)


    def gathered(j, extra):
        value = own_part(4 * j)
        for slot in (j, 4 + j) + extra:
            near_copies[slot].wait_recv()
            value = value + recv_ref[slot]
        return value

    far_list = [(2, (), 8), (1, (9,), 4), (3, (11,), -4)]

    def far_copy(i):
        return remote(far_send_ref.at[i], far_recv_ref.at[i], far_s.at[i], far_r.at[i], chip(far_list[i][2]))

    def end_e00_copies():
        for copy in stage3:
            copy.wait_send()

        @pl.when(cut_half(gr, c))
        def _():
            for i in peers:
                stage4_tile(i).wait_send()
                stage4(i, rest).wait_send()

        @pl.when(whole_half(gr, c))
        def _():
            for i in peers:
                stage4(i, mine).wait_send()
        for i in peers:
            @pl.when(cut_half(sender(i)[0], c))
            def _():
                stage5_tile(i).wait_send()
                stage5(i, rest).wait_send()

            @pl.when(whole_half(sender(i)[0], c))
            def _():
                stage5(i, mine).wait_send()

    def send_far():
        for i, (j, extra, delta) in enumerate(far_list):
            far_send_ref[i] = gathered(j, extra)
            far_copy(i).start()

    swap = remote(f_ref.at[pl.ds(pl.multiple_of(other * band, band), band)], own_ref.at[:, mine], swap_s, swap_r, partner)

    def send_own():
        value = gathered(0, (8, 10))
        for i in (1, 2, 0):
            far_copy(i).wait_recv()
            value = value + far_recv_ref[i]
        value = dielectric(value, scale_ref[...], first_row, first_col)
        f_ref[...] = value

        swap.start()
        own_ref[:, mine] = f_ref[pl.ds(pl.multiple_of(c * band, band), band)]

    def to_side(i):
        return remote(own_ref, left_ref, side_s.at[i - 1], side_r, (kb, gr, (gc + i) % grid))

    def send_side():
        swap.wait_recv()

        @pl.when(is_left)
        def _():
            for i in range(1, grid):
                to_side(i).start()

    def wait_rows():
        for i in peers:
            @pl.when(cut_half(sender(i)[0], c))
            def _():
                stage4(i, rest).wait_recv()
                stage5(i, rest).start()

            @pl.when(whole_half(sender(i)[0], c))
            def _():
                stage4(i, mine).wait_recv()
                stage5(i, mine).start()

    def wait_halves():
        for i in peers:
            @pl.when(cut_half(sender(i)[0], other))
            def _():
                stage5(i, rest).wait_recv()

            @pl.when(whole_half(sender(i)[0], other))
            def _():
                stage5(i, theirs).wait_recv()

    near_copies = {}
    for off, delta, slot in near:
        send_ref[slot] = own_part(off)
        copy = remote(send_ref.at[slot], recv_ref.at[slot], near_s.at[slot], near_r.at[slot], chip(delta))
        copy.start()
        near_copies[slot] = copy

    @pl.when(c == 0)
    def _():
        for i in peers:
            @pl.when(sender(i)[0] == 0)
            def _():
                stage4_tile(i).wait_recv()
                stage5_tile(i).start()

    @pl.when(c == 1)
    def _():
        for i in peers:
            @pl.when(sender(i)[0] == 0)
            def _():
                stage5_tile(i).wait_recv()

    plan = {
        (0, 2): send_pieces, (0, 5): wait_rows, (0, 11): wait_halves, (0, 15): end_e00_copies,
        (1, 0): send_far, (1, 2): send_column, (2, 15): send_own, (3, 1): send_core, (3, 7): send_side,
    }
    cuts = [slice(b * BLOCK, (b + 1) * BLOCK) for b in range(width // BLOCK)]
    for b, cut in enumerate(cuts):
        def hook(g):
            if (b, g) in plan:
                plan[b, g]()

        inverse = inverse_factor(e00_ref[cut, cut], hook)
        if b:
            g_ref[cut, :b * BLOCK] = product(inverse, g_ref[cut, :b * BLOCK])
        g_ref[cut, cut] = inverse
        after = (b + 1) * BLOCK
        if after < width:
            across = product(inverse, e00_ref[cut, after:])
            for cut2 in cuts[b + 1:]:
                at = cut2.start
                e00_ref[cut2, at:] = e00_ref[cut2, at:] - product(
                    across[:, at - after:at - after + BLOCK], across[:, at - after:], TN
                )
            change = product(across, g_ref[cut, :after], TN)
            if b:
                g_ref[after:, :cut.start] = g_ref[after:, :cut.start] - change[:, :cut.start]
            g_ref[after:, cut] = -change[:, cut.start:]

    @pl.when(jnp.logical_not(is_left))
    def _():
        to_side(1).wait_recv()

    @pl.when(is_left)
    def _():
        left_ref[...] = own_ref[...]

    for cut in cuts:
        low_ref[:, cut] = product(left_ref[:, :cut.stop], g_ref[cut, :cut.stop], NT)
    for cut in cuts:
        w_ref[:, cut] = product(low_ref[:, cut.start:], g_ref[cut.start:, cut])

    for i in range(1, grid):
        to_core(i).wait_recv()

    row = kb * band + lax.broadcasted_iota(jnp.int32, (band, width), 0)
    col = lax.broadcasted_iota(jnp.int32, (band, width), 1)
    factor_side = jnp.where(is_top & (col > row), 0.0, low_ref[...])
    trail = own_ref[...] - product(w_ref[...], top_ref[...])
    out_ref[...] = jnp.where(is_left, factor_side, jnp.where(is_top, own_ref[...], trail))

    for copy in stage1 + stage2 + top1 + top2 + top3 + list(pairs.values()) + list(near_copies.values()) + [swap]:
        copy.wait_send()
    for i in range(3):
        far_copy(i).wait_send()
    for i in range(1, grid):
        to_column(i).wait_send()
        to_core(i).wait_send()

    @pl.when(is_left)
    def _():
        for i in range(1, grid):
            to_side(i).wait_send()


def body(wedge_pairs, e_cond, e_val, coulomb, owned_wedge, owned_op, gmap):
    members = lax.axis_size("kb")
    grid = lax.axis_size("gr")
    chips = members // 2
    total_g = gmap.shape[1]
    width = total_g // grid
    band = width // members
    owners, slots = owned_wedge.shape
    hbm = pl.BlockSpec(memory_space=pltpu.HBM)
    x = wedge_pairs.reshape(-1, total_g)
    bands = x.shape[0]
    vmem = pl.BlockSpec(memory_space=pltpu.VMEM)
    dma = pltpu.SemaphoreType.DMA
    piece = (2 * band, width // 2)
    f32 = jnp.float32
    return pl.pallas_call(
        functools.partial(whole_kernel, chips, grid),
        out_shape=jax.ShapeDtypeStruct((band, width), f32),
        in_specs=[hbm] * 3 + [vmem] * 2 + [hbm] * 2,
        out_specs=vmem,
        scratch_shapes=[
            pltpu.VMEM((slots, owners), jnp.int32),
            pltpu.VMEM((slots, owners), jnp.int32),
            pltpu.VMEM(x.shape, x.dtype),
            pltpu.VMEM((1, total_g), f32),
            pltpu.VMEM(gmap.shape, gmap.dtype),
            pltpu.VMEM(piece, f32),
            pltpu.VMEM((width, width), f32),
            pltpu.VMEM((owners, width), f32),
            pltpu.VMEM((owners, width), f32),
            pltpu.VMEM((BLOCK, width), f32),
            pltpu.VMEM((7,) + piece, f32),
            pltpu.VMEM(piece, f32),
            pltpu.VMEM((3,) + piece, f32),
            pltpu.VMEM(piece, f32),
            pltpu.VMEM((owners * bands, 3 * width), jnp.bfloat16),
            pltpu.VMEM((bands * (total_g // LOW), LOW), jnp.bfloat16),
            pltpu.VMEM((BLOCK, width), f32),
            pltpu.VMEM((7, 8, width // 2), f32),
            pltpu.VMEM((8, width // 2), f32),
            pltpu.VMEM((3, 8, width // 2), f32),
            pltpu.VMEM((width, width), f32),
            pltpu.VMEM((width, width), f32),
            pltpu.VMEM((chips,) + piece, f32),
            pltpu.VMEM((12,) + piece, f32),
            pltpu.VMEM((12,) + piece, f32),
            pltpu.VMEM((3,) + piece, f32),
            pltpu.VMEM((3,) + piece, f32),
            pltpu.VMEM(piece, f32),
            pltpu.VMEM((band, width), f32),
            pltpu.VMEM((band, width), f32),
            pltpu.VMEM((width, width), f32),
            pltpu.VMEM((band, width), f32),
            pltpu.VMEM((band, width), f32),
            dma((7,)), dma((7,)),
            dma((3,)), dma((3,)),
            dma((7,)), dma((7,)),
            dma((grid * grid,)), dma((grid * grid,)),
            dma((grid * grid,)), dma((grid * grid,)),
            dma((grid * grid,)), dma((grid * grid,)),
            dma((grid * grid,)), dma((grid * grid,)),
            dma((chips,)), dma((chips,)),
            dma((12,)), dma((12,)),
            dma((3,)), dma((3,)),
            dma, dma,
            dma((grid - 1,)), dma,
            dma((7,)), dma((7,)),
            dma((3,)), dma((3,)),
            dma((7,)), dma((7,)),
            dma((grid - 1,)), dma((grid - 1,)),
            dma((grid - 1,)), dma((grid - 1,)),
            dma((5,)),
        ],
        compiler_params=pltpu.CompilerParams(
            collective_id=0, has_side_effects=True, vmem_limit_bytes=63 << 20
        ),
        name="whole",
    )(owned_wedge.T, owned_op.T, x, e_cond, e_val, coulomb.reshape(1, -1), gmap)


def solution(mesh):
    placed = (P("kb", None, None, None), P("kb", None), P("kb", None), P(), P(), P(), P())
    return jax.shard_map(
        body, mesh=mesh, in_specs=placed, out_specs=P(("gr", "kb"), "gc"), check_vma=False
    )
```

```python
import functools
import jax
import jax.numpy as jnp
from jax import lax
from jax.experimental import pallas as pl
from jax.experimental.pallas import tpu as pltpu
from jax.sharding import PartitionSpec as P

MESH = pl.DeviceIdType.MESH
HI = lax.Precision.HIGHEST
NT = (((1,), (1,)), ((), ()))
TN = (((0,), (0,)), ((), ()))
LOW = 256
BLOCK = 128


def product(a, b, dims=(((1,), (0,)), ((), ()))):
    return lax.dot_general(a, b, dims, precision=HI, preferred_element_type=jnp.float32)


def thirds(a):
    first = a.astype(jnp.bfloat16).astype(jnp.float32)
    second = (a - first).astype(jnp.bfloat16).astype(jnp.float32)
    return first, second, a - first - second


def gram(rows):
    p, q, r = thirds(rows)
    one = jnp.concatenate([p, p, q, p, r, q], axis=0).astype(jnp.bfloat16)
    two = jnp.concatenate([p, q, p, r, p, q], axis=0).astype(jnp.bfloat16)
    return lax.dot_general(one, two, TN, preferred_element_type=jnp.float32)


def inverse_factor(d, hook):
    n = d.shape[0]
    groups = n // 8
    lane = lax.broadcasted_iota(jnp.int32, (8, n), 1)
    sub = lax.broadcasted_iota(jnp.int32, (8, n), 0)
    rows = [d[8 * i:8 * i + 8, :] for i in range(groups)]
    out = []
    for g in range(groups):
        base = 8 * g
        hook(g)
        follows = g + 1 < groups
        head, after = rows[g], rows[g + 1] if follows else None
        cols = [jnp.broadcast_to(head[:, base + k:base + k + 1], (8, n)) for k in range(8)]
        below = [jnp.broadcast_to(after[:, base + k:base + k + 1], (8, n)) for k in range(8)] if follows else None
        inside = (lane >= base) & (lane < base + 8)
        head = jnp.where(inside, jnp.where(lane - base == sub, 1.0, 0.0), head)
        if follows:
            after = jnp.where(inside, 0.0, after)
        entry = {(i, k): jnp.broadcast_to(cols[k][i:i + 1, :], (8, n)) for i in range(8) for k in range(i + 1)}
        row = [jnp.broadcast_to(head[i:i + 1, :], (8, n)) for i in range(8)]
        done = jnp.zeros((8, n), jnp.float32)
        for j in range(0, 8, 2):
            a, b, d2 = entry[j, j], entry[j + 1, j], entry[j + 1, j + 1]
            scale = lax.rsqrt(a)
            cross = b * scale
            scale2 = lax.rsqrt(a * d2 - b * b) * (a * scale)
            pivot_row = row[j] * scale
            pivot_row2 = (row[j + 1] - cross * pivot_row) * scale2
            done = jnp.where(sub == j, pivot_row, jnp.where(sub == j + 1, pivot_row2, done))
            mult = {i: entry[i, j] * scale for i in range(j + 2, 8)}
            mult2 = {i: (entry[i, j + 1] - cross * mult[i]) * scale2 for i in range(j + 2, 8)}
            for i in range(j + 2, 8):
                row[i] = (row[i] - mult[i] * pivot_row) - mult2[i] * pivot_row2
                for k in range(j + 2, i + 1):
                    entry[i, k] = (entry[i, k] - mult[i] * mult[k]) - mult2[i] * mult2[k]
            if follows:
                step = below[j] * scale
                step2 = (below[j + 1] - step * cross) * scale2
                after = (after - step * pivot_row) - step2 * pivot_row2
                for k in range(j + 2, 8):
                    below[k] = (below[k] - step * mult[k]) - step2 * mult2[k]
        out.append(jnp.where(lane <= sub + base, done, 0.0))
        if follows:
            rows[g + 1] = after
        if g + 2 < groups:
            change = gram(done)
            for i in range(g + 2, groups):
                rows[i] = jnp.where(inside, 0.0, rows[i]) - change[8 * i:8 * i + 8, :]
    return jnp.concatenate(out, axis=0)


def whole_kernel(chips, grid, wedge_hbm, op_hbm, x_hbm, ec_ref, ev_ref, coulomb_hbm, gmap_hbm, out_ref,
                 wedge_ref, op_ref, x_ref, coulomb_ref, gmap_ref, scale_ref, g_ref,
                 lo_ref, hi_ref, pt_ref, t1_recv, t2_send, t2_recv, t_scale_ref, s_ref, y_ref, p_ref, c1_recv, c2_send, c2_recv, e00_ref, total_ref,
                 pair_ref, send_ref, recv_ref, far_send_ref, far_recv_ref, f_ref, own_ref, left_ref, top_ref,
                 low_ref, w_ref,
                 c1_s, c1_r, c2_s, c2_r, c3_s, c3_r, c4_s, c4_r, c5_s, c5_r, c6_s, c6_r, c7_s, c7_r,
                 pair_s, pair_r, near_s, near_r, far_s, far_r, swap_s, swap_r,
                 side_s, side_r, t1_s, t1_r, t2_s, t2_r, t3_s, t3_r, t4_s, t4_r, t5_s, t5_r, in_s):
    kb, gr, gc = lax.axis_index("kb"), lax.axis_index("gr"), lax.axis_index("gc")
    z, c = kb // 2, kb % 2
    other = 1 - c
    slots, owners = wedge_ref.shape
    bands, total_g = x_ref.shape
    band, width = out_ref.shape
    rows, wide = 2 * band, width // 2
    is_top, is_left = gr == 0, gc == 0

    fetched = [
        pltpu.make_async_copy(src, dst, in_s.at[i])
        for i, (src, dst) in enumerate([
            (gmap_hbm, gmap_ref), (x_hbm, x_ref), (wedge_hbm, wedge_ref), (op_hbm, op_ref), (coulomb_hbm, coulomb_ref)
        ])
    ]
    for copy in fetched:
        copy.start()

    def chip(delta, core=None):
        return (2 * ((z + delta + chips) % chips) + (c if core is None else core), gr, gc)

    def remote(src, dst, send, recv, who):
        return pltpu.make_async_remote_copy(
            src_ref=src, dst_ref=dst, send_sem=send, recv_sem=recv, device_id=who, device_id_type=MESH
        )

    partner = (2 * z + other, gr, gc)
    peers = {
        i: (kb, (gr + i // grid) % grid, (gc + i % grid) % grid) for i in range(1, grid * grid)
    }
    barrier = pltpu.get_barrier_semaphore()
    everyone = (
        [chip(d, core) for d in (1, -1, 2, -2) for core in (0, 1)]
        + [chip(d) for d in (4, -4, 8)] + [partner] + list(peers.values())
    )
    for who in everyone:
        pl.semaphore_signal(barrier, inc=1, device_id=who, device_id_type=MESH)

    for copy in fetched:
        copy.wait()

    eye = lax.broadcasted_iota(jnp.int32, (bands, bands), 0) == lax.broadcasted_iota(jnp.int32, (bands, bands), 1)
    gap = ec_ref[...] - ev_ref[...]
    weight = jnp.sqrt(4.0 / (float(owners * slots) * gap))
    weight = jnp.sum(jnp.where(eye, jnp.broadcast_to(weight, (bands, bands)), 0.0), axis=1, keepdims=True)
    y = (x_ref[...].astype(jnp.float32) * weight).astype(jnp.bfloat16)
    parts = total_g // LOW
    for h in range(parts):
        y_ref[h * bands:(h + 1) * bands, :] = y[:, h * LOW:(h + 1) * LOW]
    matched = jnp.where(wedge_ref[...] == kb, 1.0, 0.0)
    present = jnp.sum(matched, axis=0, keepdims=True)
    operation = jnp.sum(matched * op_ref[...].astype(jnp.float32), axis=0, keepdims=True)
    kinds = lax.broadcasted_iota(jnp.int32, (gmap_ref.shape[0], owners), 0).astype(jnp.float32)
    chosen = jnp.where(kinds == operation, present, 0.0).astype(jnp.bfloat16)
    count = lax.broadcasted_iota(jnp.int32, (LOW, 128), 0).astype(jnp.float32).astype(jnp.bfloat16)
    one, none = jnp.ones((LOW, 128), jnp.bfloat16), jnp.zeros((LOW, 128), jnp.bfloat16)

    def gather(side, at):
        maps = gmap_ref[:, pl.ds(at, width)]
        low_bits = (maps & (LOW - 1)).astype(jnp.float32).astype(jnp.bfloat16)
        high_bits = ((maps >> (LOW.bit_length() - 1)) + 1).astype(jnp.float32).astype(jnp.bfloat16)
        lo_ref[...] = lax.dot_general(chosen, low_bits, TN, preferred_element_type=jnp.float32)
        hi_ref[...] = lax.dot_general(chosen, high_bits, TN, preferred_element_type=jnp.float32)

        def pick(o, carry):
            low = jnp.broadcast_to(lo_ref[pl.ds(o, 1), :], (LOW, width)).astype(jnp.bfloat16)
            high = hi_ref[pl.ds(o, 1), :]
            onehot = jnp.concatenate(
                [jnp.where(count == low[:, t:t + 128], one, none) for t in range(0, width, 128)], axis=1
            )
            spread = jnp.dot(y_ref[...], onehot, preferred_element_type=jnp.float32)
            picked = jnp.zeros((bands, width), jnp.float32)
            for h in range(parts):
                picked = jnp.where(high == float(h + 1), spread[h * bands:(h + 1) * bands, :], picked)
            s_ref[pl.ds(pl.multiple_of(o * bands, bands), bands), side * width:(side + 1) * width] = picked.astype(jnp.bfloat16)
            return carry

        lax.fori_loop(0, owners, pick, 0, unroll=16)

    root = jnp.sqrt(coulomb_ref[...])

    def root_down(first, count, reach):
        ids = first + lax.broadcasted_iota(jnp.int32, (count, reach), 0)
        lanes = lax.broadcasted_iota(jnp.int32, (count, reach), 1)
        return jnp.sum(jnp.where(ids == lanes, jnp.broadcast_to(root[:, :reach], (count, reach)), 0.0), axis=1, keepdims=True)

    def scale_of(first_row, first_col, count, across):
        return root_down(first_row, count, total_g) * jnp.sqrt(
            coulomb_ref[:, pl.ds(pl.multiple_of(first_col, 128), across)]
        )

    def dielectric(value, scale, first_row, first_col):
        row = first_row + lax.broadcasted_iota(jnp.int32, value.shape, 0)
        col = first_col + lax.broadcasted_iota(jnp.int32, value.shape, 1)
        return jnp.where(row == col, 1.0, 0.0) + scale * value

    gather(0, 0)
    p_ref[...] = lax.dot_general(
        s_ref[:, pl.ds(pl.multiple_of(gr * BLOCK, BLOCK), BLOCK)], s_ref[:, :width], TN, preferred_element_type=jnp.float32
    )
    pl.semaphore_wait(barrier, len(everyone))

    def p_part(delta, core):
        k = (z + delta + chips) % grid
        return p_ref.at[pl.ds(pl.multiple_of(gc * rows + 8 * k, 8), 8), pl.ds(pl.multiple_of(core * wide, wide), wide)]

    near_parts = [(1, 0, c), (1, 1, c), (-1, 0, 2 + c), (-1, 1, 2 + c), (2, 0, 4 + c), (-2, 1, 4 + c), (0, other, 6)]
    stage1 = [
        remote(p_part(d, core), c1_recv.at[slot], c1_s.at[i], c1_r.at[slot], chip(d, core))
        for i, (d, core, slot) in enumerate(near_parts)
    ]
    for copy in stage1:
        copy.start()

    mine = pl.ds(pl.multiple_of(c * wide, wide), wide)
    theirs = pl.ds(pl.multiple_of(other * wide, wide), wide)

    gather(2, pl.multiple_of(gc * width, width))
    value = p_part(0, c)[...]
    for slot in range(7):
        remote(p_part(0, other), c1_recv.at[slot], c1_s.at[0], c1_r.at[slot], partner).wait_recv()
        value = value + c1_recv[slot]
    c2_send[...] = value
    stage2 = [
        remote(c2_send, c2_recv.at[i], c2_s.at[i], c2_r.at[i], chip(d)) for i, d in enumerate((8, 4, -4))
    ]
    for copy in stage2:
        copy.start()

    pt_ref[...] = lax.dot_general(
        s_ref[:, pl.ds(pl.multiple_of(gr * BLOCK, BLOCK), BLOCK)], s_ref[:, 2 * width:], TN, preferred_element_type=jnp.float32
    )

    def t_part(delta, core):
        k = (z + delta + chips) % grid
        return pt_ref.at[pl.ds(pl.multiple_of(rows * k, rows), rows), pl.ds(pl.multiple_of(core * wide, wide), wide)]

    top1 = [
        remote(t_part(d, core), t1_recv.at[slot], t1_s.at[i], t1_r.at[slot], chip(d, core))
        for i, (d, core, slot) in enumerate(near_parts)
    ]
    for copy in top1:
        copy.start()

    first_e = pl.multiple_of(gr * BLOCK + gc * rows + 8 * (z % grid), 8)
    scale_e = scale_of(first_e, c * wide, 8, wide)
    first_row, first_col = gr * width + z * rows, gc * width + c * wide
    first_t = pl.multiple_of(gr * BLOCK + rows * (z % grid), rows)
    scale_ref[...] = scale_of(first_row, first_col, rows, wide)
    t_scale_ref[...] = scale_of(first_t, first_col, rows, wide)

    gather(1, pl.multiple_of(gr * width, width))
    value = c2_send[...]
    for i in (1, 2, 0):
        stage2[i].wait_recv()
        value = value + c2_recv[i]
    part = e00_ref.at[pl.ds(first_e, 8), mine]
    part[...] = dielectric(value, scale_e, first_e, c * wide)
    two = jnp.where(c == 0, 2, -2)
    spread_to = [(1, 0, c), (1, 1, c), (-1, 0, 2 + c), (-1, 1, 2 + c), (two, 0, 4 + c), (two, 1, 4 + c), (0, other, 6)]
    stage3 = [
        remote(part, part, c3_s.at[i], c3_r.at[slot], chip(d, core)) for i, (d, core, slot) in enumerate(spread_to)
    ]
    for copy in stage3:
        copy.start()

    value = t_part(0, c)[...]
    for slot in range(7):
        remote(t_part(0, other), t1_recv.at[slot], t1_s.at[0], t1_r.at[slot], partner).wait_recv()
        value = value + t1_recv[slot]
    t2_send[...] = value
    top2 = [
        remote(t2_send, t2_recv.at[i], t2_s.at[i], t2_r.at[i], chip(d)) for i, d in enumerate((8, 4, -4))
    ]
    for copy in top2:
        copy.start()

    total_ref[...] = lax.dot_general(
        s_ref[:, width:2 * width], s_ref[:, 2 * width:], TN, preferred_element_type=jnp.float32
    )

    def chunk(off):
        return pl.ds(pl.multiple_of(((z + off + chips) % chips) * rows, rows), rows)

    near = [
        (9, 1, 2), (7, -1, 6), (5, 1, 1), (3, -1, 5), (6, 2, 9), (-6, -2, 11),
        (13, 1, 3), (11, -1, 7), (1, 1, 0), (15, -1, 4), (2, 2, 8), (-2, -2, 10),
    ]
    order = [off % chips for off, _, _ in near] + [8, 4, 12, 0]
    pairs = {
        off: remote(total_ref.at[chunk(off), theirs], pair_ref.at[i], pair_s.at[i], pair_r.at[i], partner)
        for i, off in enumerate(order)
    }
    for off in order:
        pairs[off].start()

    def own_part(off):
        off = off % chips
        pairs[off].wait_recv()
        return total_ref[chunk(off), mine] + pair_ref[order.index(off)]

    for slot in range(7):
        remote(part, part, c3_s.at[0], c3_r.at[slot], partner).wait_recv()

    def e00_part(r, s, half):
        return e00_ref.at[pl.ds(pl.multiple_of(r * BLOCK + s * rows, rows), rows), half]

    def whole_half(r, core):
        return jnp.logical_or(core == 1, r == 1)

    def cut_half(r, core):
        return jnp.logical_and(core == 0, r == 0)

    tile, rest = slice(0, BLOCK), slice(BLOCK, wide)

    def stage4(i, half, sends=None, recvs=None):
        part = e00_part(gr, gc, half)
        return remote(part, part, (c4_s if sends is None else sends).at[i], (c4_r if recvs is None else recvs).at[i], peers[i])

    def stage4_tile(i):
        return stage4(i, tile, c6_s, c6_r)

    def sender(i):
        return (gr + grid - i // grid) % grid, (gc + grid - i % grid) % grid

    @pl.when(cut_half(gr, c))
    def _():
        for i in peers:
            stage4_tile(i).start()
        for i in peers:
            stage4(i, rest).start()

    @pl.when(whole_half(gr, c))
    def _():
        for i in peers:
            stage4(i, mine).start()

    t_piece = top_ref.at[pl.ds(first_t, rows), mine]
    top3 = [
        remote(t_piece, t_piece, t3_s.at[i], t3_r.at[slot], chip(d, core)) for i, (d, core, slot) in enumerate(spread_to)
    ]

    def send_pieces():
        value = t2_send[...]
        for i in (1, 2, 0):
            top2[i].wait_recv()
            value = value + t2_recv[i]
        t_piece[...] = dielectric(value, t_scale_ref[...], first_t, first_col)
        for copy in top3:
            copy.start()

    def quarter(r):
        return top_ref.at[pl.ds(pl.multiple_of(r * BLOCK, BLOCK), BLOCK), mine]

    def to_column(i):
        return remote(quarter(gr), quarter(gr), t4_s.at[i - 1], t4_r.at[i - 1], (kb, (gr + i) % grid, gc))

    def to_core(i):
        r = (gr + grid - i) % grid
        return remote(quarter(r), quarter(r), t5_s.at[i - 1], t5_r.at[i - 1], partner)

    def send_column():
        for slot in range(7):
            remote(t_piece, t_piece, t3_s.at[0], t3_r.at[slot], partner).wait_recv()
        for i in range(1, grid):
            to_column(i).start()

    def send_core():
        for i in range(1, grid):
            to_column(i).wait_recv()
            to_core(i).start()

    def stage5(i, half):
        r, s = sender(i)
        return remote(e00_part(r, s, half), e00_part(r, s, half), c5_s.at[i], c5_r.at[i], partner)

    def stage5_tile(i):
        r, s = sender(i)
        return remote(e00_part(r, s, tile), e00_part(r, s, tile), c7_s.at[i], c7_r.at[i], partner)


    def gathered(j, extra):
        value = own_part(4 * j)
        for slot in (j, 4 + j) + extra:
            near_copies[slot].wait_recv()
            value = value + recv_ref[slot]
        return value

    far_list = [(2, (), 8), (1, (9,), 4), (3, (11,), -4)]

    def far_copy(i):
        return remote(far_send_ref.at[i], far_recv_ref.at[i], far_s.at[i], far_r.at[i], chip(far_list[i][2]))

    def end_e00_copies():
        for copy in stage3:
            copy.wait_send()

        @pl.when(cut_half(gr, c))
        def _():
            for i in peers:
                stage4_tile(i).wait_send()
                stage4(i, rest).wait_send()

        @pl.when(whole_half(gr, c))
        def _():
            for i in peers:
                stage4(i, mine).wait_send()
        for i in peers:
            @pl.when(cut_half(sender(i)[0], c))
            def _():
                stage5_tile(i).wait_send()
                stage5(i, rest).wait_send()

            @pl.when(whole_half(sender(i)[0], c))
            def _():
                stage5(i, mine).wait_send()

    def send_far():
        for i, (j, extra, delta) in enumerate(far_list):
            far_send_ref[i] = gathered(j, extra)
            far_copy(i).start()

    swap = remote(f_ref.at[pl.ds(pl.multiple_of(other * band, band), band)], own_ref.at[:, mine], swap_s, swap_r, partner)

    def send_own():
        value = gathered(0, (8, 10))
        for i in (1, 2, 0):
            far_copy(i).wait_recv()
            value = value + far_recv_ref[i]
        value = dielectric(value, scale_ref[...], first_row, first_col)
        f_ref[...] = value

        swap.start()
        own_ref[:, mine] = f_ref[pl.ds(pl.multiple_of(c * band, band), band)]

    def to_side(i):
        return remote(own_ref, left_ref, side_s.at[i - 1], side_r, (kb, gr, (gc + i) % grid))

    def send_side():
        swap.wait_recv()

        @pl.when(is_left)
        def _():
            for i in range(1, grid):
                to_side(i).start()

    def wait_rows():
        for i in peers:
            @pl.when(cut_half(sender(i)[0], c))
            def _():
                stage4(i, rest).wait_recv()
                stage5(i, rest).start()

            @pl.when(whole_half(sender(i)[0], c))
            def _():
                stage4(i, mine).wait_recv()
                stage5(i, mine).start()

    def wait_halves():
        for i in peers:
            @pl.when(cut_half(sender(i)[0], other))
            def _():
                stage5(i, rest).wait_recv()

            @pl.when(whole_half(sender(i)[0], other))
            def _():
                stage5(i, theirs).wait_recv()

    near_copies = {}
    for off, delta, slot in near:
        send_ref[slot] = own_part(off)
        copy = remote(send_ref.at[slot], recv_ref.at[slot], near_s.at[slot], near_r.at[slot], chip(delta))
        copy.start()
        near_copies[slot] = copy

    @pl.when(c == 0)
    def _():
        for i in peers:
            @pl.when(sender(i)[0] == 0)
            def _():
                stage4_tile(i).wait_recv()
                stage5_tile(i).start()

    @pl.when(c == 1)
    def _():
        for i in peers:
            @pl.when(sender(i)[0] == 0)
            def _():
                stage5_tile(i).wait_recv()

    plan = {
        (0, 2): send_pieces, (0, 5): wait_rows, (0, 11): wait_halves, (0, 15): end_e00_copies,
        (1, 0): send_far, (1, 2): send_column, (2, 15): send_own, (3, 1): send_core, (3, 7): send_side,
    }
    cuts = [slice(b * BLOCK, (b + 1) * BLOCK) for b in range(width // BLOCK)]
    for b, cut in enumerate(cuts):
        def hook(g):
            if (b, g) in plan:
                plan[b, g]()

        inverse = inverse_factor(e00_ref[cut, cut], hook)
        if b:
            g_ref[cut, :b * BLOCK] = product(inverse, g_ref[cut, :b * BLOCK])
        g_ref[cut, cut] = inverse
        after = (b + 1) * BLOCK
        if after < width:
            across = product(inverse, e00_ref[cut, after:])
            for cut2 in cuts[b + 1:]:
                at = cut2.start
                e00_ref[cut2, at:] = e00_ref[cut2, at:] - product(
                    across[:, at - after:at - after + BLOCK], across[:, at - after:], TN
                )
            change = product(across, g_ref[cut, :after], TN)
            if b:
                g_ref[after:, :cut.start] = g_ref[after:, :cut.start] - change[:, :cut.start]
            g_ref[after:, cut] = -change[:, cut.start:]

    @pl.when(jnp.logical_not(is_left))
    def _():
        to_side(1).wait_recv()

    @pl.when(is_left)
    def _():
        left_ref[...] = own_ref[...]

    for cut in cuts:
        low_ref[:, cut] = product(left_ref[:, :cut.stop], g_ref[cut, :cut.stop], NT)
    for cut in cuts:
        w_ref[:, cut] = product(low_ref[:, cut.start:], g_ref[cut.start:, cut])

    for i in range(1, grid):
        to_core(i).wait_recv()

    row = kb * band + lax.broadcasted_iota(jnp.int32, (band, width), 0)
    col = lax.broadcasted_iota(jnp.int32, (band, width), 1)
    factor_side = jnp.where(is_top & (col > row), 0.0, low_ref[...])
    trail = own_ref[...] - product(w_ref[...], top_ref[...])
    out_ref[...] = jnp.where(is_left, factor_side, jnp.where(is_top, own_ref[...], trail))

    for copy in stage1 + stage2 + top1 + top2 + top3 + list(pairs.values()) + list(near_copies.values()) + [swap]:
        copy.wait_send()
    for i in range(3):
        far_copy(i).wait_send()
    for i in range(1, grid):
        to_column(i).wait_send()
        to_core(i).wait_send()

    @pl.when(is_left)
    def _():
        for i in range(1, grid):
            to_side(i).wait_send()


def body(wedge_pairs, e_cond, e_val, coulomb, owned_wedge, owned_op, gmap):
    members = lax.axis_size("kb")
    grid = lax.axis_size("gr")
    chips = members // 2
    total_g = gmap.shape[1]
    width = total_g // grid
    band = width // members
    owners, slots = owned_wedge.shape
    hbm = pl.BlockSpec(memory_space=pltpu.HBM)
    x = wedge_pairs.reshape(-1, total_g)
    bands = x.shape[0]
    vmem = pl.BlockSpec(memory_space=pltpu.VMEM)
    dma = pltpu.SemaphoreType.DMA
    piece = (2 * band, width // 2)
    f32 = jnp.float32
    return pl.pallas_call(
        functools.partial(whole_kernel, chips, grid),
        out_shape=jax.ShapeDtypeStruct((band, width), f32),
        in_specs=[hbm] * 3 + [vmem] * 2 + [hbm] * 2,
        out_specs=vmem,
        scratch_shapes=[
            pltpu.VMEM((slots, owners), jnp.int32),
            pltpu.VMEM((slots, owners), jnp.int32),
            pltpu.VMEM(x.shape, x.dtype),
            pltpu.VMEM((1, total_g), f32),
            pltpu.VMEM(gmap.shape, gmap.dtype),
            pltpu.VMEM(piece, f32),
            pltpu.VMEM((width, width), f32),
            pltpu.VMEM((owners, width), f32),
            pltpu.VMEM((owners, width), f32),
            pltpu.VMEM((BLOCK, width), f32),
            pltpu.VMEM((7,) + piece, f32),
            pltpu.VMEM(piece, f32),
            pltpu.VMEM((3,) + piece, f32),
            pltpu.VMEM(piece, f32),
            pltpu.VMEM((owners * bands, 3 * width), jnp.bfloat16),
            pltpu.VMEM((bands * (total_g // LOW), LOW), jnp.bfloat16),
            pltpu.VMEM((BLOCK, width), f32),
            pltpu.VMEM((7, 8, width // 2), f32),
            pltpu.VMEM((8, width // 2), f32),
            pltpu.VMEM((3, 8, width // 2), f32),
            pltpu.VMEM((width, width), f32),
            pltpu.VMEM((width, width), f32),
            pltpu.VMEM((chips,) + piece, f32),
            pltpu.VMEM((12,) + piece, f32),
            pltpu.VMEM((12,) + piece, f32),
            pltpu.VMEM((3,) + piece, f32),
            pltpu.VMEM((3,) + piece, f32),
            pltpu.VMEM(piece, f32),
            pltpu.VMEM((band, width), f32),
            pltpu.VMEM((band, width), f32),
            pltpu.VMEM((width, width), f32),
            pltpu.VMEM((band, width), f32),
            pltpu.VMEM((band, width), f32),
            dma((7,)), dma((7,)),
            dma((3,)), dma((3,)),
            dma((7,)), dma((7,)),
            dma((grid * grid,)), dma((grid * grid,)),
            dma((grid * grid,)), dma((grid * grid,)),
            dma((grid * grid,)), dma((grid * grid,)),
            dma((grid * grid,)), dma((grid * grid,)),
            dma((chips,)), dma((chips,)),
            dma((12,)), dma((12,)),
            dma((3,)), dma((3,)),
            dma, dma,
            dma((grid - 1,)), dma,
            dma((7,)), dma((7,)),
            dma((3,)), dma((3,)),
            dma((7,)), dma((7,)),
            dma((grid - 1,)), dma((grid - 1,)),
            dma((grid - 1,)), dma((grid - 1,)),
            dma((5,)),
        ],
        compiler_params=pltpu.CompilerParams(
            collective_id=0, has_side_effects=True, vmem_limit_bytes=63 << 20
        ),
        name="whole",
    )(owned_wedge.T, owned_op.T, x, e_cond, e_val, coulomb.reshape(1, -1), gmap)


def solution(mesh):
    placed = (P("kb", None, None, None), P("kb", None), P("kb", None), P(), P(), P(), P())
    return jax.shard_map(
        body, mesh=mesh, in_specs=placed, out_specs=P(("gr", "kb"), "gc"), check_vma=False
    )
```
